32 devices in a mesh: groups: 2 (over y), dp: 4 (over z), tensor: 4 (over x, core).
Axes of the slice: x: 2, y: 2, z: 4, core: 2. Of those that a mesh axis runs over, the one named last changes fastest.
Arguments:
- partner: int32 [8], P('groups'), parts along dimension 0, may hold values from 0 to 3, as said below
- block_tenant_index: int32 [104], P(('groups', 'dp')), parts along dimension 0, may hold values from 0 to 15, as said below
- block_live_length: int32 [104], P(('groups', 'dp')), parts along dimension 0, may hold values from 9 to 128
- tenant_table_row: int32 [32], P('groups'), parts along dimension 0, may hold values from 0 to 15, as said below
- hidden: bfloat16 [13312, 8192], P(('groups', 'dp'), 'tensor'), parts along dimension 0, may hold values from -6 to 6
- cotangent: bfloat16 [13312, 1024], P(('groups', 'dp'), 'tensor'), parts along dimension 0, may hold values from -0.59765625 to 0.59765625
- frozen_value_weight: bfloat16 [8192, 1024], P('tensor'), may hold values from -0.0625 to 0.0625
- adapter_down_rows: bfloat16 [104, 64, 8192], P(('groups', 'dp'), None, 'tensor'), parts along dimension 0, as said below
- adapter_up_matrix: bfloat16 [104, 64, 1024], P(('groups', 'dp'), None, 'tensor'), parts along dimension 0, as said below
Outputs:
- projected_values: bfloat16 [13312, 1024], P(('groups', 'dp'), 'tensor'), parts along dimension 0
- down_grad_table: bfloat16 [32, 64, 8192], P(('groups', 'dp'), None, 'tensor'), parts along dimension 0
- up_grad_table: bfloat16 [32, 64, 1024], P(('groups', 'dp'), None, 'tensor'), parts along dimension 0
The draws below stay inside these ranges and needn't reach their ends.
There are 2 independent parts, one for each index of `groups`. The reference program is written for one: setup_inputs(seed, part) draws one part's arguments, and reference() takes and returns one part's arrays. A program takes and returns all parts, laid end to end along the dimension named above; an argument that names none is the same for every part. Nothing has to cross between parts.
Inputs may be any that keep to these rules, and one draw needn't show every extreme that they name: partner is a permutation of the dp indices; a device may be its own partner. `block_tenant_index`: the worked blocks of one dp device have distinct tenants; with owner tenant_table_row[t] // 4, at most 4 of them share an owner, and some owner takes exactly 4 of them. `tenant_table_row`: each value once; the table rows of dp device o are o * 4 to o * 4 + 3. `adapter_down_rows`: worked blocks with the same tenant hold the same adapter. `adapter_up_matrix`: worked blocks with the same tenant hold the same adapter.
All inputs are finite; a program needn't handle non-finite values.
Results may differ from the reference program's by a relative error of at most 0.015.
Values may be sent and summed in bfloat16 or wider, within the bound.
No kernel may reach another device: no remote copies, remote signals or barrier semaphores. Data moves between devices by JAX's collectives and lax.ppermute only.
A program may use at most 192 MiB of HBM per device.

```python
import jax
import jax.numpy as jnp
from jax import lax

D = 8192
VALUE_WIDTH = 1024
R = 64
BLOCK = 128
NB = 13
SW = 1
OWN = 4
TENANTS = 16
ROWS = 6656
N_DP = 4
N_TENSOR = 4


def plan(key):
    keys = jax.random.split(key, 4)
    partners = jax.random.permutation(keys[0], N_DP).astype(jnp.int32)
    inverse = jnp.zeros((N_DP,), jnp.int32).at[partners].set(jnp.arange(N_DP, dtype=jnp.int32))
    table_rows = jax.random.permutation(keys[1], TENANTS).astype(jnp.int32)
    tenant_at = jnp.zeros((TENANTS,), jnp.int32).at[table_rows].set(jnp.arange(TENANTS, dtype=jnp.int32))
    owner_orders = jax.vmap(lambda small_key: jax.random.permutation(small_key, N_DP).astype(jnp.int32))(jax.random.split(keys[2], N_DP))
    offsets = jax.random.randint(keys[3], (N_DP, N_DP), 0, OWN).astype(jnp.int32)
    capacity = max(2, (NB + N_DP - 1) // N_DP)
    slot_index = jnp.arange(NB, dtype=jnp.int32)
    owners = owner_orders[:, slot_index // capacity]
    repeat_index = slot_index % capacity
    starts = jnp.take_along_axis(offsets, owners, axis=1)
    wanted_rows = owners * OWN + (starts + repeat_index[None, :]) % OWN
    worked = tenant_at[wanted_rows]
    source = jnp.where(slot_index[None, :] < NB - SW, worked, worked[inverse])
    return (partners, table_rows, worked, source)


def adapter_maps(key, worked, cols, fan_in):

    def one_tenant(tenant):
        tenant_key = jax.random.fold_in(key, tenant)
        values = jax.random.normal(tenant_key, (R, cols), jnp.float32)
        return values * fan_in ** (-0.5)
    return jax.vmap(one_tenant)(worked.reshape(-1)).astype(jnp.bfloat16)


def draw_partner(key, part):
    partners = plan(key)[0]
    return partners


def draw_block_tenant_index(key, part):
    source = plan(key)[3]
    return source.reshape(-1)


def draw_tenant_table_row(key, part):
    table_rows = plan(key)[1]
    return table_rows


def draw_adapter_down_rows(key, part):
    worked = plan(key)[2]
    key = jax.random.fold_in(key, 4)
    return adapter_maps(key, worked, D, D)


def draw_adapter_up_matrix(key, part):
    worked = plan(key)[2]
    key = jax.random.fold_in(key, 5)
    return adapter_maps(key, worked, VALUE_WIDTH, R)


def plant(values, stream_key, smallest, high):
    dims = values.shape
    index_at = [jax.random.randint(jax.random.fold_in(stream_key, axis), (), 0, dims[axis]) for axis in range(len(dims))]
    values = values.at[tuple(index_at)].set(smallest)
    longest = dims.index(max(dims))
    index_at[longest] = (index_at[longest] + 1) % dims[longest]
    return values.at[tuple(index_at)].set(high)


def level_of(own_key, shape, shards, least, high):
    level, own = 1.0, jax.random.fold_in(own_key, 6)
    for dim, shards_of in shards:
        heights = jnp.exp(jax.random.uniform(jax.random.fold_in(own, dim), (shards_of,), jnp.float32, least / len(shards), high / len(shards)))
        level = level * jnp.repeat(heights, shape[dim] // shards_of).reshape([-1 if axis == dim else 1 for axis in range(len(shape))])
    return level


def bell_draw(stream_key, dims, spread, reach, cuts=(), kind=jnp.bfloat16):
    drawn = jax.random.normal(stream_key, dims, jnp.float32) * spread
    if len(cuts) > 0:
        drawn = level_of(stream_key, dims, cuts, -0.22, 0.18) * drawn
    return jnp.clip(drawn, min=-reach, max=reach).astype(kind)


def setup_inputs(seed: int = 0, part: int = 0) -> dict:
    splits = jax.random.split(jax.random.key(seed), 10)
    part_keys = jax.random.split(jax.random.fold_in(splits[9], part), 10)
    return {
        "partner": draw_partner(jax.random.fold_in(jax.random.fold_in(splits[9], part), 71), part),
        "block_tenant_index": draw_block_tenant_index(jax.random.fold_in(jax.random.fold_in(splits[9], part), 71), part),
        "block_live_length": plant(jax.random.randint(part_keys[2], (N_DP * NB,), BLOCK // 16 + 1, BLOCK + 1), jax.random.fold_in(part_keys[2], 1), BLOCK // 16 + 1, BLOCK).astype(jnp.int32),
        "tenant_table_row": draw_tenant_table_row(jax.random.fold_in(jax.random.fold_in(splits[9], part), 71), part),
        "hidden": bell_draw(part_keys[4], (ROWS, D), 1.0, 6.0, ((0, 4), (1, 4))),
        "cotangent": bell_draw(part_keys[5], (ROWS, VALUE_WIDTH), 0.1, 0.59765625, ((0, 4), (1, 4))),
        "frozen_value_weight": bell_draw(splits[6], (D, VALUE_WIDTH), D ** -0.5, 0.0625, ((0, 4),)),
        "adapter_down_rows": draw_adapter_down_rows(jax.random.fold_in(jax.random.fold_in(splits[9], part), 71), part),
        "adapter_up_matrix": draw_adapter_up_matrix(jax.random.fold_in(jax.random.fold_in(splits[9], part), 71), part),
    }


ADAPTER_SCALE = 0.5


def reference(partner, block_tenant_index, block_live_length, tenant_table_row, hidden, cotangent, frozen_value_weight, adapter_down_rows, adapter_up_matrix):
    slot_index = jnp.arange(NB, dtype=jnp.int32)
    device_index = jnp.arange(N_DP, dtype=jnp.int32)
    source_device = jnp.where(slot_index[None, :] < NB - SW, device_index[:, None], partner[:, None])
    source_block = (source_device * NB + slot_index[None, :]).reshape(-1).astype(jnp.int32)
    worked_in = hidden.reshape(N_DP * NB, BLOCK, D)[source_block]
    worked_cot = cotangent.reshape(N_DP * NB, BLOCK, VALUE_WIDTH)[source_block]
    lengths = block_live_length[source_block]
    tenants = block_tenant_index[source_block]
    valid = (jnp.arange(BLOCK, dtype=jnp.int32)[None, :] < lengths[:, None])[:, :, None]
    masked_input = jnp.where(valid, worked_in, jnp.zeros((), worked_in.dtype))
    masked_output_gradient = jnp.where(valid, worked_cot, jnp.zeros((), worked_cot.dtype))
    flat_in = masked_input.reshape(-1, D)
    width = D // N_TENSOR
    frozen_values = jnp.zeros((flat_in.shape[0], VALUE_WIDTH), jnp.float32)
    for shard in range(N_TENSOR):
        part_sum = jnp.dot(flat_in[:, shard * width:(shard + 1) * width], frozen_value_weight[shard * width:(shard + 1) * width], preferred_element_type=jnp.float32)
        rounded = lax.optimization_barrier(part_sum.astype(jnp.bfloat16))
        frozen_values = frozen_values + rounded.astype(jnp.float32)

    def block_wise(inputs):
        block_input, block_output_gradient, down_map, up_matrix = inputs
        rank_input = jnp.dot(block_input, down_map.T, preferred_element_type=jnp.float32).astype(jnp.bfloat16)
        rank_gradient = jnp.dot(block_output_gradient, up_matrix.T, preferred_element_type=jnp.float32).astype(jnp.bfloat16)
        adapter_output = ADAPTER_SCALE * jnp.dot(rank_input, up_matrix, preferred_element_type=jnp.float32)
        down_gradient = (ADAPTER_SCALE * jnp.dot(rank_gradient.T, block_input, preferred_element_type=jnp.float32)).astype(jnp.bfloat16)
        up_gradient = (ADAPTER_SCALE * jnp.dot(rank_input.T, block_output_gradient, preferred_element_type=jnp.float32)).astype(jnp.bfloat16)
        return adapter_output, down_gradient, up_gradient

    adapter_output, down_gradients, up_gradients = lax.map(block_wise, (masked_input, masked_output_gradient, adapter_down_rows, adapter_up_matrix))
    projected_values = (frozen_values + adapter_output.reshape(-1, VALUE_WIDTH)).astype(jnp.bfloat16)
    table_rows = tenant_table_row[tenants]
    down_table = jnp.zeros((TENANTS, R, D), jnp.float32).at[table_rows].add(down_gradients.astype(jnp.float32))
    up_table = jnp.zeros((TENANTS, R, VALUE_WIDTH), jnp.float32).at[table_rows].add(up_gradients.astype(jnp.float32))
    return projected_values, down_table.astype(jnp.bfloat16), up_table.astype(jnp.bfloat16)
```

```python
import functools

import jax
import jax.numpy as jnp
from jax import lax
from jax.experimental import pallas as pl
from jax.experimental.pallas import tpu as pltpu
from jax.sharding import PartitionSpec as P

BLOCK = 128
SW = 1
OWN = 4


ADAPTER_SCALE = 0.5


def table_kernel(block_of, has_block, has_last, first_row, rank_ref, rows_ref, last_ref, out_ref):
    row = first_row[0] + pl.program_id(0)
    mine = rank_ref[block_of[row]]
    mine = jnp.where(has_block[row] > 0, mine, jnp.zeros_like(mine))
    total = jnp.dot(mine, rows_ref[...], preferred_element_type=jnp.float32)

    @pl.when(has_last[row] == 0)
    def _():
        out_ref[0] = (ADAPTER_SCALE * total).astype(out_ref.dtype)

    @pl.when(has_last[row] > 0)
    def _():
        late = jnp.dot(rank_ref[rank_ref.shape[0] - 1], last_ref[...], preferred_element_type=jnp.float32)
        out_ref[0] = (ADAPTER_SCALE * (total + late)).astype(out_ref.dtype)


def grad_table(labels, first_row, rows, rank, features):
    blocks, rank_width, _ = rank.shape
    width = features.shape[1]
    return pl.pallas_call(
        table_kernel,
        grid_spec=pltpu.PrefetchScalarGridSpec(
            num_scalar_prefetch=4,
            grid=(rows,),
            in_specs=[
                pl.BlockSpec(rank.shape, lambda r, *refs: (0, 0, 0)),
                pl.BlockSpec((BLOCK, width), lambda r, at, a, b, first: (at[first[0] + r], 0)),
                pl.BlockSpec((BLOCK, width), lambda r, *refs: (blocks - 1, 0)),
            ],
            out_specs=pl.BlockSpec((1, rank_width, width), lambda r, *refs: (r, 0, 0)),
        ),
        out_shape=jax.ShapeDtypeStruct((rows, rank_width, width), rank.dtype),
        compiler_params=pltpu.CompilerParams(vmem_limit_bytes=24 * 1024 * 1024),
        cost_estimate=pl.CostEstimate(
            flops=2 * rows * rank_width * BLOCK * width,
            bytes_accessed=2 * rows * (BLOCK + rank_width) * width,
            transcendentals=0,
        ),
    )(*labels, first_row, rank, features, features)


def fetch(array, axis, source):
    size = lax.axis_size(axis)
    me = lax.axis_index(axis)
    if size > 4:
        return lax.dynamic_index_in_dim(lax.all_gather(array, axis), source, 0, keepdims=False)
    taken = array
    for shift in range(1, size):
        arrived = lax.ppermute(array, axis, [(i, (i + shift) % size) for i in range(size)])
        taken = jnp.where((me - shift) % size == source, arrived, taken)
    return taken


def exchange_sum(array, axis):
    size = lax.axis_size(axis)
    stride = 1
    while stride < size:
        arrived = lax.ppermute(array, axis, [(i, i ^ stride) for i in range(size)])
        array = (array.astype(jnp.float32) + arrived.astype(jnp.float32)).astype(array.dtype)
        stride *= 2
    return array


def line_reduce_scatter(table, axis):
    size = lax.axis_size(axis)
    me = lax.axis_index(axis)

    def entry(index):
        index = jnp.clip(index, 0, size - 1)
        return lax.dynamic_index_in_dim(table, index, 0, keepdims=False).astype(jnp.float32)

    from_left = from_right = None
    for step in range(size - 1):
        right = entry(size - 1 - step + me)
        left = entry(step - (size - 1 - me))
        if step > 0:
            right = right + from_left.astype(jnp.float32)
            left = left + from_right.astype(jnp.float32)
        from_left = lax.ppermute(
            right.astype(table.dtype), axis, [(i, i + 1) for i in range(step + 1)]
        )
        from_right = lax.ppermute(
            left.astype(table.dtype), axis, [(i, i - 1) for i in range(size - 1 - step, size)]
        )
    own = entry(me)
    if size > 1:
        own = own + from_left.astype(jnp.float32) + from_right.astype(jnp.float32)
    return own.astype(table.dtype)


def base_sum(hidden, weight, axis):
    size = lax.axis_size(axis)
    me = lax.axis_index(axis)
    width = weight.shape[1] // size

    def term(columns):
        part = lax.dynamic_slice_in_dim(weight, columns * width, width, 1)
        return jnp.dot(hidden, part, preferred_element_type=jnp.float32).astype(hidden.dtype)

    near = [(i, i ^ 1) for i in range(size)]
    far = [(i, i ^ 2) for i in range(size)]
    first = lax.ppermute(term(me ^ 3), axis, near)
    away = (term(me ^ 2).astype(jnp.float32) + first.astype(jnp.float32)).astype(hidden.dtype)
    second = lax.ppermute(away, axis, far)
    third = lax.ppermute(term(me ^ 1), axis, near)
    return (
        term(me).astype(jnp.float32) + third.astype(jnp.float32) + second.astype(jnp.float32)
    )


def body(
    partner,
    block_tenant_index,
    block_live_length,
    tenant_table_row,
    hidden,
    cotangent,
    frozen_value_weight,
    adapter_down_rows,
    adapter_up_matrix,
):
    blocks = block_tenant_index.shape[0]
    output_width = cotangent.shape[1]
    rank_width = adapter_down_rows.shape[1]
    kept = blocks - SW
    kind = hidden.dtype
    devices = lax.axis_size("dp")
    me = lax.axis_index("dp")
    holder = jnp.sum(jnp.where(partner == me, jnp.arange(devices, dtype=jnp.int32), 0))
    source = partner[me]
    up_last = fetch(adapter_up_matrix[kept:], "dp", holder)
    up_maps = jnp.concatenate([adapter_up_matrix[:kept], up_last], axis=0)
    live = (jnp.arange(BLOCK, dtype=jnp.int32)[None, :] < block_live_length[:, None])[:, None, :]
    cot_blocks = cotangent.reshape(blocks, BLOCK, output_width)
    hidden_blocks = hidden.reshape(blocks, BLOCK, hidden.shape[1])

    cot_terms = jnp.einsum("zaj,zuj->zau", up_maps, cot_blocks, preferred_element_type=jnp.float32)
    rank_cot = exchange_sum(jnp.where(live, cot_terms, 0.0).astype(kind), "tensor")

    table_rows = jnp.sum(
        jnp.where(
            block_tenant_index[:, None] == jnp.arange(tenant_table_row.shape[0], dtype=jnp.int32)[None, :],
            tenant_table_row[None, :],
            0,
        ),
        axis=1,
    )
    rows = devices * OWN
    matches = jnp.arange(rows, dtype=jnp.int32)[:, None] == table_rows[None, :]
    block_of = jnp.sum(jnp.where(matches[:, :kept], jnp.arange(kept, dtype=jnp.int32)[None, :], 0), axis=1)
    has_block = jnp.any(matches[:, :kept], axis=1).astype(jnp.int32)
    has_last = matches[:, kept].astype(jnp.int32)
    labels = (block_of, has_block, has_last)
    start = jnp.zeros((1,), jnp.int32)

    down_table = grad_table(labels, start, rows, rank_cot, hidden)
    down_out = line_reduce_scatter(
        down_table.reshape(devices, OWN, rank_width, hidden.shape[1]), "dp"
    )

    down_last = fetch(adapter_down_rows[kept:], "dp", holder)
    in_terms = jnp.concatenate(
        [
            jnp.einsum(
                "xlf,xhf->xlh", adapter_down_rows[:kept], hidden_blocks[:kept], preferred_element_type=jnp.float32
            ),
            jnp.einsum("xlf,xhf->xlh", down_last, hidden_blocks[kept:], preferred_element_type=jnp.float32),
        ],
        axis=0,
    )
    rank_in = exchange_sum(jnp.where(live, in_terms, 0.0).astype(kind), "tensor")
    up_table = grad_table(labels, start, rows, rank_in, cotangent)
    up_out = line_reduce_scatter(up_table.reshape(devices, OWN, rank_width, output_width), "dp")

    frozen_values = base_sum(hidden, frozen_value_weight, "tensor")
    adapter_terms = jnp.einsum("wxf,wxm->wfm", rank_in, up_maps, preferred_element_type=jnp.float32)
    values = frozen_values + ADAPTER_SCALE * adapter_terms.reshape(-1, output_width)
    values = jnp.where(live.reshape(-1, 1), values, 0.0).astype(kind)
    last_values = fetch(values[kept * BLOCK :], "dp", source)
    projected_values = jnp.concatenate([values[: kept * BLOCK], last_values], axis=0)
    return (projected_values, down_out, up_out)


def solution(mesh):
    in_specs = (
        P("groups"),
        P(("groups", "dp")),
        P(("groups", "dp")),
        P("groups"),
        P(("groups", "dp"), "tensor"),
        P(("groups", "dp"), "tensor"),
        P("tensor", None),
        P(("groups", "dp"), None, "tensor"),
        P(("groups", "dp"), None, "tensor"),
    )
    out_specs = (
        P(("groups", "dp"), "tensor"),
        P(("groups", "dp"), None, "tensor"),
        P(("groups", "dp"), None, "tensor"),
    )
    return jax.shard_map(body, mesh=mesh, in_specs=in_specs, out_specs=out_specs, check_vma=False)
```

```python
import functools

import jax
import jax.numpy as jnp
from jax import lax
from jax.experimental import pallas as pl
from jax.experimental.pallas import tpu as pltpu
from jax.sharding import PartitionSpec as P

BLOCK = 128
SW = 1
OWN = 4


ADAPTER_SCALE = 0.5

ANYWHERE = pl.BlockSpec(memory_space=pl.ANY)
ROW_PRODUCT = (((1,), (1,)), ((), ()))


def call(kernel, scalars, grid, inputs, outputs, tokens=(), work=0, aliases=None):
    def run(*refs):
        cut = len(scalars) + len(inputs)
        return kernel(*refs[:cut], *refs[cut + len(tokens) :])

    moved = sum(array.size * array.dtype.itemsize for array, _ in inputs)
    moved += sum(2 * functools.reduce(lambda a, b: a * b, shape) for shape, _, _ in outputs)
    return pl.pallas_call(
        run,
        grid_spec=pltpu.PrefetchScalarGridSpec(
            num_scalar_prefetch=len(scalars),
            grid=grid,
            in_specs=[spec for _, spec in inputs] + [ANYWHERE] * len(tokens),
            out_specs=[spec for _, _, spec in outputs],
        ),
        out_shape=[jax.ShapeDtypeStruct(shape, kind) for shape, kind, _ in outputs],
        input_output_aliases=aliases or {},
        cost_estimate=pl.CostEstimate(flops=work, bytes_accessed=moved, transcendentals=0),
    )(*scalars, *[array for array, _ in inputs], *tokens)


def whole(array):
    return (array, pl.BlockSpec(array.shape, lambda *_: (0,) * array.ndim))


def nothing(*refs):
    pass


def after(array, *tokens):
    return call(nothing, (), (1,), [(array, ANYWHERE)], [(array.shape, array.dtype, ANYWHERE)], tokens, aliases={0: 0})[0]


def masked_rank(adapter, rows, length):
    ranks = lax.dot_general(adapter, rows, ROW_PRODUCT, preferred_element_type=jnp.float32)
    live = lax.broadcasted_iota(jnp.int32, ranks.shape, 1) < length
    return jnp.where(live, ranks, 0.0).astype(rows.dtype)


def rank_terms(lengths, maps, features, blocks, each, tokens=()):
    rank, width = maps.shape[1:]

    def kernel(lengths_ref, maps_ref, rows_ref, out_ref):
        for k in range(each):
            out_ref[k] = masked_rank(
                maps_ref[k], rows_ref[k * BLOCK : (k + 1) * BLOCK], lengths_ref[pl.program_id(0) * each + k]
            )

    return call(
        kernel,
        (lengths,),
        (blocks // each,),
        [
            (maps, pl.BlockSpec((each, rank, width), lambda i, *_: (i, 0, 0))),
            (features, pl.BlockSpec((each * BLOCK, width), lambda i, *_: (i, 0))),
        ],
        [((blocks, rank, BLOCK), features.dtype, pl.BlockSpec((each, rank, BLOCK), lambda i, *_: (i, 0, 0)))],
        tokens,
        work=2 * blocks * rank * BLOCK * width,
    )[0]


def last_rank(lengths, pick, choices, features, tokens=()):
    shape = choices[0].shape
    block = features.shape[0] // BLOCK - 1

    def kernel(lengths_ref, pick_ref, *refs):
        rows_ref, out_ref, chosen_ref = refs[-3:]
        for k, choice in enumerate(refs[:-3]):

            @pl.when(pick_ref[0] == k)
            def _():
                chosen_ref[...] = choice[...]

        out_ref[0] = masked_rank(chosen_ref[0], rows_ref[...], lengths_ref[block])

    return call(
        kernel,
        (lengths, pick),
        (1,),
        [whole(choice) for choice in choices]
        + [(features, pl.BlockSpec((BLOCK, shape[2]), lambda i, *_: (block, 0)))],
        [
            ((1, shape[1], BLOCK), features.dtype, pl.BlockSpec((1, shape[1], BLOCK), lambda i, *_: (0, 0, 0))),
            (shape, features.dtype, pl.BlockSpec(shape, lambda i, *_: (0, 0, 0))),
        ],
        tokens,
        work=2 * shape[1] * BLOCK * shape[2],
    )


def table_row(labels, row, ranks, last_ranks, rows_of, last_rows):
    block_of, has_block, has_last = labels
    at = block_of[row]
    mine = ranks[0][at].astype(jnp.float32) + ranks[1][at].astype(jnp.float32)
    mine = jnp.where(has_block[row] > 0, mine, 0.0).astype(last_rows.dtype)
    total = jnp.dot(mine, rows_of(at), preferred_element_type=jnp.float32)

    def with_last():
        late = (last_ranks[0][0].astype(jnp.float32) + last_ranks[1][0].astype(jnp.float32)).astype(last_rows.dtype)
        return total + jnp.dot(late, last_rows[...], preferred_element_type=jnp.float32)

    return has_last[row] > 0, total, with_last


def down_rows(labels, first_row, rows, ranks, last_ranks, features, tokens=()):
    _, rank, _ = ranks[0].shape
    width = features.shape[1]
    block = features.shape[0] // BLOCK - 1

    def kernel(block_of, has_block, has_last, first, a, b, c, d, rows_ref, last_ref, out_ref):
        more, total, with_last = table_row(
            (block_of, has_block, has_last),
            first[0] + pl.program_id(0),
            (a, b),
            (c, d),
            lambda _: rows_ref[...],
            last_ref,
        )

        @pl.when(jnp.logical_not(more))
        def _():
            out_ref[0] = (ADAPTER_SCALE * total).astype(out_ref.dtype)

        @pl.when(more)
        def _():
            out_ref[0] = (ADAPTER_SCALE * with_last()).astype(out_ref.dtype)

    return call(
        kernel,
        (*labels, first_row),
        (rows,),
        [whole(array) for array in (*ranks, *last_ranks)]
        + [
            (features, pl.BlockSpec((BLOCK, width), lambda r, at, x, y, first: (at[first[0] + r], 0))),
            (features, pl.BlockSpec((BLOCK, width), lambda r, *_: (block, 0))),
        ],
        [((rows, rank, width), features.dtype, pl.BlockSpec((1, rank, width), lambda r, *_: (r, 0, 0)))],
        tokens,
        work=2 * rows * rank * BLOCK * width,
    )[0]


def up_rows(labels, row_of, parts, ranks, last_ranks, features, tokens=()):
    _, rank, _ = ranks[0].shape
    width = features.shape[1]
    block = features.shape[0] // BLOCK - 1

    def kernel(block_of, has_block, has_last, row_ref, a, b, c, d, rows_ref, *outs):
        done = 0
        for out_ref in outs:

            def one(r, carry, out_ref=out_ref, done=done):
                more, total, with_last = table_row(
                    (block_of, has_block, has_last),
                    row_ref[done + r],
                    (a, b),
                    (c, d),
                    lambda at: rows_ref[pl.ds(pl.multiple_of(at * BLOCK, BLOCK), BLOCK), :],
                    rows_ref.at[pl.ds(block * BLOCK, BLOCK), :],
                )
                out_ref[r] = (ADAPTER_SCALE * total).astype(out_ref.dtype)

                @pl.when(more)
                def _():
                    out_ref[r] = (ADAPTER_SCALE * with_last()).astype(out_ref.dtype)

                return carry

            lax.fori_loop(0, out_ref.shape[0], one, 0)
            done += out_ref.shape[0]

    return call(
        kernel,
        (*labels, row_of),
        (1,),
        [whole(array) for array in (*ranks, *last_ranks, features)],
        [
            ((rows, rank, width), features.dtype, pl.BlockSpec((rows, rank, width), lambda i, *_: (0, 0, 0)))
            for rows in parts
        ],
        tokens,
        work=2 * sum(parts) * rank * BLOCK * width,
    )


def base_terms(columns, hidden, weight, width, tokens=()):
    rows, depth = hidden.shape
    tile = rows // 4

    def kernel(columns_ref, rows_ref, one_ref, two_ref, one_out, two_out):
        one_out[...] = jnp.dot(rows_ref[...], one_ref[...], preferred_element_type=jnp.float32).astype(one_out.dtype)
        two_out[...] = jnp.dot(rows_ref[...], two_ref[...], preferred_element_type=jnp.float32).astype(two_out.dtype)

    return call(
        kernel,
        (columns,),
        (rows // tile,),
        [
            (hidden, pl.BlockSpec((tile, depth), lambda i, *_: (i, 0))),
            (weight, pl.BlockSpec((depth, width), lambda i, at: (0, at[0]))),
            (weight, pl.BlockSpec((depth, width), lambda i, at: (0, at[1]))),
        ],
        [((rows, width), hidden.dtype, pl.BlockSpec((tile, width), lambda i, *_: (i, 0)))] * 2,
        tokens,
        work=4 * rows * depth * width,
    )


def values_of(lengths, base, ranks, last_ranks, maps, last_map, tokens=()):
    rows, width = base[0].shape
    blocks = rows // BLOCK

    def kernel(lengths_ref, one, two, three, a, b, c, d, maps_ref, last_ref, out_ref, last_out):
        for k in range(blocks):
            at = slice(k * BLOCK, (k + 1) * BLOCK)
            pair = (a[k], b[k]) if k < blocks - 1 else (c[0], d[0])
            adapter = maps_ref[k] if k < blocks - 1 else last_ref[0]
            ranks_k = (pair[0].astype(jnp.float32) + pair[1].astype(jnp.float32)).astype(adapter.dtype)
            added = lax.dot_general(
                ranks_k, adapter, (((0,), (0,)), ((), ())), preferred_element_type=jnp.float32
            )
            frozen = one[at].astype(jnp.float32) + two[at].astype(jnp.float32) + three[at].astype(jnp.float32)
            live = lax.broadcasted_iota(jnp.int32, frozen.shape, 0) < lengths_ref[k]
            values = jnp.where(live, frozen + ADAPTER_SCALE * added, 0.0).astype(out_ref.dtype)
            out_ref[at] = values
            if k == blocks - 1:
                last_out[...] = values

    return call(
        kernel,
        (lengths,),
        (1,),
        [whole(array) for array in (*base, *ranks, *last_ranks, maps, last_map)],
        [
            ((rows, width), maps.dtype, pl.BlockSpec((rows, width), lambda i, *_: (0, 0))),
            ((BLOCK, width), maps.dtype, pl.BlockSpec((BLOCK, width), lambda i, *_: (0, 0))),
        ],
        tokens,
        work=2 * rows * maps.shape[1] * width,
    )


def put_last(pick, values, choices):
    width = values.shape[1]
    block = values.shape[0] // BLOCK - 1

    def kernel(pick_ref, *refs):
        for k, choice in enumerate(refs[:-2]):

            @pl.when(pick_ref[0] == k)
            def _():
                refs[-1][...] = choice[...]

    return call(
        kernel,
        (pick,),
        (1,),
        [whole(choice) for choice in choices] + [(values, ANYWHERE)],
        [(values.shape, values.dtype, pl.BlockSpec((BLOCK, width), lambda i, *_: (block, 0)))],
        aliases={1 + len(choices): 0},
    )[0]


def shifted(array, source):
    size = lax.axis_size("dp")
    me = lax.axis_index("dp")
    if size > 4:
        taken = lax.dynamic_index_in_dim(lax.all_gather(array, "dp"), source, 0, keepdims=False)
        return [taken], jnp.zeros((1,), jnp.int32)
    choices = [array] + [
        lax.ppermute(array, "dp", [(i, (i + shift) % size) for i in range(size)]) for shift in range(1, size)
    ]
    return choices, ((me - source) % size).reshape(1)


def routed(array, holders):
    if lax.axis_size("dp") != 4:
        return shifted(array, holders[lax.axis_index("dp")])
    me = lax.axis_index("dp")
    source = holders[me]
    from_left = lax.ppermute(array, "dp", [(0, 1), (1, 2)])
    from_right = lax.ppermute(array, "dp", [(3, 2), (2, 1)])
    passed = lax.ppermute(jnp.where(me == 1, from_left, from_right), "dp", [(1, 2), (2, 1)])
    wanted = jnp.where(me == 1, holders[0], holders[3])
    onward = jnp.where(wanted == me - 1, from_left, jnp.where(wanted == me + 1, from_right, passed))
    onward = jnp.where(wanted == me, array, onward)
    outward = lax.ppermute(onward, "dp", [(2, 3), (1, 0)])
    inner = (me == 1) | (me == 2)
    pick = jnp.where(
        source == me,
        0,
        jnp.where(inner, jnp.where(source == me - 1, 1, jnp.where(source == me + 1, 2, 3)), 4),
    )
    return [array, from_left, from_right, passed, outward], pick.reshape(1).astype(jnp.int32)


def add(*arrays):
    return sum(array.astype(jnp.float32) for array in arrays).astype(arrays[0].dtype)


def near_sum(array):
    size = lax.axis_size("tensor")
    return add(array, lax.ppermute(array, "tensor", [(i, i ^ 1) for i in range(size)]))


def far(array):
    size = lax.axis_size("tensor")
    return lax.ppermute(array, "tensor", [(i, i ^ 2) for i in range(size)])


def exchanged(array):
    array = near_sum(array)
    return array, far(array)


def line_reduce_scatter(table):
    size = lax.axis_size("dp")
    me = lax.axis_index("dp")

    def entry(index):
        return lax.dynamic_index_in_dim(table, jnp.clip(index, 0, size - 1), 0, keepdims=False)

    from_left = from_right = None
    for step in range(size - 1):
        right = entry(size - 1 - step + me)
        left = entry(step - (size - 1 - me))
        if step > 0:
            right = add(right, from_left)
            left = add(left, from_right)
        from_left = lax.ppermute(right, "dp", [(i, i + 1) for i in range(step + 1)])
        from_right = lax.ppermute(left, "dp", [(i, i - 1) for i in range(size - 1 - step, size)])
    return entry(me) if size == 1 else add(entry(me), from_left, from_right)


TO_INNER = [(0, 1), (3, 2)]
ACROSS = [(1, 2), (2, 1)]
TO_OUTER = [(2, 3), (1, 0)]


def body(
    partner,
    block_tenant_index,
    block_live_length,
    tenant_table_row,
    hidden,
    cotangent,
    frozen_value_weight,
    adapter_down_rows,
    adapter_up_matrix,
):
    blocks = block_tenant_index.shape[0]
    output_width = cotangent.shape[1]
    kept = blocks - SW
    devices = lax.axis_size("dp")
    me = lax.axis_index("dp")
    column = lax.axis_index("tensor")
    lengths = block_live_length
    order = jnp.arange(devices, dtype=jnp.int32)
    holders = jnp.sum(jnp.where(partner[None, :] == order[:, None], order[None, :], 0), axis=1)

    up_choices, up_pick = shifted(adapter_up_matrix[kept:], holders[me])
    cot_terms = rank_terms(lengths, adapter_up_matrix, cotangent, kept, 4)
    rank_cot = exchanged(cot_terms)
    last_terms, up_last = last_rank(lengths, up_pick, up_choices, cotangent, [cot_terms])
    last_cot = exchanged(last_terms)

    table_rows = jnp.sum(
        jnp.where(
            block_tenant_index[:, None] == jnp.arange(tenant_table_row.shape[0], dtype=jnp.int32)[None, :],
            tenant_table_row[None, :],
            0,
        ),
        axis=1,
    )
    rows = devices * OWN
    matches = jnp.arange(rows, dtype=jnp.int32)[:, None] == table_rows[None, :]
    block_of = jnp.sum(jnp.where(matches[:, :kept], jnp.arange(kept, dtype=jnp.int32)[None, :], 0), axis=1)
    has_block = jnp.any(matches[:, :kept], axis=1).astype(jnp.int32)
    has_last = matches[:, kept].astype(jnp.int32)
    labels = (block_of, has_block, has_last)

    owners = jnp.where(me < devices // 2, order[::-1], order)
    line = devices == 4

    def down_part(owner, count=OWN, tokens=()):
        return down_rows(
            labels, (owner * OWN).reshape(1).astype(jnp.int32), count, rank_cot, last_cot, hidden, tokens
        )

    if line:
        part0 = down_part(owners[0])
        token = part0
    else:
        token = down_part(jnp.zeros((), jnp.int32), rows)
        down_out = line_reduce_scatter(token.reshape(devices, OWN, *token.shape[1:]))

    def copy_kernel(in_ref, out_ref):
        out_ref[...] = in_ref[...]

    down_own = call(
        copy_kernel,
        (),
        (1,),
        [(adapter_down_rows, pl.BlockSpec((SW, *adapter_down_rows.shape[1:]), lambda i: (kept, 0, 0)))],
        [
            (
                (SW, *adapter_down_rows.shape[1:]),
                hidden.dtype,
                pl.BlockSpec((SW, *adapter_down_rows.shape[1:]), lambda i: (0, 0, 0)),
            )
        ],
        [cot_terms],
    )[0]
    down_choices, down_pick = routed(down_own, holders)
    in_terms = rank_terms(lengths, adapter_down_rows, hidden, kept, 2, [token])
    rank_in = exchanged(in_terms)
    last_in = exchanged(last_rank(lengths, down_pick, down_choices, hidden, [in_terms])[0])

    if line:
        from0 = lax.ppermute(part0, "dp", TO_INNER)
        part1 = down_part(owners[1], tokens=[part0])
        part2 = down_part(owners[2], tokens=[part1])
        part3 = down_part(owners[3], tokens=[part2])
        part_own = down_part(me, tokens=[part3])
        part1 = after(part1, from0)
        from1 = lax.ppermute(part1, "dp", TO_INNER)
        across0 = lax.ppermute(add(part0, from0), "dp", ACROSS)
        from2 = lax.ppermute(after(part2, from1), "dp", TO_INNER)
        across1 = lax.ppermute(add(part1, from1), "dp", ACROSS)
        outer = lax.ppermute(add(part3, across0), "dp", TO_OUTER)
        down_out = add(part_own, from2, across1, outer)

        row_of = (owners[:, None] * OWN + jnp.arange(OWN, dtype=jnp.int32)[None, :]).reshape(-1)
        up_sent, up_kept = up_rows(labels, row_of, (3 * OWN, OWN), rank_in, last_in, cotangent)
        up_in = lax.ppermute(up_sent, "dp", TO_INNER)
        up_across = lax.ppermute(add(up_sent[: 2 * OWN], up_in[: 2 * OWN]), "dp", ACROSS)
        up_outer = lax.ppermute(add(up_kept, up_across[:OWN]), "dp", TO_OUTER)
        inner = (me == 1) | (me == 2)
        up_out = jnp.where(
            inner,
            add(up_sent[2 * OWN :], up_in[2 * OWN :], up_across[OWN:]),
            add(up_kept, up_outer),
        )
    else:
        (up_table,) = up_rows(labels, jnp.arange(rows, dtype=jnp.int32), (rows,), rank_in, last_in, cotangent)
        up_out = line_reduce_scatter(up_table.reshape(devices, OWN, *up_table.shape[1:]))

    pair = jnp.stack([column ^ 3, column ^ 2]).astype(jnp.int32)
    given, away = base_terms(pair, hidden, frozen_value_weight, output_width, [in_terms])
    size = lax.axis_size("tensor")
    near = [(i, i ^ 1) for i in range(size)]
    across = far(add(away, lax.ppermute(given, "tensor", near)))
    pair = jnp.stack([column ^ 1, column]).astype(jnp.int32)
    given, mine = base_terms(pair, hidden, frozen_value_weight, output_width, [away])
    base = (mine, lax.ppermute(given, "tensor", near), across)
    values, last_values = values_of(lengths, base, rank_in, last_in, adapter_up_matrix, up_last)
    value_choices, value_pick = shifted(last_values, partner[me])
    projected_values = put_last(value_pick, values, value_choices)
    return (projected_values, down_out, up_out)


def solution(mesh):
    in_specs = (
        P("groups"),
        P(("groups", "dp")),
        P(("groups", "dp")),
        P("groups"),
        P(("groups", "dp"), "tensor"),
        P(("groups", "dp"), "tensor"),
        P("tensor", None),
        P(("groups", "dp"), None, "tensor"),
        P(("groups", "dp"), None, "tensor"),
    )
    out_specs = (
        P(("groups", "dp"), "tensor"),
        P(("groups", "dp"), None, "tensor"),
        P(("groups", "dp"), None, "tensor"),
    )
    return jax.shard_map(body, mesh=mesh, in_specs=in_specs, out_specs=out_specs, check_vma=False)
```

```python
import jax
import jax.numpy as jnp
from jax import lax
from jax.experimental import pallas as pl
from jax.experimental.pallas import tpu as pltpu
from jax.sharding import PartitionSpec as P

BLOCK = 128
SW = 1
OWN = 4


ADAPTER_SCALE = 0.5

ANYWHERE = pl.BlockSpec(memory_space=pl.ANY)
ROW_PRODUCT = (((1,), (1,)), ((), ()))


def call(kernel, scalars, grid, inputs, outputs, tokens=(), us=1.0, scratch=(), aliases=None):
    def run(*refs):
        cut = len(scalars) + len(inputs)
        return kernel(*refs[:cut], *refs[cut + len(tokens) :])

    return pl.pallas_call(
        run,
        grid_spec=pltpu.PrefetchScalarGridSpec(
            num_scalar_prefetch=len(scalars),
            grid=grid,
            in_specs=[spec for _, spec in inputs] + [ANYWHERE] * len(tokens),
            out_specs=[spec for _, _, spec in outputs],
            scratch_shapes=scratch,
        ),
        out_shape=[jax.ShapeDtypeStruct(shape, kind) for shape, kind, _ in outputs],
        input_output_aliases=aliases or {},
        cost_estimate=pl.CostEstimate(flops=0, bytes_accessed=int(us * 3.6e6), transcendentals=0),
    )(*scalars, *[array for array, _ in inputs], *tokens)


def constant_spec(shape):
    return pl.BlockSpec(shape, lambda *_: (0,) * len(shape), pipeline_mode=pl.Buffered(1))


def whole(array):
    return (array, constant_spec(array.shape))


def nothing(*refs):
    pass


def after(array, *tokens):
    return call(
        nothing, (), (1,), [(array, ANYWHERE)], [(array.shape, array.dtype, ANYWHERE)], tokens, 0.1, aliases={0: 0}
    )[0]


def own_last(maps, us, tokens=()):
    shape = (SW, *maps.shape[1:])
    last = maps.shape[0] - SW

    def kernel(in_ref, out_ref):
        out_ref[...] = in_ref[...]

    return call(
        kernel,
        (),
        (1,),
        [(maps, pl.BlockSpec(shape, lambda i: (last, 0, 0)))],
        [(shape, maps.dtype, pl.BlockSpec(shape, lambda i: (0, 0, 0)))],
        tokens,
        us,
    )[0]


def masked_rank(adapter, rows, length):
    ranks = lax.dot_general(adapter, rows, ROW_PRODUCT, preferred_element_type=jnp.float32)
    live = lax.broadcasted_iota(jnp.int32, ranks.shape, 1) < length
    return jnp.where(live, ranks, 0.0).astype(rows.dtype)


def rank_terms(lengths, maps, pick, choices, features, each, us, tokens=()):
    blocks, rank, width = maps.shape
    steps = pl.cdiv(blocks, each)

    def kernel(lengths_ref, pick_ref, *refs):
        maps_refs, rows_refs, (out_ref, chosen_ref) = refs[:each], refs[each : 2 * each], refs[-2:]
        step = pl.program_id(0)

        def one(k):
            block = step * each + k
            out_ref[block] = masked_rank(maps_refs[k][0], rows_refs[k][...], lengths_ref[block])

        def last(k):
            for j, choice in enumerate(refs[2 * each : -2]):

                @pl.when(pick_ref[0] == j)
                def _():
                    chosen_ref[...] = choice[...]

            out_ref[blocks - 1] = masked_rank(chosen_ref[0], rows_refs[k][...], lengths_ref[blocks - 1])

        end = blocks - 1 - (steps - 1) * each

        @pl.when(step < steps - 1)
        def _():
            for k in range(each):
                one(k)

        @pl.when(step == steps - 1)
        def _():
            for k in range(end):
                one(k)
            last(end)

    def at(i, k):
        block = i * each + k
        return jnp.where(block < blocks, block, block - each)

    return call(
        kernel,
        (lengths, pick),
        (steps,),
        [(maps, pl.BlockSpec((1, rank, width), lambda i, *_, k=k: (at(i, k), 0, 0))) for k in range(each)]
        + [(features, pl.BlockSpec((BLOCK, width), lambda i, *_, k=k: (at(i, k), 0))) for k in range(each)]
        + [whole(choice) for choice in choices],
        [
            ((blocks, rank, BLOCK), features.dtype, constant_spec((blocks, rank, BLOCK))),
            (choices[0].shape, features.dtype, constant_spec(choices[0].shape)),
        ],
        tokens,
        us,
    )


def summed(pair, at):
    return (pair[0][at].astype(jnp.float32) + pair[1][at].astype(jnp.float32)).astype(pair[0].dtype)


def down_rows(codes, first, parts, copies, ranks, features, us, tokens=()):
    blocks, rank, _ = ranks[0].shape
    width = features.shape[1]

    def block_at(code):
        return jnp.maximum((code >> 1) - 1, 0)

    def kernel(codes_ref, a, b, *refs):
        rows_refs, last_ref, outs, late = refs[:OWN], refs[OWN], refs[OWN + 1 : -1], refs[-1]
        step = pl.program_id(0)

        @pl.when(step == 0)
        def _():
            late[...] = jnp.dot(summed((a, b), blocks - 1), last_ref[...], preferred_element_type=jnp.float32)

        for k in range(OWN):
            code = codes_ref[first + step * OWN + k]
            mine = summed((a, b), block_at(code))
            mine = jnp.where(code > 1, mine, jnp.zeros_like(mine))
            total = jnp.dot(mine, rows_refs[k][...], preferred_element_type=jnp.float32)
            total = total + jnp.where((code & 1) > 0, late[...], 0.0)
            value = (ADAPTER_SCALE * total).astype(features.dtype)
            for part, out_ref in enumerate(outs):
                if len(outs) == 1:
                    out_ref[k] = value
                    continue

                @pl.when(step == min(part, parts - 1))
                def _():
                    out_ref[k] = value

    def rows_spec(k):
        return pl.BlockSpec((BLOCK, width), lambda r, at: (block_at(at[first + r * OWN + k]), 0))

    shape = (OWN, rank, width)
    if copies:
        outs = [(shape, features.dtype, constant_spec(shape))] * (parts - 1 + copies)
    else:
        outs = [((parts * OWN, rank, width), features.dtype, pl.BlockSpec(shape, lambda r, *_: (r, 0, 0)))]
    return call(
        kernel,
        (codes,),
        (parts,),
        [whole(array) for array in ranks]
        + [(features, rows_spec(k)) for k in range(OWN)]
        + [(features, pl.BlockSpec((BLOCK, width), lambda r, *_: (blocks - 1, 0), pipeline_mode=pl.Buffered(1)))],
        outs,
        tokens,
        us,
        [pltpu.VMEM((rank, width), jnp.float32)],
    )


def up_rows(codes, parts, ranks, features, us, tokens=()):
    blocks, rank, _ = ranks[0].shape
    width = features.shape[1]

    def kernel(codes_ref, a, b, rows_ref, *outs):
        late = jnp.dot(
            summed((a, b), blocks - 1), rows_ref[(blocks - 1) * BLOCK :], preferred_element_type=jnp.float32
        )
        done = 0
        for out_ref in outs:

            def one(r, carry, out_ref=out_ref, done=done):
                code = codes_ref[done + r]
                at = jnp.maximum((code >> 1) - 1, 0)
                mine = summed((a, b), at)
                mine = jnp.where(code > 1, mine, jnp.zeros_like(mine))
                mine_rows = rows_ref[pl.ds(pl.multiple_of(at * BLOCK, BLOCK), BLOCK), :]
                total = jnp.dot(mine, mine_rows, preferred_element_type=jnp.float32)
                total = total + jnp.where((code & 1) > 0, late, 0.0)
                out_ref[r] = (ADAPTER_SCALE * total).astype(out_ref.dtype)
                return carry

            if out_ref.shape[0] <= OWN:
                for r in range(out_ref.shape[0]):
                    one(r, 0)
            else:
                lax.fori_loop(0, out_ref.shape[0], one, 0)
            done += out_ref.shape[0]

    return call(
        kernel,
        (codes,),
        (1,),
        [whole(array) for array in (*ranks, features)],
        [((rows, rank, width), features.dtype, constant_spec((rows, rank, width))) for rows in parts],
        tokens,
        us,
    )


def base_terms(columns, hidden, weight, us, tokens=()):
    rows, depth = hidden.shape
    width = weight.shape[1] // 4
    tile = rows // 4

    def kernel(columns_ref, rows_ref, *refs):
        for k in range(4):
            out_ref = refs[4 + k // 2]
            out_ref[k % 2] = jnp.dot(rows_ref[...], refs[k][...], preferred_element_type=jnp.float32).astype(
                out_ref.dtype
            )

    def column(k):
        return pl.BlockSpec((depth, width), lambda i, at: (0, at[k]), pipeline_mode=pl.Buffered(1))

    return call(
        kernel,
        (columns,),
        (rows // tile,),
        [(hidden, pl.BlockSpec((tile, depth), lambda i, *_: (i, 0)))]
        + [(weight, column(k)) for k in range(4)],
        [((2, rows, width), hidden.dtype, pl.BlockSpec((2, tile, width), lambda i, *_: (0, i, 0)))] * 2,
        tokens,
        us,
    )


def values_of(lengths, base, ranks, maps, last_map, us, tokens=()):
    _, rows, width = base[0].shape
    blocks = rows // BLOCK

    def kernel(lengths_ref, one, two, three, a, b, maps_ref, last_ref, out_ref, last_out):
        for k in range(blocks):
            at = slice(k * BLOCK, (k + 1) * BLOCK)
            adapter = maps_ref[k] if k < blocks - 1 else last_ref[0]
            added = lax.dot_general(
                summed((a, b), k), adapter, (((0,), (0,)), ((), ())), preferred_element_type=jnp.float32
            )
            frozen = one[0, at].astype(jnp.float32) + two[0, at].astype(jnp.float32) + three[at].astype(jnp.float32)
            live = lax.broadcasted_iota(jnp.int32, frozen.shape, 0) < lengths_ref[k]
            values = jnp.where(live, frozen + ADAPTER_SCALE * added, 0.0).astype(out_ref.dtype)
            out_ref[at] = values
            if k == blocks - 1:
                last_out[...] = values

    second = pl.BlockSpec((1, rows, width), lambda *_: (1, 0, 0), pipeline_mode=pl.Buffered(1))
    return call(
        kernel,
        (lengths,),
        (1,),
        [(base[0], second), (base[1], second)] + [whole(array) for array in (base[2], *ranks, maps, last_map)],
        [
            ((rows, width), maps.dtype, constant_spec((rows, width))),
            ((BLOCK, width), maps.dtype, constant_spec((BLOCK, width))),
        ],
        tokens,
        us,
    )


def put_last(pick, values, choices, us):
    width = values.shape[1]
    block = values.shape[0] // BLOCK - 1

    def kernel(pick_ref, *refs):
        for k, choice in enumerate(refs[:-2]):

            @pl.when(pick_ref[0] == k)
            def _():
                refs[-1][...] = choice[...]

    return call(
        kernel,
        (pick,),
        (1,),
        [whole(choice) for choice in choices] + [(values, ANYWHERE)],
        [(values.shape, values.dtype, pl.BlockSpec((BLOCK, width), lambda i, *_: (block, 0)))],
        us=us,
        aliases={1 + len(choices): 0},
    )[0]


def shift(array, by):
    size = lax.axis_size("dp")
    return lax.ppermute(array, "dp", [(i, (i + by) % size) for i in range(size)])


def shifted(array, source):
    size = lax.axis_size("dp")
    me = lax.axis_index("dp")
    if size > 4:
        taken = lax.dynamic_index_in_dim(lax.all_gather(array, "dp"), source, 0, keepdims=False)
        return [taken], jnp.zeros((1,), jnp.int32)
    choices = [array] + [shift(array, by) for by in range(1, size)]
    return choices, ((me - source) % size).reshape(1)


def add(*arrays):
    return sum(array.astype(jnp.float32) for array in arrays).astype(arrays[0].dtype)


def near(array):
    size = lax.axis_size("tensor")
    return lax.ppermute(array, "tensor", [(i, i ^ 1) for i in range(size)])


def far(array):
    size = lax.axis_size("tensor")
    return lax.ppermute(array, "tensor", [(i, i ^ 2) for i in range(size)])


def exchanged(array):
    array = add(array, near(array))
    return array, far(array)


def line_reduce_scatter(table):
    size = lax.axis_size("dp")
    me = lax.axis_index("dp")

    def entry(index):
        return lax.dynamic_index_in_dim(table, jnp.clip(index, 0, size - 1), 0, keepdims=False)

    from_left = from_right = None
    for step in range(size - 1):
        right = entry(size - 1 - step + me)
        left = entry(step - (size - 1 - me))
        if step > 0:
            right = add(right, from_left)
            left = add(left, from_right)
        from_left = lax.ppermute(right, "dp", [(i, i + 1) for i in range(step + 1)])
        from_right = lax.ppermute(left, "dp", [(i, i - 1) for i in range(size - 1 - step, size)])
    return entry(me) if size == 1 else add(entry(me), from_left, from_right)


ROLES = ((3, 2, 0, 1), (0, 3, 1, 2), (3, 0, 2, 1), (0, 1, 3, 2))


def body(
    partner,
    block_tenant_index,
    block_live_length,
    tenant_table_row,
    hidden,
    cotangent,
    frozen_value_weight,
    adapter_down_rows,
    adapter_up_matrix,
):
    blocks = block_tenant_index.shape[0]
    kept = blocks - SW
    devices = lax.axis_size("dp")
    me = lax.axis_index("dp")
    column = lax.axis_index("tensor")
    lengths = block_live_length
    line = devices == 4
    order = jnp.arange(devices, dtype=jnp.int32)
    holder = jnp.sum(jnp.where(partner == me, order, 0))

    up_choices, up_pick = shifted(own_last(adapter_up_matrix, 1.0), holder)
    cot_terms, up_last = rank_terms(
        lengths, adapter_up_matrix, up_pick, up_choices, cotangent, blocks, 3.0
    )
    rank_cot = exchanged(cot_terms)
    down_choices, down_pick = shifted(own_last(adapter_down_rows, 1.5, [cot_terms]), holder)

    table_rows = jnp.sum(
        jnp.where(
            block_tenant_index[:, None] == jnp.arange(tenant_table_row.shape[0], dtype=jnp.int32)[None, :],
            tenant_table_row[None, :],
            0,
        ),
        axis=1,
    )
    weights = jnp.where(jnp.arange(blocks) < kept, 2 * (jnp.arange(blocks, dtype=jnp.int32) + 1), 1)

    def codes_of(owners):
        rows = (owners[:, None] * OWN + jnp.arange(OWN, dtype=jnp.int32)[None, :]).reshape(-1)
        return jnp.sum(jnp.where(rows[:, None] == table_rows[None, :], weights[None, :], 0), axis=1)

    if line:
        inner = (me == 1) | (me == 2)
        codes = codes_of(jnp.array(ROLES, jnp.int32)[me])
        (first,) = down_rows(codes, 0, 1, 1, rank_cot, hidden, 3.0)
        from_first = lax.ppermute(first, "dp", [(0, 1), (3, 2), (1, 0), (2, 3)])
        second, own, third, third_too = down_rows(codes, OWN, 3, 2, rank_cot, hidden, 6.0, [first])
        from_inner = lax.ppermute(third, "dp", [(1, 2), (2, 1)])
        second = add(second, jnp.where(inner, from_first, jnp.zeros((), first.dtype)))
        from_second = lax.ppermute(second, "dp", [(0, 2), (3, 1), (1, 3), (2, 0)])
        from_third = lax.ppermute(after(third_too, from_first), "dp", [(0, 1), (3, 2)])
        near_total = lax.optimization_barrier(
            own.astype(jnp.float32)
            + jnp.where(inner, from_inner, from_first).astype(jnp.float32)
        )
        down_out = (near_total + from_second.astype(jnp.float32) + from_third.astype(jnp.float32)).astype(own.dtype)
        start, window = third, second
    else:
        codes = codes_of(order)
        (start,) = down_rows(codes, 0, devices, 0, rank_cot, hidden, 3.0)
        down_out = line_reduce_scatter(start.reshape(devices, OWN, *start.shape[1:]))
        window = start

    in_terms, _ = rank_terms(
        lengths, adapter_down_rows, down_pick, down_choices, hidden, 4, 6.0, [start]
    )
    rank_in = exchanged(in_terms)

    columns = jnp.stack([column ^ 3, column ^ 1, column ^ 2, column]).astype(jnp.int32)
    given, mine = base_terms(columns, hidden, frozen_value_weight, 10.0, [in_terms])
    taken = near(given)
    across = far(add(mine[0], taken[0]))

    if line:
        up_codes = codes_of((me + jnp.array([1, 2, 3, 0], jnp.int32)) % devices)
        *sent, up_own = up_rows(up_codes, [OWN] * 4, rank_in, cotangent, 3.0, [window])
        up_out = add(up_own, *[shift(array, by + 1) for by, array in enumerate(sent)])
    else:
        (up_table,) = up_rows(codes, [devices * OWN], rank_in, cotangent, 3.0)
        up_out = line_reduce_scatter(up_table.reshape(devices, OWN, *up_table.shape[1:]))

    values, last_values = values_of(
        lengths, (mine, taken, across), rank_in, adapter_up_matrix, up_last, 4.0, [window]
    )
    value_choices, value_pick = shifted(last_values, partner[me])
    projected_values = put_last(value_pick, values, value_choices, 1.5)
    return (projected_values, down_out, up_out)


def solution(mesh):
    in_specs = (
        P("groups"),
        P(("groups", "dp")),
        P(("groups", "dp")),
        P("groups"),
        P(("groups", "dp"), "tensor"),
        P(("groups", "dp"), "tensor"),
        P("tensor", None),
        P(("groups", "dp"), None, "tensor"),
        P(("groups", "dp"), None, "tensor"),
    )
    out_specs = (
        P(("groups", "dp"), "tensor"),
        P(("groups", "dp"), None, "tensor"),
        P(("groups", "dp"), None, "tensor"),
    )
    return jax.shard_map(body, mesh=mesh, in_specs=in_specs, out_specs=out_specs, check_vma=False)
```

```python
import jax
import jax.numpy as jnp
from jax import lax
from jax.experimental import pallas as pl
from jax.experimental.pallas import tpu as pltpu
from jax.sharding import PartitionSpec as P

BLOCK = 128
SW = 1
OWN = 4


ADAPTER_SCALE = 0.5

ANYWHERE = pl.BlockSpec(memory_space=pl.ANY)
ROW_PRODUCT = (((1,), (1,)), ((), ()))


def call(kernel, scalars, grid, inputs, outputs, tokens=(), us=1.0, scratch=(), aliases=None):
    def run(*refs):
        cut = len(scalars) + len(inputs)
        return kernel(*refs[:cut], *refs[cut + len(tokens) :])

    return pl.pallas_call(
        run,
        grid_spec=pltpu.PrefetchScalarGridSpec(
            num_scalar_prefetch=len(scalars),
            grid=grid,
            in_specs=[spec for _, spec in inputs] + [ANYWHERE] * len(tokens),
            out_specs=[spec for _, _, spec in outputs],
            scratch_shapes=scratch,
        ),
        out_shape=[jax.ShapeDtypeStruct(shape, kind) for shape, kind, _ in outputs],
        input_output_aliases=aliases or {},
        cost_estimate=pl.CostEstimate(flops=0, bytes_accessed=int(us * 3.6e5), transcendentals=0),
    )(*scalars, *[array for array, _ in inputs], *tokens)


def constant_spec(shape):
    return pl.BlockSpec(shape, lambda *_: (0,) * len(shape), pipeline_mode=pl.Buffered(1))


def whole(array):
    return (array, constant_spec(array.shape))


def nothing(*refs):
    pass


def after(array, *tokens):
    return call(
        nothing, (), (1,), [(array, ANYWHERE)], [(array.shape, array.dtype, ANYWHERE)], tokens, 0.1, aliases={0: 0}
    )[0]


def own_last(maps, tokens=()):
    shape = (SW, *maps.shape[1:])
    last = maps.shape[0] - SW

    def kernel(in_ref, out_ref):
        out_ref[...] = in_ref[...]

    return call(
        kernel,
        (),
        (1,),
        [(maps, pl.BlockSpec(shape, lambda i: (last, 0, 0)))],
        [(shape, maps.dtype, pl.BlockSpec(shape, lambda i: (0, 0, 0)))],
        tokens,
    )[0]


def chosen(pick, choices, tokens=()):
    def kernel(pick_ref, *refs):
        for k, choice in enumerate(refs[:-1]):

            @pl.when(pick_ref[0] == k)
            def _():
                refs[-1][...] = choice[...]

    shape = choices[0].shape
    return call(
        kernel,
        (pick,),
        (1,),
        [whole(choice) for choice in choices],
        [(shape, choices[0].dtype, constant_spec(shape))],
        tokens,
    )[0]


def masked_rank(adapter, rows, length):
    ranks = lax.dot_general(adapter, rows, ROW_PRODUCT, preferred_element_type=jnp.float32)
    live = lax.broadcasted_iota(jnp.int32, ranks.shape, 1) < length
    return jnp.where(live, ranks, 0.0).astype(rows.dtype)


def kept_ranks(lengths, maps, features):
    blocks, rank, width = maps.shape
    kept = blocks - SW

    def kernel(lengths_ref, maps_ref, rows_ref, out_ref, last_ref):
        last_ref[...] = maps_ref[kept:]
        for k in range(kept):
            out_ref[k] = masked_rank(maps_ref[k], rows_ref[k * BLOCK : (k + 1) * BLOCK], lengths_ref[k])

    return call(
        kernel,
        (lengths,),
        (1,),
        [whole(maps), whole(features)],
        [
            ((kept, rank, BLOCK), features.dtype, constant_spec((kept, rank, BLOCK))),
            ((SW, rank, width), features.dtype, constant_spec((SW, rank, width))),
        ],
    )


def last_ranks(lengths, pick, choices, features):
    shape = choices[0].shape
    block = features.shape[0] // BLOCK - 1

    def kernel(lengths_ref, pick_ref, *refs):
        rows_ref, out_ref, chosen_ref = refs[-3:]
        for k, choice in enumerate(refs[:-3]):

            @pl.when(pick_ref[0] == k)
            def _():
                chosen_ref[...] = choice[...]

        out_ref[0] = masked_rank(chosen_ref[0], rows_ref[...], lengths_ref[block])

    return call(
        kernel,
        (lengths, pick),
        (1,),
        [whole(choice) for choice in choices]
        + [(features, pl.BlockSpec((BLOCK, shape[2]), lambda i, *_: (block, 0), pipeline_mode=pl.Buffered(1)))],
        [
            ((1, shape[1], BLOCK), features.dtype, constant_spec((1, shape[1], BLOCK))),
            (shape, features.dtype, constant_spec(shape)),
        ],
    )


def rank_terms(lengths, maps, pick, choices, features, each, tokens=()):
    blocks, rank, width = maps.shape
    steps = pl.cdiv(blocks, each)

    def kernel(lengths_ref, pick_ref, *refs):
        maps_refs, rows_refs, (out_ref, chosen_ref) = refs[:each], refs[each : 2 * each], refs[-2:]
        step = pl.program_id(0)

        def one(k):
            block = step * each + k
            out_ref[block] = masked_rank(maps_refs[k][0], rows_refs[k][...], lengths_ref[block])

        def last(k):
            for j, choice in enumerate(refs[2 * each : -2]):

                @pl.when(pick_ref[0] == j)
                def _():
                    chosen_ref[...] = choice[...]

            out_ref[blocks - 1] = masked_rank(chosen_ref[0], rows_refs[k][...], lengths_ref[blocks - 1])

        end = blocks - 1 - (steps - 1) * each

        @pl.when(step < steps - 1)
        def _():
            for k in range(each):
                one(k)

        @pl.when(step == steps - 1)
        def _():
            for k in range(end):
                one(k)
            last(end)

    def at(i, k):
        block = i * each + k
        return jnp.where(block < blocks, block, block - each)

    return call(
        kernel,
        (lengths, pick),
        (steps,),
        [(maps, pl.BlockSpec((1, rank, width), lambda i, *_, k=k: (at(i, k), 0, 0))) for k in range(each)]
        + [(features, pl.BlockSpec((BLOCK, width), lambda i, *_, k=k: (at(i, k), 0))) for k in range(each)]
        + [whole(choice) for choice in choices],
        [
            ((blocks, rank, BLOCK), features.dtype, constant_spec((blocks, rank, BLOCK))),
            (choices[0].shape, features.dtype, constant_spec(choices[0].shape)),
        ],
        tokens,
    )


def summed(terms, at):
    return sum(term[at].astype(jnp.float32) for term in terms).astype(terms[0].dtype)


def down_rows(codes, first, parts, copies, ranks, last, features, tokens=()):
    kept, rank, _ = ranks[0].shape
    width = features.shape[1]
    piece = min(width, 512)

    def block_at(code):
        return jnp.maximum((code >> 1) - 1, 0)

    def kernel(codes_ref, a, b, *refs):
        lasts, refs = refs[: len(last)], refs[len(last) :]
        rows_refs, last_ref, outs = refs[:OWN], refs[OWN], refs[OWN + 1 :]
        step = pl.program_id(0)

        def fill(to):
            for k in range(OWN):
                code = codes_ref[first + step * OWN + k]
                mine = summed((a, b), block_at(code))
                mine = jnp.where(code > 1, mine, jnp.zeros_like(mine))

                def put(at, total):
                    value = (ADAPTER_SCALE * total).astype(features.dtype)
                    for out_ref in to:
                        out_ref[k, :, at] = value

                for at in [slice(c, c + piece) for c in range(0, width, piece)]:
                    put(at, jnp.dot(mine, rows_refs[k][:, at], preferred_element_type=jnp.float32))

                @pl.when((code & 1) > 0)
                def _():
                    late = summed(lasts, 0)
                    for at in [slice(c, c + piece) for c in range(0, width, piece)]:
                        put(
                            at,
                            jnp.dot(mine, rows_refs[k][:, at], preferred_element_type=jnp.float32)
                            + jnp.dot(late, last_ref[:, at], preferred_element_type=jnp.float32),
                        )

        if not copies or parts == 1:
            fill(outs)
        else:
            for part in range(parts):

                @pl.when(step == part)
                def _():
                    fill(outs[part:] if part == parts - 1 else outs[part : part + 1])

    def rows_spec(k):
        return pl.BlockSpec((BLOCK, width), lambda r, at: (block_at(at[first + r * OWN + k]), 0))

    shape = (OWN, rank, width)
    if copies:
        outs = [(shape, features.dtype, constant_spec(shape))] * (parts - 1 + copies)
    else:
        outs = [((parts * OWN, rank, width), features.dtype, pl.BlockSpec(shape, lambda r, *_: (r, 0, 0)))]
    return call(
        kernel,
        (codes,),
        (parts,),
        [whole(array) for array in (*ranks, *last)]
        + [(features, rows_spec(k)) for k in range(OWN)]
        + [(features, pl.BlockSpec((BLOCK, width), lambda r, *_: (kept, 0), pipeline_mode=pl.Buffered(1)))],
        outs,
        tokens,
    )


def up_rows(codes, parts, ranks, features, tokens=()):
    blocks, rank, _ = ranks[0].shape
    width = features.shape[1]

    def kernel(codes_ref, a, b, rows_ref, *outs):
        late = jnp.dot(
            summed((a, b), blocks - 1), rows_ref[(blocks - 1) * BLOCK :], preferred_element_type=jnp.float32
        )
        done = 0
        for out_ref in outs:

            def one(r, carry, out_ref=out_ref, done=done):
                code = codes_ref[done + r]
                at = jnp.maximum((code >> 1) - 1, 0)
                mine = summed((a, b), at)
                mine = jnp.where(code > 1, mine, jnp.zeros_like(mine))
                mine_rows = rows_ref[pl.ds(pl.multiple_of(at * BLOCK, BLOCK), BLOCK), :]
                total = jnp.dot(mine, mine_rows, preferred_element_type=jnp.float32)
                total = total + jnp.where((code & 1) > 0, late, 0.0)
                out_ref[r] = (ADAPTER_SCALE * total).astype(out_ref.dtype)
                return carry

            if out_ref.shape[0] <= OWN:
                for r in range(out_ref.shape[0]):
                    one(r, 0)
            else:
                lax.fori_loop(0, out_ref.shape[0], one, 0)
            done += out_ref.shape[0]

    return call(
        kernel,
        (codes,),
        (1,),
        [whole(array) for array in (*ranks, features)],
        [((rows, rank, width), features.dtype, constant_spec((rows, rank, width))) for rows in parts],
        tokens,
    )


def base_terms(columns, hidden, weight, tokens=()):
    rows, depth = hidden.shape
    width = weight.shape[1] // 4
    tile = rows // 4

    def kernel(columns_ref, rows_ref, *refs):
        for k in range(4):
            out_ref = refs[4 + k // 2]
            out_ref[k % 2] = jnp.dot(rows_ref[...], refs[k][...], preferred_element_type=jnp.float32).astype(
                out_ref.dtype
            )

    def column(k):
        return pl.BlockSpec((depth, width), lambda i, at: (0, at[k]), pipeline_mode=pl.Buffered(1))

    return call(
        kernel,
        (columns,),
        (rows // tile,),
        [(hidden, pl.BlockSpec((tile, depth), lambda i, *_: (i, 0)))]
        + [(weight, column(k)) for k in range(4)],
        [((2, rows, width), hidden.dtype, pl.BlockSpec((2, tile, width), lambda i, *_: (0, i, 0)))] * 2,
        tokens,
    )


def values_of(lengths, base, ranks, maps, last_map, tokens=()):
    _, rows, width = base[0].shape
    blocks = rows // BLOCK

    def kernel(lengths_ref, one, two, three, a, b, maps_ref, last_ref, out_ref, last_out):
        for k in range(blocks):
            at = slice(k * BLOCK, (k + 1) * BLOCK)
            adapter = maps_ref[k] if k < blocks - 1 else last_ref[0]
            added = lax.dot_general(
                summed((a, b), k), adapter, (((0,), (0,)), ((), ())), preferred_element_type=jnp.float32
            )
            frozen = one[0, at].astype(jnp.float32) + two[0, at].astype(jnp.float32) + three[at].astype(jnp.float32)
            live = lax.broadcasted_iota(jnp.int32, frozen.shape, 0) < lengths_ref[k]
            values = jnp.where(live, frozen + ADAPTER_SCALE * added, 0.0).astype(out_ref.dtype)
            out_ref[at] = values
            if k == blocks - 1:
                last_out[...] = values

    second = pl.BlockSpec((1, rows, width), lambda *_: (1, 0, 0), pipeline_mode=pl.Buffered(1))
    return call(
        kernel,
        (lengths,),
        (1,),
        [(base[0], second), (base[1], second)] + [whole(array) for array in (base[2], *ranks, maps, last_map)],
        [
            ((rows, width), maps.dtype, constant_spec((rows, width))),
            ((BLOCK, width), maps.dtype, constant_spec((BLOCK, width))),
        ],
        tokens,
    )


def put_last(pick, values, choices):
    width = values.shape[1]
    block = values.shape[0] // BLOCK - 1

    def kernel(pick_ref, *refs):
        for k, choice in enumerate(refs[:-2]):

            @pl.when(pick_ref[0] == k)
            def _():
                refs[-1][...] = choice[...]

    return call(
        kernel,
        (pick,),
        (1,),
        [whole(choice) for choice in choices] + [(values, ANYWHERE)],
        [(values.shape, values.dtype, pl.BlockSpec((BLOCK, width), lambda i, *_: (block, 0)))],
        aliases={1 + len(choices): 0},
    )[0]


def shift(array, by):
    size = lax.axis_size("dp")
    return lax.ppermute(array, "dp", [(i, (i + by) % size) for i in range(size)])


def shifted(array, source):
    size = lax.axis_size("dp")
    me = lax.axis_index("dp")
    if size > 4:
        taken = lax.dynamic_index_in_dim(lax.all_gather(array, "dp"), source, 0, keepdims=False)
        return [taken], jnp.zeros((1,), jnp.int32)
    choices = [array] + [shift(array, by) for by in range(1, size)]
    return choices, ((me - source) % size).reshape(1)


def routed(array, partner, tokens):
    size = lax.axis_size("dp")
    me = lax.axis_index("dp")
    order = jnp.arange(size, dtype=jnp.int32)
    holders = jnp.sum(jnp.where(partner[None, :] == order[:, None], order[None, :], 0), axis=1)
    source = jnp.sum(jnp.where(partner == me, order, 0))
    if size != 4:
        return shifted(array, source)
    from_left = lax.ppermute(array, "dp", [(0, 1), (1, 2)])
    from_right = lax.ppermute(array, "dp", [(3, 2), (2, 1)])

    def scalar(value):
        return value.reshape(1).astype(jnp.int32)

    def place(wanted):
        return jnp.where(wanted == me, 0, jnp.where(wanted == me - 1, 1, jnp.where(wanted == me + 1, 2, 3)))

    passed = chosen(scalar(jnp.where(me == 1, 0, 1)), [from_left, from_right], tokens[:1])
    passed = lax.ppermute(passed, "dp", [(1, 2), (2, 1)])
    choices = [array, from_left, from_right, passed]
    outward = chosen(scalar(place(jnp.where(me == 1, holders[0], holders[3]))), choices, tokens[1:])
    outward = lax.ppermute(outward, "dp", [(2, 3), (1, 0)])
    inner = (me == 1) | (me == 2)
    pick = jnp.where(inner | (source == me), place(source), 4)
    return [*choices, outward], scalar(pick)


def add(*arrays):
    return sum(array.astype(jnp.float32) for array in arrays).astype(arrays[0].dtype)


def crossed(array, by):
    return lax.ppermute(array, "tensor", [(i, i ^ by) for i in range(lax.axis_size("tensor"))])


def near(array):
    return crossed(array, 1)


def far(array):
    return crossed(array, 2)


def exchanged(array):
    array = add(array, near(array))
    return array, far(array)


def line_reduce_scatter(table):
    size = lax.axis_size("dp")
    me = lax.axis_index("dp")

    def entry(index):
        return lax.dynamic_index_in_dim(table, jnp.clip(index, 0, size - 1), 0, keepdims=False)

    from_left = from_right = None
    for step in range(size - 1):
        right = entry(size - 1 - step + me)
        left = entry(step - (size - 1 - me))
        if step > 0:
            right = add(right, from_left)
            left = add(left, from_right)
        from_left = lax.ppermute(right, "dp", [(i, i + 1) for i in range(step + 1)])
        from_right = lax.ppermute(left, "dp", [(i, i - 1) for i in range(size - 1 - step, size)])
    return entry(me) if size == 1 else add(entry(me), from_left, from_right)


ROLES = ((3, 2, 0, 1), (0, 3, 1, 2), (3, 0, 2, 1), (0, 1, 3, 2))


def body(
    partner,
    block_tenant_index,
    block_live_length,
    tenant_table_row,
    hidden,
    cotangent,
    frozen_value_weight,
    adapter_down_rows,
    adapter_up_matrix,
):
    blocks = block_tenant_index.shape[0]
    kept = blocks - SW
    devices = lax.axis_size("dp")
    me = lax.axis_index("dp")
    column = lax.axis_index("tensor")
    lengths = block_live_length
    line = devices == 4
    order = jnp.arange(devices, dtype=jnp.int32)
    holder = jnp.sum(jnp.where(partner == me, order, 0))

    cot_terms, up_own = kept_ranks(lengths, adapter_up_matrix, cotangent)
    rank_cot = exchanged(cot_terms)
    last_terms, up_last = last_ranks(lengths, *shifted(up_own, holder)[::-1], cotangent)
    last_cot = [last_terms] + [crossed(last_terms, by) for by in range(1, lax.axis_size("tensor"))]

    table_rows = jnp.sum(
        jnp.where(
            block_tenant_index[:, None] == jnp.arange(tenant_table_row.shape[0], dtype=jnp.int32)[None, :],
            tenant_table_row[None, :],
            0,
        ),
        axis=1,
    )
    weights = jnp.where(jnp.arange(blocks) < kept, 2 * (jnp.arange(blocks, dtype=jnp.int32) + 1), 1)

    def codes_of(owners):
        rows = (owners[:, None] * OWN + jnp.arange(OWN, dtype=jnp.int32)[None, :]).reshape(-1)
        return jnp.sum(jnp.where(rows[:, None] == table_rows[None, :], weights[None, :], 0), axis=1)

    columns = jnp.stack([column ^ 3, column ^ 1, column ^ 2, column]).astype(jnp.int32)

    def base(token):
        given, mine = base_terms(columns, hidden, frozen_value_weight, [token])
        taken = near(given)
        return mine, taken, far(add(mine[0], taken[0]))

    down_own = own_last(adapter_down_rows, [rank_cot[0]])
    if line:
        inner = (me == 1) | (me == 2)
        codes = codes_of(jnp.array(ROLES, jnp.int32)[me])
        (first,) = down_rows(codes, 0, 1, 1, rank_cot, last_cot, hidden)
        from_first = lax.ppermute(first, "dp", [(0, 1), (3, 2), (1, 0), (2, 3)])
        second, own, third, third_too = down_rows(codes, OWN, 3, 2, rank_cot, last_cot, hidden, [first])
        from_inner = lax.ppermute(third, "dp", [(1, 2), (2, 1)])
        down_choices, down_pick = routed(down_own, partner, [first, third])
        base_parts = base(third)
        second = add(after(second, base_parts[0]), jnp.where(inner, from_first, jnp.zeros((), first.dtype)))
        from_second = lax.ppermute(second, "dp", [(0, 2), (3, 1), (1, 3), (2, 0)])
        from_third = lax.ppermute(after(third_too, from_first), "dp", [(0, 1), (3, 2)])
        near_total = lax.optimization_barrier(
            after(own, second).astype(jnp.float32) + jnp.where(inner, from_inner, from_first).astype(jnp.float32)
        )
        down_out = (near_total + from_second.astype(jnp.float32) + from_third.astype(jnp.float32)).astype(own.dtype)
        window = second
    else:
        codes = codes_of(order)
        (table,) = down_rows(codes, 0, devices, 0, rank_cot, last_cot, hidden)
        down_out = line_reduce_scatter(table.reshape(devices, OWN, *table.shape[1:]))
        down_choices, down_pick = routed(down_own, partner, [])
        base_parts = base(table)
        window = table

    in_terms, _ = rank_terms(lengths, adapter_down_rows, down_pick, down_choices, hidden, 4, [window])
    rank_in = exchanged(in_terms)
    if line:
        up_codes = codes_of((me + jnp.array([1, 2, 3, 0], jnp.int32)) % devices)
        *sent, up_kept = up_rows(up_codes, [OWN] * 4, rank_in, cotangent)
        up_out = add(up_kept, *[shift(array, by + 1) for by, array in enumerate(sent)])
    else:
        (up_table,) = up_rows(codes, [devices * OWN], rank_in, cotangent)
        up_out = line_reduce_scatter(up_table.reshape(devices, OWN, *up_table.shape[1:]))

    values, last_values = values_of(lengths, base_parts, rank_in, adapter_up_matrix, up_last)
    value_choices, value_pick = shifted(last_values, partner[me])
    projected_values = put_last(value_pick, values, value_choices)
    return (projected_values, down_out, up_out)


def solution(mesh):
    in_specs = (
        P("groups"),
        P(("groups", "dp")),
        P(("groups", "dp")),
        P("groups"),
        P(("groups", "dp"), "tensor"),
        P(("groups", "dp"), "tensor"),
        P("tensor", None),
        P(("groups", "dp"), None, "tensor"),
        P(("groups", "dp"), None, "tensor"),
    )
    out_specs = (
        P(("groups", "dp"), "tensor"),
        P(("groups", "dp"), None, "tensor"),
        P(("groups", "dp"), None, "tensor"),
    )
    return jax.shard_map(body, mesh=mesh, in_specs=in_specs, out_specs=out_specs, check_vma=False)
```

```python
import jax
import jax.numpy as jnp
from jax import lax
from jax.experimental import pallas as pl
from jax.experimental.pallas import tpu as pltpu
from jax.sharding import PartitionSpec as P

BLOCK = 128
SW = 1
OWN = 4


ADAPTER_SCALE = 0.5

ANYWHERE = pl.BlockSpec(memory_space=pl.ANY)
ROW_PRODUCT = (((1,), (1,)), ((), ()))


def call(kernel, scalars, grid, inputs, outputs, tokens=(), us=1.0, scratch=(), aliases=None):
    def run(*refs):
        cut = len(scalars) + len(inputs)
        return kernel(*refs[:cut], *refs[cut + len(tokens) :])

    return pl.pallas_call(
        run,
        grid_spec=pltpu.PrefetchScalarGridSpec(
            num_scalar_prefetch=len(scalars),
            grid=grid,
            in_specs=[spec for _, spec in inputs] + [ANYWHERE] * len(tokens),
            out_specs=[spec for _, _, spec in outputs],
            scratch_shapes=scratch,
        ),
        out_shape=[jax.ShapeDtypeStruct(shape, kind) for shape, kind, _ in outputs],
        input_output_aliases=aliases or {},
        cost_estimate=pl.CostEstimate(flops=int(us * 1e9), bytes_accessed=int(us * 3.6e5), transcendentals=0),
    )(*scalars, *[array for array, _ in inputs], *tokens)


def constant_spec(shape):
    return pl.BlockSpec(shape, lambda *_: (0,) * len(shape), pipeline_mode=pl.Buffered(1))


def whole(array):
    return (array, constant_spec(array.shape))


def nothing(*refs):
    pass


def after(array, *tokens):
    return call(
        nothing, (), (1,), [(array, ANYWHERE)], [(array.shape, array.dtype, ANYWHERE)], tokens, 0.1, aliases={0: 0}
    )[0]


def masked_rank(adapter, rows, length):
    ranks = lax.dot_general(adapter, rows, ROW_PRODUCT, preferred_element_type=jnp.float32)
    live = lax.broadcasted_iota(jnp.int32, ranks.shape, 1) < length
    return jnp.where(live, ranks, 0.0).astype(rows.dtype)


def kept_ranks(lengths, maps, features, others):
    blocks, rank, width = maps.shape
    kept = blocks - SW
    last_shapes = [(SW, rank, width), (SW, *others.shape[1:])]

    def kernel(lengths_ref, maps_ref, rows_ref, others_ref, out_ref, last_ref, last_other):
        last_ref[...] = maps_ref[kept:]
        last_other[...] = others_ref[...]
        for k in range(kept):
            out_ref[k] = masked_rank(maps_ref[k], rows_ref[k * BLOCK : (k + 1) * BLOCK], lengths_ref[k])

    return call(
        kernel,
        (lengths,),
        (1,),
        [
            whole(maps),
            whole(features),
            (others, pl.BlockSpec(last_shapes[1], lambda i, *_: (kept, 0, 0), pipeline_mode=pl.Buffered(1))),
        ],
        [((kept, rank, BLOCK), features.dtype, constant_spec((kept, rank, BLOCK)))]
        + [(shape, features.dtype, constant_spec(shape)) for shape in last_shapes],
    )


def streamed_ranks(lengths, maps, features, each, tokens=()):
    blocks, rank, width = maps.shape
    kept = blocks - SW

    def kernel(lengths_ref, *refs):
        step = pl.program_id(0)
        for k in range(each):
            refs[-1][k] = masked_rank(refs[k][0], refs[each + k][...], lengths_ref[step * each + k])

    return call(
        kernel,
        (lengths,),
        (kept // each,),
        [(maps, pl.BlockSpec((1, rank, width), lambda i, *_, k=k: (i * each + k, 0, 0))) for k in range(each)]
        + [(features, pl.BlockSpec((BLOCK, width), lambda i, *_, k=k: (i * each + k, 0))) for k in range(each)],
        [((kept, rank, BLOCK), features.dtype, pl.BlockSpec((each, rank, BLOCK), lambda i, *_: (i, 0, 0)))],
        tokens,
    )[0]


def last_ranks(lengths, pick, choices, features, tokens=()):
    shape = choices[0].shape
    block = features.shape[0] // BLOCK - 1

    def kernel(lengths_ref, pick_ref, *refs):
        rows_ref, out_ref, chosen_ref = refs[-3:]
        for k, choice in enumerate(refs[:-3]):

            @pl.when(pick_ref[0] == k)
            def _():
                chosen_ref[...] = choice[...]

        out_ref[0] = masked_rank(chosen_ref[0], rows_ref[...], lengths_ref[block])

    return call(
        kernel,
        (lengths, pick),
        (1,),
        [whole(choice) for choice in choices]
        + [(features, pl.BlockSpec((BLOCK, shape[2]), lambda i, *_: (block, 0), pipeline_mode=pl.Buffered(1)))],
        [
            ((1, shape[1], BLOCK), features.dtype, constant_spec((1, shape[1], BLOCK))),
            (shape, features.dtype, constant_spec(shape)),
        ],
        tokens,
    )


def summed(terms, at):
    return sum(term[at].astype(jnp.float32) for term in terms).astype(terms[0].dtype)


def down_rows(codes, first, parts, copies, ranks, last, features, tokens=(), us=1.0):
    kept, rank, _ = ranks[0].shape
    width = features.shape[1]
    piece = min(width, 512)

    def block_at(code):
        return jnp.maximum((code >> 1) - 1, 0)

    def kernel(codes_ref, a, b, *refs):
        lasts, refs = refs[: len(last)], refs[len(last) :]
        rows_refs, last_ref, outs = refs[:OWN], refs[OWN], refs[OWN + 1 :]
        step = pl.program_id(0)

        def fill(to):
            for k in range(OWN):
                code = codes_ref[first + step * OWN + k]
                mine = summed((a, b), block_at(code))
                mine = jnp.where(code > 1, mine, jnp.zeros_like(mine))

                def put(at, total):
                    value = (ADAPTER_SCALE * total).astype(features.dtype)
                    for out_ref in to:
                        out_ref[k, :, at] = value

                for at in [slice(c, c + piece) for c in range(0, width, piece)]:
                    put(at, jnp.dot(mine, rows_refs[k][:, at], preferred_element_type=jnp.float32))

                @pl.when((code & 1) > 0)
                def _():
                    late = summed(lasts, 0)
                    for at in [slice(c, c + piece) for c in range(0, width, piece)]:
                        put(
                            at,
                            jnp.dot(mine, rows_refs[k][:, at], preferred_element_type=jnp.float32)
                            + jnp.dot(late, last_ref[:, at], preferred_element_type=jnp.float32),
                        )

        if not copies or parts == 1:
            fill(outs)
        else:
            for part in range(parts):

                @pl.when(step == part)
                def _():
                    fill(outs[part:] if part == parts - 1 else outs[part : part + 1])

    def rows_spec(k):
        return pl.BlockSpec((BLOCK, width), lambda r, at: (block_at(at[first + r * OWN + k]), 0))

    shape = (OWN, rank, width)
    if copies:
        outs = [(shape, features.dtype, constant_spec(shape))] * (parts - 1 + copies)
    else:
        outs = [((parts * OWN, rank, width), features.dtype, pl.BlockSpec(shape, lambda r, *_: (r, 0, 0)))]
    return call(
        kernel,
        (codes,),
        (parts,),
        [whole(array) for array in (*ranks, *last)]
        + [(features, rows_spec(k)) for k in range(OWN)]
        + [(features, pl.BlockSpec((BLOCK, width), lambda r, *_: (kept, 0), pipeline_mode=pl.Buffered(1)))],
        outs,
        tokens,
        us,
    )


def outputs_of(lengths, codes, parts, base, ranks, last, features, maps, last_map):
    rows, width = base[0].shape
    blocks = rows // BLOCK
    rank = maps.shape[1]

    def kernel(lengths_ref, codes_ref, one, two, three, *refs):
        terms, refs = refs[: len(ranks)], refs[len(ranks) :]
        lasts, refs = refs[: len(last)], refs[len(last) :]
        rows_ref, maps_ref, last_ref, out_ref, *outs = refs
        late = summed(lasts, 0)
        for k in range(blocks):
            at = slice(k * BLOCK, (k + 1) * BLOCK)
            adapter = maps_ref[k] if k < blocks - 1 else last_ref[0]
            added = lax.dot_general(
                summed(terms, k) if k < blocks - 1 else late,
                adapter,
                (((0,), (0,)), ((), ())),
                preferred_element_type=jnp.float32,
            )
            frozen = one[at].astype(jnp.float32) + two[at].astype(jnp.float32) + three[at].astype(jnp.float32)
            live = lax.broadcasted_iota(jnp.int32, frozen.shape, 0) < lengths_ref[k]
            values = jnp.where(live, frozen + ADAPTER_SCALE * added, 0.0).astype(out_ref.dtype)
            out_ref[at] = values
            if k == blocks - 1:
                for count, out in zip(parts, outs):
                    out[count * rank :] = values
        late_rows = jnp.dot(late, rows_ref[(blocks - 1) * BLOCK :], preferred_element_type=jnp.float32)
        done = 0
        for count, out in zip(parts, outs):

            def one_row(r, carry, out=out, done=done):
                code = codes_ref[done + r]
                at = jnp.maximum((code >> 1) - 1, 0)
                mine = summed(terms, at)
                mine = jnp.where(code > 1, mine, jnp.zeros_like(mine))
                mine_rows = rows_ref[pl.ds(pl.multiple_of(at * BLOCK, BLOCK), BLOCK), :]
                total = jnp.dot(mine, mine_rows, preferred_element_type=jnp.float32)
                total = total + jnp.where((code & 1) > 0, late_rows, 0.0)
                to = r * rank if isinstance(r, int) else pl.ds(pl.multiple_of(r * rank, rank), rank)
                to = slice(to, to + rank) if isinstance(r, int) else to
                out[to] = (ADAPTER_SCALE * total).astype(out.dtype)
                return carry

            if count <= OWN:
                for r in range(count):
                    one_row(r, 0)
            else:
                lax.fori_loop(0, count, one_row, 0)
            done += count

    return call(
        kernel,
        (lengths, codes),
        (1,),
        [whole(array) for array in (*base, *ranks, *last, features, maps, last_map)],
        [((rows, width), maps.dtype, constant_spec((rows, width)))]
        + [
            ((count * rank + BLOCK, width), maps.dtype, constant_spec((count * rank + BLOCK, width)))
            for count in parts
        ],
    )


def finish(pick, values, own, arrived):
    width = values.shape[1]
    block = values.shape[0] // BLOCK - 1
    rows = own.shape[0] - BLOCK

    def kernel(pick_ref, *refs):
        choices, table_ref, last_ref = refs[:-3], refs[-2], refs[-1]
        table_ref[...] = sum(choice[:rows].astype(jnp.float32) for choice in choices).astype(own.dtype)
        for k, choice in enumerate(choices):

            @pl.when(pick_ref[0] == k)
            def _():
                last_ref[...] = choice[rows:]

    return call(
        kernel,
        (pick,),
        (1,),
        [whole(choice) for choice in (own, *arrived)] + [(values, ANYWHERE)],
        [
            ((rows, width), own.dtype, constant_spec((rows, width))),
            (values.shape, values.dtype, pl.BlockSpec((BLOCK, width), lambda i, *_: (block, 0))),
        ],
        aliases={2 + len(arrived): 1},
    )


def base_terms(columns, hidden, weight, tokens=()):
    rows, depth = hidden.shape
    width = weight.shape[1] // 4
    tile = rows // 4

    def kernel(columns_ref, rows_ref, *refs):
        for k in range(4):
            out_ref = refs[4 + k]
            out_ref[...] = jnp.dot(rows_ref[...], refs[k][...], preferred_element_type=jnp.float32).astype(out_ref.dtype)

    def column(k):
        return pl.BlockSpec((depth, width), lambda i, at: (0, at[k]), pipeline_mode=pl.Buffered(1))

    return call(
        kernel,
        (columns,),
        (rows // tile,),
        [(hidden, pl.BlockSpec((tile, depth), lambda i, *_: (i, 0)))]
        + [(weight, column(k)) for k in range(4)],
        [((rows, width), hidden.dtype, pl.BlockSpec((tile, width), lambda i, *_: (i, 0)))] * 4,
        tokens,
        100.0,
    )


def shift(array, by):
    size = lax.axis_size("dp")
    return lax.ppermute(array, "dp", [(i, (i + by) % size) for i in range(size)])


def shifted(array, source):
    size = lax.axis_size("dp")
    me = lax.axis_index("dp")
    if size > 4:
        taken = lax.dynamic_index_in_dim(lax.all_gather(array, "dp"), source, 0, keepdims=False)
        return [taken], jnp.zeros((1,), jnp.int32)
    choices = [array] + [shift(array, by) for by in range(1, size)]
    return choices, ((me - source) % size).reshape(1)


def add(*arrays):
    return sum(array.astype(jnp.float32) for array in arrays).astype(arrays[0].dtype)


def crossed(array, by):
    return lax.ppermute(array, "tensor", [(i, i ^ by) for i in range(lax.axis_size("tensor"))])


def near(array):
    return crossed(array, 1)


def far(array):
    return crossed(array, 2)


def exchanged(array):
    array = add(array, near(array))
    return array, far(array)


def spread(array):
    return [array] + [crossed(array, by) for by in range(1, lax.axis_size("tensor"))]


def line_reduce_scatter(table):
    size = lax.axis_size("dp")
    me = lax.axis_index("dp")

    def entry(index):
        return lax.dynamic_index_in_dim(table, jnp.clip(index, 0, size - 1), 0, keepdims=False)

    from_left = from_right = None
    for step in range(size - 1):
        right = entry(size - 1 - step + me)
        left = entry(step - (size - 1 - me))
        if step > 0:
            right = add(right, from_left)
            left = add(left, from_right)
        from_left = lax.ppermute(right, "dp", [(i, i + 1) for i in range(step + 1)])
        from_right = lax.ppermute(left, "dp", [(i, i - 1) for i in range(size - 1 - step, size)])
    return entry(me) if size == 1 else add(entry(me), from_left, from_right)


ROLES = ((3, 1, 2, 0), (0, 2, 3, 1), (3, 1, 0, 2), (0, 2, 1, 3))


def body(
    partner,
    block_tenant_index,
    block_live_length,
    tenant_table_row,
    hidden,
    cotangent,
    frozen_value_weight,
    adapter_down_rows,
    adapter_up_matrix,
):
    blocks = block_tenant_index.shape[0]
    kept = blocks - SW
    devices = lax.axis_size("dp")
    me = lax.axis_index("dp")
    column = lax.axis_index("tensor")
    lengths = block_live_length
    line = devices == 4
    order = jnp.arange(devices, dtype=jnp.int32)
    holder = jnp.sum(jnp.where(partner == me, order, 0))

    cot_terms, up_own, down_own = kept_ranks(lengths, adapter_up_matrix, cotangent, adapter_down_rows)
    rank_cot = exchanged(cot_terms)
    up_choices, up_pick = shifted(up_own, holder)
    last_terms, up_last = last_ranks(lengths, up_pick, up_choices, cotangent, [rank_cot[1]])
    last_cot = spread(last_terms)
    down_choices, down_pick = shifted(down_own, holder)

    table_rows = jnp.sum(
        jnp.where(
            block_tenant_index[:, None] == jnp.arange(tenant_table_row.shape[0], dtype=jnp.int32)[None, :],
            tenant_table_row[None, :],
            0,
        ),
        axis=1,
    )
    weights = jnp.where(jnp.arange(blocks) < kept, 2 * (jnp.arange(blocks, dtype=jnp.int32) + 1), 1)

    def codes_of(owners):
        rows = (owners[:, None] * OWN + jnp.arange(OWN, dtype=jnp.int32)[None, :]).reshape(-1)
        return jnp.sum(jnp.where(rows[:, None] == table_rows[None, :], weights[None, :], 0), axis=1)

    columns = jnp.stack([column ^ 3, column ^ 2, column ^ 1, column]).astype(jnp.int32)

    def base(*tokens):
        return base_terms(columns, hidden, frozen_value_weight, tokens)

    def base_parts(terms, *tokens):
        sent, away, given, mine = terms
        away = add(after(away, *tokens), near(sent))
        return (mine, near(given), far(away)), away

    def last_in(token):
        terms, _ = last_ranks(lengths, down_pick, down_choices, hidden, [token])
        return spread(terms)

    def inputs(*tokens):
        return spread(streamed_ranks(lengths, adapter_down_rows, hidden, 4, tokens))

    def outputs(codes, parts, base_sums, rank_in, last):
        return outputs_of(
            lengths, codes, parts, base_sums, rank_in, last, cotangent, adapter_up_matrix, up_last
        )

    if line:
        inner = (me == 1) | (me == 2)
        codes = codes_of(jnp.array(ROLES, jnp.int32)[me])
        first, third, third_too = down_rows(codes, 0, 2, 2, rank_cot, last_cot, hidden)
        from_first = lax.ppermute(first, "dp", [(0, 1), (3, 2), (1, 0), (2, 3)])
        from_inner = lax.ppermute(third, "dp", [(1, 2), (2, 1)])
        last = last_in(first)
        second, own = down_rows(codes, 2 * OWN, 2, 1, rank_cot, last_cot, hidden, [last[0]], 100.0)
        terms = base(second)
        second = add(
            after(second, terms[0], from_inner), jnp.where(inner, from_first, jnp.zeros((), first.dtype))
        )
        from_second = lax.ppermute(second, "dp", [(0, 2), (3, 1), (1, 3), (2, 0)])
        from_third = lax.ppermute(after(third_too, from_first), "dp", [(0, 1), (3, 2)])
        near_total = lax.optimization_barrier(
            after(own, second).astype(jnp.float32) + jnp.where(inner, from_inner, from_first).astype(jnp.float32)
        )
        down_out = (near_total + from_second.astype(jnp.float32) + from_third.astype(jnp.float32)).astype(own.dtype)

        up_codes = codes_of((me + jnp.array([1, 2, 3, 0], jnp.int32)) % devices)
        parts, away = base_parts(terms, second)
        values, *sent, kept_here = outputs(up_codes, [OWN] * 4, parts, inputs(away), last)
        arrived = [shift(array, by + 1) for by, array in enumerate(sent)]
        value_pick = ((me - partner[me]) % devices).reshape(1)
        up_out, values = finish(value_pick, values, kept_here, arrived)
    else:
        codes = codes_of(order)
        (table,) = down_rows(codes, 0, devices, 0, rank_cot, last_cot, hidden)
        down_out = line_reduce_scatter(table.reshape(devices, OWN, *table.shape[1:]))
        parts, _ = base_parts(base(table))
        values, table = outputs(codes, [devices * OWN], parts, inputs(table), last_in(table))
        up_table, last_values = table[:-BLOCK], table[-BLOCK:]
        up_out = line_reduce_scatter(up_table.reshape(devices, OWN, -1, values.shape[1]))
        (last_values,), _ = shifted(last_values, partner[me])
        values = jnp.concatenate([values[: kept * BLOCK], last_values], axis=0)
    return (values, down_out, up_out.reshape(OWN, -1, values.shape[1]))


def solution(mesh):
    in_specs = (
        P("groups"),
        P(("groups", "dp")),
        P(("groups", "dp")),
        P("groups"),
        P(("groups", "dp"), "tensor"),
        P(("groups", "dp"), "tensor"),
        P("tensor", None),
        P(("groups", "dp"), None, "tensor"),
        P(("groups", "dp"), None, "tensor"),
    )
    out_specs = (
        P(("groups", "dp"), "tensor"),
        P(("groups", "dp"), None, "tensor"),
        P(("groups", "dp"), None, "tensor"),
    )
    return jax.shard_map(body, mesh=mesh, in_specs=in_specs, out_specs=out_specs, check_vma=False)
```

```python
import jax
import jax.numpy as jnp
from jax import lax
from jax.experimental import pallas as pl
from jax.experimental.pallas import tpu as pltpu
from jax.sharding import PartitionSpec as P

BLOCK = 128
SW = 1
OWN = 4


ADAPTER_SCALE = 0.5

ANYWHERE = pl.BlockSpec(memory_space=pl.ANY)
ROW_PRODUCT = (((1,), (1,)), ((), ()))


def call(kernel, scalars, grid, inputs, outputs, tokens=(), us=1.0, scratch=(), aliases=None):
    def run(*refs):
        cut = len(scalars) + len(inputs)
        return kernel(*refs[:cut], *refs[cut + len(tokens) :])

    return pl.pallas_call(
        run,
        grid_spec=pltpu.PrefetchScalarGridSpec(
            num_scalar_prefetch=len(scalars),
            grid=grid,
            in_specs=[spec for _, spec in inputs] + [ANYWHERE] * len(tokens),
            out_specs=[spec for _, _, spec in outputs],
            scratch_shapes=scratch,
        ),
        out_shape=[jax.ShapeDtypeStruct(shape, kind) for shape, kind, _ in outputs],
        input_output_aliases=aliases or {},
        cost_estimate=pl.CostEstimate(flops=int(us * 1e9), bytes_accessed=int(us * 3.6e5), transcendentals=0),
    )(*scalars, *[array for array, _ in inputs], *tokens)


def constant_spec(shape):
    return pl.BlockSpec(shape, lambda *_: (0,) * len(shape), pipeline_mode=pl.Buffered(1))


def whole(array):
    return (array, constant_spec(array.shape))


def nothing(*refs):
    pass


def after(array, *tokens):
    return call(
        nothing, (), (1,), [(array, ANYWHERE)], [(array.shape, array.dtype, ANYWHERE)], tokens, 0.1, aliases={0: 0}
    )[0]


def masked_rank(adapter, rows, length):
    ranks = lax.dot_general(adapter, rows, ROW_PRODUCT, preferred_element_type=jnp.float32)
    live = lax.broadcasted_iota(jnp.int32, ranks.shape, 1) < length
    return jnp.where(live, ranks, 0.0).astype(rows.dtype)


def kept_ranks(lengths, maps, features, others):
    blocks, rank, width = maps.shape
    kept = blocks - SW
    last_shapes = [(SW, rank, width), (SW, *others.shape[1:])]

    def kernel(lengths_ref, maps_ref, rows_ref, others_ref, out_ref, last_ref, last_other):
        last_ref[...] = maps_ref[kept:]
        last_other[...] = others_ref[...]
        for k in range(kept):
            out_ref[k] = masked_rank(maps_ref[k], rows_ref[k * BLOCK : (k + 1) * BLOCK], lengths_ref[k])

    return call(
        kernel,
        (lengths,),
        (1,),
        [
            whole(maps),
            whole(features),
            (others, pl.BlockSpec(last_shapes[1], lambda i, *_: (kept, 0, 0), pipeline_mode=pl.Buffered(1))),
        ],
        [((blocks, rank, BLOCK), features.dtype, pl.BlockSpec((kept, rank, BLOCK), lambda i, *_: (0, 0, 0)))]
        + [(shape, features.dtype, constant_spec(shape)) for shape in last_shapes],
    )


def with_last_rank(lengths, pick, choices, features, ranks):
    shape = choices[0].shape
    block = ranks.shape[0] - 1

    def kernel(lengths_ref, pick_ref, *refs):
        rows_ref, _, out_ref, chosen_ref = refs[-4:]
        for k, choice in enumerate(refs[:-4]):

            @pl.when(pick_ref[0] == k)
            def _():
                chosen_ref[...] = choice[...]

        out_ref[0] = masked_rank(chosen_ref[0], rows_ref[...], lengths_ref[block])

    return call(
        kernel,
        (lengths, pick),
        (1,),
        [whole(choice) for choice in choices]
        + [(features, pl.BlockSpec((BLOCK, shape[2]), lambda i, *_: (block, 0), pipeline_mode=pl.Buffered(1)))]
        + [(ranks, ANYWHERE)],
        [
            (ranks.shape, ranks.dtype, pl.BlockSpec((1, *ranks.shape[1:]), lambda i, *_: (block, 0, 0))),
            (shape, features.dtype, constant_spec(shape)),
        ],
        aliases={3 + len(choices): 0},
    )


def streamed_ranks(lengths, maps, pick, choices, features, each, tokens=(), us=1.0):
    blocks, rank, width = maps.shape
    steps = pl.cdiv(blocks, each)
    end = blocks - 1 - (steps - 1) * each

    def kernel(lengths_ref, pick_ref, *refs):
        maps_refs, rows_refs, choices_refs, out_ref = refs[:each], refs[each : 2 * each], refs[2 * each : -1], refs[-1]
        step = pl.program_id(0)

        def one(k):
            block = step * each + k
            out_ref[block] = masked_rank(maps_refs[k][0], rows_refs[k][...], lengths_ref[block])

        @pl.when(step < steps - 1)
        def _():
            for k in range(each):
                one(k)

        @pl.when(step == steps - 1)
        def _():
            for k in range(end):
                one(k)
            for j, choice in enumerate(choices_refs):

                @pl.when(pick_ref[0] == j)
                def _():
                    out_ref[blocks - 1] = masked_rank(choice[0], rows_refs[end][...], lengths_ref[blocks - 1])

    def at(i, k):
        block = i * each + k
        return jnp.where(block < blocks, block, block - each)

    return call(
        kernel,
        (lengths, pick),
        (steps,),
        [(maps, pl.BlockSpec((1, rank, width), lambda i, *_, k=k: (at(i, k), 0, 0))) for k in range(each)]
        + [(features, pl.BlockSpec((BLOCK, width), lambda i, *_, k=k: (at(i, k), 0))) for k in range(each)]
        + [whole(choice) for choice in choices],
        [((blocks, rank, BLOCK), features.dtype, constant_spec((blocks, rank, BLOCK)))],
        tokens,
        us,
    )[0]


def summed(terms, at):
    return sum(term[at].astype(jnp.float32) for term in terms).astype(terms[0].dtype)


def down_rows(codes, first, parts, copies, ranks, features, tokens=(), us=1.0):
    blocks, rank, _ = ranks[0].shape
    width = features.shape[1]
    piece = min(width, 512)

    def block_at(code):
        return jnp.maximum((code >> 1) - 1, 0)

    def kernel(codes_ref, a, b, *refs):
        rows_refs, last_ref, outs = refs[:OWN], refs[OWN], refs[OWN + 1 :]
        step = pl.program_id(0)

        def fill(to):
            for k in range(OWN):
                code = codes_ref[first + step * OWN + k]
                mine = summed((a, b), block_at(code))
                mine = jnp.where(code > 1, mine, jnp.zeros_like(mine))

                def put(at, total):
                    value = (ADAPTER_SCALE * total).astype(features.dtype)
                    for out_ref in to:
                        out_ref[k, :, at] = value

                for at in [slice(c, c + piece) for c in range(0, width, piece)]:
                    put(at, jnp.dot(mine, rows_refs[k][:, at], preferred_element_type=jnp.float32))

                @pl.when((code & 1) > 0)
                def _():
                    late = summed((a, b), blocks - 1)
                    for at in [slice(c, c + piece) for c in range(0, width, piece)]:
                        put(
                            at,
                            jnp.dot(mine, rows_refs[k][:, at], preferred_element_type=jnp.float32)
                            + jnp.dot(late, last_ref[:, at], preferred_element_type=jnp.float32),
                        )

        if not copies or parts == 1:
            fill(outs)
        else:
            for part in range(parts):

                @pl.when(step == part)
                def _():
                    fill(outs[part:] if part == parts - 1 else outs[part : part + 1])

    def rows_spec(k):
        return pl.BlockSpec((BLOCK, width), lambda r, at: (block_at(at[first + r * OWN + k]), 0))

    shape = (OWN, rank, width)
    if copies:
        outs = [(shape, features.dtype, constant_spec(shape))] * (parts - 1 + copies)
    else:
        outs = [((parts * OWN, rank, width), features.dtype, pl.BlockSpec(shape, lambda r, *_: (r, 0, 0)))]
    return call(
        kernel,
        (codes,),
        (parts,),
        [whole(array) for array in ranks]
        + [(features, rows_spec(k)) for k in range(OWN)]
        + [(features, pl.BlockSpec((BLOCK, width), lambda r, *_: (blocks - 1, 0), pipeline_mode=pl.Buffered(1)))],
        outs,
        tokens,
        us,
    )


def outputs_of(lengths, codes, parts, base, ranks, features, maps, last_map):
    rows, width = base[0].shape
    blocks = rows // BLOCK
    rank = maps.shape[1]

    def kernel(lengths_ref, codes_ref, one, two, three, *refs):
        terms, refs = refs[: len(ranks)], refs[len(ranks) :]
        rows_ref, maps_ref, last_ref, out_ref, *outs = refs
        late = summed(terms, blocks - 1)
        for k in range(blocks):
            at = slice(k * BLOCK, (k + 1) * BLOCK)
            adapter = maps_ref[k] if k < blocks - 1 else last_ref[0]
            added = lax.dot_general(
                summed(terms, k) if k < blocks - 1 else late,
                adapter,
                (((0,), (0,)), ((), ())),
                preferred_element_type=jnp.float32,
            )
            frozen = one[at].astype(jnp.float32) + two[at].astype(jnp.float32) + three[at].astype(jnp.float32)
            live = lax.broadcasted_iota(jnp.int32, frozen.shape, 0) < lengths_ref[k]
            values = jnp.where(live, frozen + ADAPTER_SCALE * added, 0.0).astype(out_ref.dtype)
            out_ref[at] = values
            if k == blocks - 1:
                for count, out in zip(parts, outs):
                    out[count * rank :] = values
        late_rows = jnp.dot(late, rows_ref[(blocks - 1) * BLOCK :], preferred_element_type=jnp.float32)
        done = 0
        for count, out in zip(parts, outs):

            def one_row(r, carry, out=out, done=done):
                code = codes_ref[done + r]
                at = jnp.maximum((code >> 1) - 1, 0)
                mine = summed(terms, at)
                mine = jnp.where(code > 1, mine, jnp.zeros_like(mine))
                mine_rows = rows_ref[pl.ds(pl.multiple_of(at * BLOCK, BLOCK), BLOCK), :]
                total = jnp.dot(mine, mine_rows, preferred_element_type=jnp.float32)
                total = total + jnp.where((code & 1) > 0, late_rows, 0.0)
                to = r * rank if isinstance(r, int) else pl.ds(pl.multiple_of(r * rank, rank), rank)
                to = slice(to, to + rank) if isinstance(r, int) else to
                out[to] = (ADAPTER_SCALE * total).astype(out.dtype)
                return carry

            if count <= OWN:
                for r in range(count):
                    one_row(r, 0)
            else:
                lax.fori_loop(0, count, one_row, 0)
            done += count

    return call(
        kernel,
        (lengths, codes),
        (1,),
        [whole(array) for array in (*base, *ranks, features, maps, last_map)],
        [((rows, width), maps.dtype, constant_spec((rows, width)))]
        + [
            ((count * rank + BLOCK, width), maps.dtype, constant_spec((count * rank + BLOCK, width)))
            for count in parts
        ],
    )


def finish(pick, values, own, arrived, tokens):
    width = values.shape[1]
    block = values.shape[0] // BLOCK - 1
    rows = own.shape[0] - BLOCK

    def kernel(pick_ref, *refs):
        choices, table_ref, last_ref = refs[:-3], refs[-2], refs[-1]
        table_ref[...] = sum(choice[:rows].astype(jnp.float32) for choice in choices).astype(own.dtype)
        for k, choice in enumerate(choices):

            @pl.when(pick_ref[0] == k)
            def _():
                last_ref[...] = choice[rows:]

    return call(
        kernel,
        (pick,),
        (1,),
        [whole(choice) for choice in (own, *arrived)] + [(values, ANYWHERE)],
        [
            ((rows, width), own.dtype, constant_spec((rows, width))),
            (values.shape, values.dtype, pl.BlockSpec((BLOCK, width), lambda i, *_: (block, 0))),
        ],
        tokens,
        aliases={2 + len(arrived): 1},
    )


def base_terms(columns, hidden, weight, tokens=()):
    rows, depth = hidden.shape
    width = weight.shape[1] // 4
    tile = rows // 4

    def kernel(columns_ref, rows_ref, *refs):
        for k in range(4):
            out_ref = refs[4 + k]
            out_ref[...] = jnp.dot(rows_ref[...], refs[k][...], preferred_element_type=jnp.float32).astype(out_ref.dtype)

    def column(k):
        return pl.BlockSpec((depth, width), lambda i, at: (0, at[k]), pipeline_mode=pl.Buffered(1))

    return call(
        kernel,
        (columns,),
        (rows // tile,),
        [(hidden, pl.BlockSpec((tile, depth), lambda i, *_: (i, 0)))]
        + [(weight, column(k)) for k in range(4)],
        [((rows, width), hidden.dtype, pl.BlockSpec((tile, width), lambda i, *_: (i, 0)))] * 4,
        tokens,
        100.0,
    )


def shift(array, by):
    size = lax.axis_size("dp")
    return lax.ppermute(array, "dp", [(i, (i + by) % size) for i in range(size)])


def shifted(array, source):
    size = lax.axis_size("dp")
    me = lax.axis_index("dp")
    if size > 4:
        taken = lax.dynamic_index_in_dim(lax.all_gather(array, "dp"), source, 0, keepdims=False)
        return [taken], jnp.zeros((1,), jnp.int32)
    choices = [array] + [shift(array, by) for by in range(1, size)]
    return choices, ((me - source) % size).reshape(1)


def add(*arrays):
    return sum(array.astype(jnp.float32) for array in arrays).astype(arrays[0].dtype)


def crossed(array, by):
    return lax.ppermute(array, "tensor", [(i, i ^ by) for i in range(lax.axis_size("tensor"))])


def near(array):
    return crossed(array, 1)


def far(array):
    return crossed(array, 2)


def exchanged(array):
    array = add(array, near(array))
    return array, far(array)


def spread(array):
    return [array] + [crossed(array, by) for by in range(1, lax.axis_size("tensor"))]


def line_reduce_scatter(table):
    size = lax.axis_size("dp")
    me = lax.axis_index("dp")

    def entry(index):
        return lax.dynamic_index_in_dim(table, jnp.clip(index, 0, size - 1), 0, keepdims=False)

    from_left = from_right = None
    for step in range(size - 1):
        right = entry(size - 1 - step + me)
        left = entry(step - (size - 1 - me))
        if step > 0:
            right = add(right, from_left)
            left = add(left, from_right)
        from_left = lax.ppermute(right, "dp", [(i, i + 1) for i in range(step + 1)])
        from_right = lax.ppermute(left, "dp", [(i, i - 1) for i in range(size - 1 - step, size)])
    return entry(me) if size == 1 else add(entry(me), from_left, from_right)


ROLES = ((3, 1, 2, 0), (0, 2, 3, 1), (3, 1, 0, 2), (0, 2, 1, 3))


def body(
    partner,
    block_tenant_index,
    block_live_length,
    tenant_table_row,
    hidden,
    cotangent,
    frozen_value_weight,
    adapter_down_rows,
    adapter_up_matrix,
):
    blocks = block_tenant_index.shape[0]
    kept = blocks - SW
    devices = lax.axis_size("dp")
    me = lax.axis_index("dp")
    column = lax.axis_index("tensor")
    lengths = block_live_length
    line = devices == 4
    order = jnp.arange(devices, dtype=jnp.int32)
    holder = jnp.sum(jnp.where(partner == me, order, 0))

    cot_terms, up_own, down_own = kept_ranks(lengths, adapter_up_matrix, cotangent, adapter_down_rows)
    up_choices, up_pick = shifted(up_own, holder)
    down_choices, down_pick = shifted(down_own, holder)
    cot_terms, up_last = with_last_rank(lengths, up_pick, up_choices, cotangent, cot_terms)
    rank_cot = exchanged(cot_terms)

    table_rows = jnp.sum(
        jnp.where(
            block_tenant_index[:, None] == jnp.arange(tenant_table_row.shape[0], dtype=jnp.int32)[None, :],
            tenant_table_row[None, :],
            0,
        ),
        axis=1,
    )
    weights = jnp.where(jnp.arange(blocks) < kept, 2 * (jnp.arange(blocks, dtype=jnp.int32) + 1), 1)

    def codes_of(owners):
        rows = (owners[:, None] * OWN + jnp.arange(OWN, dtype=jnp.int32)[None, :]).reshape(-1)
        return jnp.sum(jnp.where(rows[:, None] == table_rows[None, :], weights[None, :], 0), axis=1)

    columns = jnp.stack([column ^ 3, column ^ 2, column ^ 1, column]).astype(jnp.int32)

    def base(*tokens):
        sent, away, given, mine = base_terms(columns, hidden, frozen_value_weight, tokens)
        away = add(away, near(sent))
        return (mine, near(given), far(away)), away

    def inputs(*tokens):
        return spread(
            streamed_ranks(lengths, adapter_down_rows, down_pick, down_choices, hidden, 4, tokens, 100.0)
        )

    def outputs(codes, parts, base_sums, rank_in):
        return outputs_of(
            lengths, codes, parts, base_sums, rank_in, cotangent, adapter_up_matrix, up_last
        )

    if line:
        inner = (me == 1) | (me == 2)
        codes = codes_of(jnp.array(ROLES, jnp.int32)[me])
        first, third, third_too = down_rows(codes, 0, 2, 2, rank_cot, hidden)
        from_first = lax.ppermute(first, "dp", [(0, 1), (3, 2), (1, 0), (2, 3)])
        from_inner = lax.ppermute(third, "dp", [(1, 2), (2, 1)])
        base_sums, away = base(first, *down_choices[1:])
        second, own = down_rows(codes, 2 * OWN, 2, 1, rank_cot, hidden, [base_sums[0]], 100.0)
        second = add(after(second, away, from_inner), jnp.where(inner, from_first, jnp.zeros((), first.dtype)))
        from_second = lax.ppermute(second, "dp", [(0, 2), (3, 1), (1, 3), (2, 0)])
        from_third = lax.ppermute(after(third_too, from_first), "dp", [(0, 1), (3, 2)])
        near_total = lax.optimization_barrier(
            after(own, second).astype(jnp.float32) + jnp.where(inner, from_inner, from_first).astype(jnp.float32)
        )
        down_out = (near_total + from_second.astype(jnp.float32) + from_third.astype(jnp.float32)).astype(own.dtype)

        up_codes = codes_of((me + jnp.array([1, 2, 3, 0], jnp.int32)) % devices)
        values, *sent, kept_here = outputs(up_codes, [OWN] * 4, base_sums, inputs(second))
        arrived = [shift(array, by + 1) for by, array in enumerate(sent)]
        value_pick = ((me - partner[me]) % devices).reshape(1)
        up_out, values = finish(value_pick, values, kept_here, arrived, [down_out])
    else:
        codes = codes_of(order)
        (table,) = down_rows(codes, 0, devices, 0, rank_cot, hidden)
        down_out = line_reduce_scatter(table.reshape(devices, OWN, *table.shape[1:]))
        values, table = outputs(codes, [devices * OWN], base(table)[0], inputs(table))
        up_table, last_values = table[:-BLOCK], table[-BLOCK:]
        up_out = line_reduce_scatter(up_table.reshape(devices, OWN, -1, values.shape[1]))
        (last_values,), _ = shifted(last_values, partner[me])
        values = jnp.concatenate([values[: kept * BLOCK], last_values], axis=0)
    return (values, down_out, up_out.reshape(OWN, -1, values.shape[1]))


def solution(mesh):
    in_specs = (
        P("groups"),
        P(("groups", "dp")),
        P(("groups", "dp")),
        P("groups"),
        P(("groups", "dp"), "tensor"),
        P(("groups", "dp"), "tensor"),
        P("tensor", None),
        P(("groups", "dp"), None, "tensor"),
        P(("groups", "dp"), None, "tensor"),
    )
    out_specs = (
        P(("groups", "dp"), "tensor"),
        P(("groups", "dp"), None, "tensor"),
        P(("groups", "dp"), None, "tensor"),
    )
    return jax.shard_map(body, mesh=mesh, in_specs=in_specs, out_specs=out_specs, check_vma=False)
```

```python
import jax
import jax.numpy as jnp
from jax import lax
from jax.experimental import pallas as pl
from jax.experimental.pallas import tpu as pltpu
from jax.sharding import PartitionSpec as P

BLOCK = 128
SW = 1
OWN = 4


ADAPTER_SCALE = 0.5

ANYWHERE = pl.BlockSpec(memory_space=pl.ANY)
ROW_PRODUCT = (((1,), (1,)), ((), ()))


def call(kernel, scalars, grid, inputs, outputs, tokens=(), us=1.0, scratch=(), aliases=None):
    def run(*refs):
        cut = len(scalars) + len(inputs)
        return kernel(*refs[:cut], *refs[cut + len(tokens) :])

    return pl.pallas_call(
        run,
        grid_spec=pltpu.PrefetchScalarGridSpec(
            num_scalar_prefetch=len(scalars),
            grid=grid,
            in_specs=[spec for _, spec in inputs] + [ANYWHERE] * len(tokens),
            out_specs=[spec for _, _, spec in outputs],
            scratch_shapes=scratch,
        ),
        out_shape=[jax.ShapeDtypeStruct(shape, kind) for shape, kind, _ in outputs],
        input_output_aliases=aliases or {},
        cost_estimate=pl.CostEstimate(flops=int(us * 1e9), bytes_accessed=int(us * 3.6e5), transcendentals=0),
    )(*scalars, *[array for array, _ in inputs], *tokens)


def constant_spec(shape):
    return pl.BlockSpec(shape, lambda *_: (0,) * len(shape), pipeline_mode=pl.Buffered(1))


def whole(array):
    return (array, constant_spec(array.shape))


def nothing(*refs):
    pass


def after(array, *tokens):
    return call(
        nothing, (), (1,), [(array, ANYWHERE)], [(array.shape, array.dtype, ANYWHERE)], tokens, 0.1, aliases={0: 0}
    )[0]


def masked_rank(adapter, rows, length):
    ranks = lax.dot_general(adapter, rows, ROW_PRODUCT, preferred_element_type=jnp.float32)
    live = lax.broadcasted_iota(jnp.int32, ranks.shape, 1) < length
    return jnp.where(live, ranks, 0.0).astype(rows.dtype)


def kept_ranks(lengths, maps, features, others, tokens=()):
    blocks, rank, width = maps.shape
    kept = blocks - SW
    last_shape = (SW, *others.shape[1:])

    def kernel(lengths_ref, maps_ref, rows_ref, others_ref, out_ref, last_other):
        last_other[...] = others_ref[...]
        for k in range(kept):
            out_ref[k] = masked_rank(maps_ref[k], rows_ref[k * BLOCK : (k + 1) * BLOCK], lengths_ref[k])

    return call(
        kernel,
        (lengths,),
        (1,),
        [
            (maps, pl.BlockSpec((kept, rank, width), lambda i, *_: (0, 0, 0), pipeline_mode=pl.Buffered(1))),
            (features, pl.BlockSpec((kept * BLOCK, width), lambda i, *_: (0, 0), pipeline_mode=pl.Buffered(1))),
            (others, pl.BlockSpec(last_shape, lambda i, *_: (kept, 0, 0), pipeline_mode=pl.Buffered(1))),
        ],
        [
            ((blocks, rank, BLOCK), features.dtype, pl.BlockSpec((kept, rank, BLOCK), lambda i, *_: (0, 0, 0))),
            (last_shape, features.dtype, constant_spec(last_shape)),
        ],
        tokens,
    )


def with_last_rank(lengths, pick, choices, features, ranks):
    shape = choices[0].shape
    block = ranks.shape[0] - 1

    def kernel(lengths_ref, pick_ref, *refs):
        rows_ref, _, out_ref, chosen_ref = refs[-4:]
        for k, choice in enumerate(refs[:-4]):

            @pl.when(pick_ref[0] == k)
            def _():
                chosen_ref[...] = choice[...]

        out_ref[0] = masked_rank(chosen_ref[0], rows_ref[...], lengths_ref[block])

    return call(
        kernel,
        (lengths, pick),
        (1,),
        [whole(choice) for choice in choices]
        + [(features, pl.BlockSpec((BLOCK, shape[2]), lambda i, *_: (block, 0), pipeline_mode=pl.Buffered(1)))]
        + [(ranks, ANYWHERE)],
        [
            (ranks.shape, ranks.dtype, pl.BlockSpec((1, *ranks.shape[1:]), lambda i, *_: (block, 0, 0))),
            (shape, features.dtype, constant_spec(shape)),
        ],
        aliases={3 + len(choices): 0},
    )


def streamed_ranks(lengths, maps, pick, choices, features, each, tokens=(), us=1.0):
    blocks, rank, width = maps.shape
    steps = pl.cdiv(blocks, each)
    end = blocks - 1 - (steps - 1) * each

    def kernel(lengths_ref, pick_ref, *refs):
        maps_refs, rows_refs, choices_refs, out_ref = refs[:each], refs[each : 2 * each], refs[2 * each : -1], refs[-1]
        step = pl.program_id(0)

        def one(k):
            block = step * each + k
            out_ref[block] = masked_rank(maps_refs[k][0], rows_refs[k][...], lengths_ref[block])

        @pl.when(step < steps - 1)
        def _():
            for k in range(each):
                one(k)

        @pl.when(step == steps - 1)
        def _():
            for k in range(end):
                one(k)
            for j, choice in enumerate(choices_refs):

                @pl.when(pick_ref[0] == j)
                def _():
                    out_ref[blocks - 1] = masked_rank(choice[0], rows_refs[end][...], lengths_ref[blocks - 1])

    def at(i, k):
        block = i * each + k
        return jnp.where(block < blocks, block, block - each)

    return call(
        kernel,
        (lengths, pick),
        (steps,),
        [(maps, pl.BlockSpec((1, rank, width), lambda i, *_, k=k: (at(i, k), 0, 0))) for k in range(each)]
        + [(features, pl.BlockSpec((BLOCK, width), lambda i, *_, k=k: (at(i, k), 0))) for k in range(each)]
        + [whole(choice) for choice in choices],
        [((blocks, rank, BLOCK), features.dtype, constant_spec((blocks, rank, BLOCK)))],
        tokens,
        us,
    )[0]


def summed(terms, at):
    return sum(term[at].astype(jnp.float32) for term in terms).astype(terms[0].dtype)


def down_rows(codes, first, parts, copies, ranks, features, tokens=(), us=1.0):
    blocks, rank, _ = ranks[0].shape
    width = features.shape[1]
    piece = min(width, 512)

    def block_at(code):
        return jnp.maximum((code >> 1) - 1, 0)

    def kernel(codes_ref, a, b, *refs):
        rows_refs, last_ref, outs = refs[:OWN], refs[OWN], refs[OWN + 1 :]
        step = pl.program_id(0)

        def fill(to):
            for k in range(OWN):
                code = codes_ref[first + step * OWN + k]
                mine = summed((a, b), block_at(code))
                mine = jnp.where(code > 1, mine, jnp.zeros_like(mine))

                def put(at, total):
                    value = (ADAPTER_SCALE * total).astype(features.dtype)
                    for out_ref in to:
                        out_ref[k, :, at] = value

                for at in [slice(c, c + piece) for c in range(0, width, piece)]:
                    put(at, jnp.dot(mine, rows_refs[k][:, at], preferred_element_type=jnp.float32))

                @pl.when((code & 1) > 0)
                def _():
                    late = summed((a, b), blocks - 1)
                    for at in [slice(c, c + piece) for c in range(0, width, piece)]:
                        put(
                            at,
                            jnp.dot(mine, rows_refs[k][:, at], preferred_element_type=jnp.float32)
                            + jnp.dot(late, last_ref[:, at], preferred_element_type=jnp.float32),
                        )

        if not copies or parts == 1:
            fill(outs)
        else:
            for part in range(parts):

                @pl.when(step == part)
                def _():
                    fill(outs[part:] if part == parts - 1 else outs[part : part + 1])

    def rows_spec(k):
        return pl.BlockSpec((BLOCK, width), lambda r, at: (block_at(at[first + r * OWN + k]), 0))

    shape = (OWN, rank, width)
    if copies:
        outs = [(shape, features.dtype, constant_spec(shape))] * (parts - 1 + copies)
    else:
        outs = [((parts * OWN, rank, width), features.dtype, pl.BlockSpec(shape, lambda r, *_: (r, 0, 0)))]
    return call(
        kernel,
        (codes,),
        (parts,),
        [whole(array) for array in ranks]
        + [(features, rows_spec(k)) for k in range(OWN)]
        + [(features, pl.BlockSpec((BLOCK, width), lambda r, *_: (blocks - 1, 0), pipeline_mode=pl.Buffered(1)))],
        outs,
        tokens,
        us,
    )


def outputs_of(lengths, codes, parts, base, ranks, features, maps, last_map):
    rows, width = base[0].shape
    blocks = rows // BLOCK
    rank = maps.shape[1]

    def kernel(lengths_ref, codes_ref, one, two, three, *refs):
        terms, refs = refs[: len(ranks)], refs[len(ranks) :]
        rows_ref, maps_ref, last_ref, out_ref, *outs = refs
        late = summed(terms, blocks - 1)
        for k in range(blocks):
            at = slice(k * BLOCK, (k + 1) * BLOCK)
            adapter = maps_ref[k] if k < blocks - 1 else last_ref[0]
            added = lax.dot_general(
                summed(terms, k) if k < blocks - 1 else late,
                adapter,
                (((0,), (0,)), ((), ())),
                preferred_element_type=jnp.float32,
            )
            frozen = one[at].astype(jnp.float32) + two[at].astype(jnp.float32) + three[at].astype(jnp.float32)
            live = lax.broadcasted_iota(jnp.int32, frozen.shape, 0) < lengths_ref[k]
            values = jnp.where(live, frozen + ADAPTER_SCALE * added, 0.0).astype(out_ref.dtype)
            out_ref[at] = values
            if k == blocks - 1:
                for count, out in zip(parts, outs):
                    out[count * rank :] = values
        late_rows = jnp.dot(late, rows_ref[(blocks - 1) * BLOCK :], preferred_element_type=jnp.float32)
        done = 0
        for count, out in zip(parts, outs):

            def one_row(r, carry, out=out, done=done):
                code = codes_ref[done + r]
                at = jnp.maximum((code >> 1) - 1, 0)
                mine = summed(terms, at)
                mine = jnp.where(code > 1, mine, jnp.zeros_like(mine))
                mine_rows = rows_ref[pl.ds(pl.multiple_of(at * BLOCK, BLOCK), BLOCK), :]
                total = jnp.dot(mine, mine_rows, preferred_element_type=jnp.float32)
                total = total + jnp.where((code & 1) > 0, late_rows, 0.0)
                to = r * rank if isinstance(r, int) else pl.ds(pl.multiple_of(r * rank, rank), rank)
                to = slice(to, to + rank) if isinstance(r, int) else to
                out[to] = (ADAPTER_SCALE * total).astype(out.dtype)
                return carry

            if count <= OWN:
                for r in range(count):
                    one_row(r, 0)
            else:
                lax.fori_loop(0, count, one_row, 0)
            done += count

    return call(
        kernel,
        (lengths, codes),
        (1,),
        [whole(array) for array in (*base, *ranks, features, maps, last_map)],
        [((rows, width), maps.dtype, constant_spec((rows, width)))]
        + [
            ((count * rank + BLOCK, width), maps.dtype, constant_spec((count * rank + BLOCK, width)))
            for count in parts
        ],
    )


def finish(pick, values, own, arrived, tokens):
    width = values.shape[1]
    block = values.shape[0] // BLOCK - 1
    rows = own.shape[0] - BLOCK

    def kernel(pick_ref, *refs):
        choices, table_ref, last_ref = refs[:-3], refs[-2], refs[-1]
        table_ref[...] = sum(choice[:rows].astype(jnp.float32) for choice in choices).astype(own.dtype)
        for k, choice in enumerate(choices):

            @pl.when(pick_ref[0] == k)
            def _():
                last_ref[...] = choice[rows:]

    return call(
        kernel,
        (pick,),
        (1,),
        [whole(choice) for choice in (own, *arrived)] + [(values, ANYWHERE)],
        [
            ((rows, width), own.dtype, constant_spec((rows, width))),
            (values.shape, values.dtype, pl.BlockSpec((BLOCK, width), lambda i, *_: (block, 0))),
        ],
        tokens,
        aliases={2 + len(arrived): 1},
    )


def base_terms(columns, hidden, weight, tokens=()):
    rows, depth = hidden.shape
    width = weight.shape[1] // 4
    tile = rows // 4

    def kernel(columns_ref, rows_ref, *refs):
        for k in range(4):
            out_ref = refs[4 + k]
            out_ref[...] = jnp.dot(rows_ref[...], refs[k][...], preferred_element_type=jnp.float32).astype(out_ref.dtype)

    def column(k):
        return pl.BlockSpec((depth, width), lambda i, at: (0, at[k]), pipeline_mode=pl.Buffered(1))

    return call(
        kernel,
        (columns,),
        (rows // tile,),
        [(hidden, pl.BlockSpec((tile, depth), lambda i, *_: (i, 0)))]
        + [(weight, column(k)) for k in range(4)],
        [((rows, width), hidden.dtype, pl.BlockSpec((tile, width), lambda i, *_: (i, 0)))] * 4,
        tokens,
        100.0,
    )


def shift(array, by):
    size = lax.axis_size("dp")
    return lax.ppermute(array, "dp", [(i, (i + by) % size) for i in range(size)])


def shifted(array, source):
    size = lax.axis_size("dp")
    me = lax.axis_index("dp")
    if size > 4:
        taken = lax.dynamic_index_in_dim(lax.all_gather(array, "dp"), source, 0, keepdims=False)
        return [taken], jnp.zeros((1,), jnp.int32)
    choices = [array] + [shift(array, by) for by in range(1, size)]
    return choices, ((me - source) % size).reshape(1)


def add(*arrays):
    return sum(array.astype(jnp.float32) for array in arrays).astype(arrays[0].dtype)


def crossed(array, by):
    return lax.ppermute(array, "tensor", [(i, i ^ by) for i in range(lax.axis_size("tensor"))])


def near(array):
    return crossed(array, 1)


def far(array):
    return crossed(array, 2)


def exchanged(array):
    array = add(array, near(array))
    return array, far(array)


def spread(array):
    return [array] + [crossed(array, by) for by in range(1, lax.axis_size("tensor"))]


def line_reduce_scatter(table):
    size = lax.axis_size("dp")
    me = lax.axis_index("dp")

    def entry(index):
        return lax.dynamic_index_in_dim(table, jnp.clip(index, 0, size - 1), 0, keepdims=False)

    from_left = from_right = None
    for step in range(size - 1):
        right = entry(size - 1 - step + me)
        left = entry(step - (size - 1 - me))
        if step > 0:
            right = add(right, from_left)
            left = add(left, from_right)
        from_left = lax.ppermute(right, "dp", [(i, i + 1) for i in range(step + 1)])
        from_right = lax.ppermute(left, "dp", [(i, i - 1) for i in range(size - 1 - step, size)])
    return entry(me) if size == 1 else add(entry(me), from_left, from_right)


ROLES = ((3, 1, 2, 0), (0, 2, 3, 1), (3, 1, 0, 2), (0, 2, 1, 3))


def body(
    partner,
    block_tenant_index,
    block_live_length,
    tenant_table_row,
    hidden,
    cotangent,
    frozen_value_weight,
    adapter_down_rows,
    adapter_up_matrix,
):
    blocks = block_tenant_index.shape[0]
    kept = blocks - SW
    devices = lax.axis_size("dp")
    me = lax.axis_index("dp")
    column = lax.axis_index("tensor")
    lengths = block_live_length
    line = devices == 4
    order = jnp.arange(devices, dtype=jnp.int32)
    holder = jnp.sum(jnp.where(partner == me, order, 0))

    up_own = adapter_up_matrix[kept:]
    up_choices, up_pick = shifted(up_own, holder)
    cot_terms, down_own = kept_ranks(lengths, adapter_up_matrix, cotangent, adapter_down_rows, [up_own])
    cot_terms, up_last = with_last_rank(lengths, up_pick, up_choices, cotangent, cot_terms)
    rank_cot = exchanged(cot_terms)
    down_choices, down_pick = shifted(after(down_own, rank_cot[0]), holder)

    table_rows = jnp.sum(
        jnp.where(
            block_tenant_index[:, None] == jnp.arange(tenant_table_row.shape[0], dtype=jnp.int32)[None, :],
            tenant_table_row[None, :],
            0,
        ),
        axis=1,
    )
    weights = jnp.where(jnp.arange(blocks) < kept, 2 * (jnp.arange(blocks, dtype=jnp.int32) + 1), 1)

    def codes_of(owners):
        rows = (owners[:, None] * OWN + jnp.arange(OWN, dtype=jnp.int32)[None, :]).reshape(-1)
        return jnp.sum(jnp.where(rows[:, None] == table_rows[None, :], weights[None, :], 0), axis=1)

    columns = jnp.stack([column ^ 3, column ^ 2, column ^ 1, column]).astype(jnp.int32)

    def base(*tokens):
        return base_terms(columns, hidden, frozen_value_weight, tokens)

    def base_parts(terms, *tokens):
        sent, away, given, mine = terms
        return mine, near(given), far(add(after(away, *tokens), near(sent)))

    def inputs(*tokens):
        return spread(
            streamed_ranks(lengths, adapter_down_rows, down_pick, down_choices, hidden, 4, tokens, 100.0)
        )

    def outputs(codes, parts, base_sums, rank_in):
        return outputs_of(
            lengths, codes, parts, base_sums, rank_in, cotangent, adapter_up_matrix, up_last
        )

    if line:
        inner = (me == 1) | (me == 2)
        codes = codes_of(jnp.array(ROLES, jnp.int32)[me])
        first, third, third_too = down_rows(codes, 0, 2, 2, rank_cot, hidden)
        from_first = lax.ppermute(first, "dp", [(0, 1), (3, 2), (1, 0), (2, 3)])
        from_inner = lax.ppermute(third, "dp", [(1, 2), (2, 1)])
        second, own = down_rows(codes, 2 * OWN, 2, 1, rank_cot, hidden, [first], 1.0)
        terms = base(second, *down_choices[1:])
        second = add(after(second, terms[0], from_inner), jnp.where(inner, from_first, jnp.zeros((), first.dtype)))
        base_sums = base_parts(terms, second)
        from_second = lax.ppermute(second, "dp", [(0, 2), (3, 1), (1, 3), (2, 0)])
        from_third = lax.ppermute(after(third_too, second), "dp", [(0, 1), (3, 2)])
        near_total = lax.optimization_barrier(
            after(own, second).astype(jnp.float32) + jnp.where(inner, from_inner, from_first).astype(jnp.float32)
        )
        down_out = (near_total + from_second.astype(jnp.float32) + from_third.astype(jnp.float32)).astype(own.dtype)

        up_codes = codes_of((me + jnp.array([1, 2, 3, 0], jnp.int32)) % devices)
        values, *sent, kept_here = outputs(up_codes, [OWN] * 4, base_sums, inputs(second))
        arrived = [shift(array, by + 1) for by, array in enumerate(sent)]
        value_pick = ((me - partner[me]) % devices).reshape(1)
        up_out, values = finish(value_pick, values, kept_here, arrived, [down_out])
    else:
        codes = codes_of(order)
        (table,) = down_rows(codes, 0, devices, 0, rank_cot, hidden)
        down_out = line_reduce_scatter(table.reshape(devices, OWN, *table.shape[1:]))
        values, table = outputs(codes, [devices * OWN], base_parts(base(table)), inputs(table))
        up_table, last_values = table[:-BLOCK], table[-BLOCK:]
        up_out = line_reduce_scatter(up_table.reshape(devices, OWN, -1, values.shape[1]))
        (last_values,), _ = shifted(last_values, partner[me])
        values = jnp.concatenate([values[: kept * BLOCK], last_values], axis=0)
    return (values, down_out, up_out.reshape(OWN, -1, values.shape[1]))


def solution(mesh):
    in_specs = (
        P("groups"),
        P(("groups", "dp")),
        P(("groups", "dp")),
        P("groups"),
        P(("groups", "dp"), "tensor"),
        P(("groups", "dp"), "tensor"),
        P("tensor", None),
        P(("groups", "dp"), None, "tensor"),
        P(("groups", "dp"), None, "tensor"),
    )
    out_specs = (
        P(("groups", "dp"), "tensor"),
        P(("groups", "dp"), None, "tensor"),
        P(("groups", "dp"), None, "tensor"),
    )
    return jax.shard_map(body, mesh=mesh, in_specs=in_specs, out_specs=out_specs, check_vma=False)
```

```python
import jax
import jax.numpy as jnp
from jax import lax
from jax.experimental import pallas as pl
from jax.experimental.pallas import tpu as pltpu
from jax.sharding import PartitionSpec as P

BLOCK = 128
SW = 1
OWN = 4


ADAPTER_SCALE = 0.5

ANYWHERE = pl.BlockSpec(memory_space=pl.ANY)
ROW_PRODUCT = (((1,), (1,)), ((), ()))


def call(kernel, scalars, grid, inputs, outputs, tokens=(), us=1.0, scratch=(), aliases=None):
    def run(*refs):
        cut = len(scalars) + len(inputs)
        return kernel(*refs[:cut], *refs[cut + len(tokens) :])

    return pl.pallas_call(
        run,
        grid_spec=pltpu.PrefetchScalarGridSpec(
            num_scalar_prefetch=len(scalars),
            grid=grid,
            in_specs=[spec for _, spec in inputs] + [ANYWHERE] * len(tokens),
            out_specs=[spec for _, _, spec in outputs],
            scratch_shapes=scratch,
        ),
        out_shape=[jax.ShapeDtypeStruct(shape, kind) for shape, kind, _ in outputs],
        input_output_aliases=aliases or {},
        cost_estimate=pl.CostEstimate(flops=int(us * 1e9), bytes_accessed=int(us * 3.6e5), transcendentals=0),
    )(*scalars, *[array for array, _ in inputs], *tokens)


def constant_spec(shape):
    return pl.BlockSpec(shape, lambda *_: (0,) * len(shape), pipeline_mode=pl.Buffered(1))


def whole(array):
    return (array, constant_spec(array.shape))


def nothing(*refs):
    pass


def after(array, *tokens):
    return call(
        nothing, (), (1,), [(array, ANYWHERE)], [(array.shape, array.dtype, ANYWHERE)], tokens, 0.1, aliases={0: 0}
    )[0]


def masked_rank(adapter, rows, length):
    ranks = lax.dot_general(adapter, rows, ROW_PRODUCT, preferred_element_type=jnp.float32)
    live = lax.broadcasted_iota(jnp.int32, ranks.shape, 1) < length
    return jnp.where(live, ranks, 0.0).astype(rows.dtype)


def kept_ranks(lengths, maps, features, others, tokens=()):
    blocks, rank, width = maps.shape
    kept = blocks - SW
    last_shape = (SW, *others.shape[1:])

    def kernel(lengths_ref, maps_ref, rows_ref, others_ref, out_ref, last_other):
        last_other[...] = others_ref[...]
        for k in range(kept):
            out_ref[k] = masked_rank(maps_ref[k], rows_ref[k * BLOCK : (k + 1) * BLOCK], lengths_ref[k])

    return call(
        kernel,
        (lengths,),
        (1,),
        [
            (maps, pl.BlockSpec((kept, rank, width), lambda i, *_: (0, 0, 0), pipeline_mode=pl.Buffered(1))),
            (features, pl.BlockSpec((kept * BLOCK, width), lambda i, *_: (0, 0), pipeline_mode=pl.Buffered(1))),
            (others, pl.BlockSpec(last_shape, lambda i, *_: (kept, 0, 0), pipeline_mode=pl.Buffered(1))),
        ],
        [
            ((blocks, rank, BLOCK), features.dtype, pl.BlockSpec((kept, rank, BLOCK), lambda i, *_: (0, 0, 0))),
            (last_shape, features.dtype, constant_spec(last_shape)),
        ],
        tokens,
    )


def with_last_rank(lengths, pick, choices, features, ranks):
    shape = choices[0].shape
    block = ranks.shape[0] - 1

    def kernel(lengths_ref, pick_ref, *refs):
        rows_ref, _, out_ref, chosen_ref = refs[-4:]
        for k, choice in enumerate(refs[:-4]):

            @pl.when(pick_ref[0] == k)
            def _():
                chosen_ref[...] = choice[...]

        out_ref[0] = masked_rank(chosen_ref[0], rows_ref[...], lengths_ref[block])

    return call(
        kernel,
        (lengths, pick),
        (1,),
        [whole(choice) for choice in choices]
        + [(features, pl.BlockSpec((BLOCK, shape[2]), lambda i, *_: (block, 0), pipeline_mode=pl.Buffered(1)))]
        + [(ranks, ANYWHERE)],
        [
            (ranks.shape, ranks.dtype, pl.BlockSpec((1, *ranks.shape[1:]), lambda i, *_: (block, 0, 0))),
            (shape, features.dtype, constant_spec(shape)),
        ],
        aliases={3 + len(choices): 0},
    )


def streamed_ranks(lengths, maps, pick, choices, features, each, tokens=(), us=1.0):
    blocks, rank, width = maps.shape
    steps = pl.cdiv(blocks, each)
    end = blocks - 1 - (steps - 1) * each

    def kernel(lengths_ref, pick_ref, *refs):
        maps_refs, rows_refs, choices_refs, out_ref = refs[:each], refs[each : 2 * each], refs[2 * each : -1], refs[-1]
        step = pl.program_id(0)

        def one(k):
            block = step * each + k
            out_ref[block] = masked_rank(maps_refs[k][0], rows_refs[k][...], lengths_ref[block])

        @pl.when(step < steps - 1)
        def _():
            for k in range(each):
                one(k)

        @pl.when(step == steps - 1)
        def _():
            for k in range(end):
                one(k)
            for j, choice in enumerate(choices_refs):

                @pl.when(pick_ref[0] == j)
                def _():
                    out_ref[blocks - 1] = masked_rank(choice[0], rows_refs[end][...], lengths_ref[blocks - 1])

    def at(i, k):
        block = i * each + k
        return jnp.where(block < blocks, block, block - each)

    return call(
        kernel,
        (lengths, pick),
        (steps,),
        [(maps, pl.BlockSpec((1, rank, width), lambda i, *_, k=k: (at(i, k), 0, 0))) for k in range(each)]
        + [(features, pl.BlockSpec((BLOCK, width), lambda i, *_, k=k: (at(i, k), 0))) for k in range(each)]
        + [whole(choice) for choice in choices],
        [((blocks, rank, BLOCK), features.dtype, constant_spec((blocks, rank, BLOCK)))],
        tokens,
        us,
    )[0]


def summed(terms, at):
    return sum(term[at].astype(jnp.float32) for term in terms).astype(terms[0].dtype)


def down_rows(codes, first, parts, copies, ranks, features, tokens=(), us=1.0):
    blocks, rank, _ = ranks[0].shape
    width = features.shape[1]
    piece = min(width, 512)

    def block_at(code):
        return jnp.maximum((code >> 1) - 1, 0)

    def kernel(codes_ref, a, b, *refs):
        rows_refs, last_ref, outs = refs[:OWN], refs[OWN], refs[OWN + 1 :]
        step = pl.program_id(0)

        def fill(to):
            for k in range(OWN):
                code = codes_ref[first + step * OWN + k]
                mine = summed((a, b), block_at(code))
                mine = jnp.where(code > 1, mine, jnp.zeros_like(mine))

                def put(at, total):
                    value = (ADAPTER_SCALE * total).astype(features.dtype)
                    for out_ref in to:
                        out_ref[k, :, at] = value

                for at in [slice(c, c + piece) for c in range(0, width, piece)]:
                    put(at, jnp.dot(mine, rows_refs[k][:, at], preferred_element_type=jnp.float32))

                @pl.when((code & 1) > 0)
                def _():
                    late = summed((a, b), blocks - 1)
                    for at in [slice(c, c + piece) for c in range(0, width, piece)]:
                        put(
                            at,
                            jnp.dot(mine, rows_refs[k][:, at], preferred_element_type=jnp.float32)
                            + jnp.dot(late, last_ref[:, at], preferred_element_type=jnp.float32),
                        )

        if not copies or parts == 1:
            fill(outs)
        else:
            for part in range(parts):

                @pl.when(step == part)
                def _():
                    fill(outs[part:] if part == parts - 1 else outs[part : part + 1])

    def rows_spec(k):
        return pl.BlockSpec((BLOCK, width), lambda r, at: (block_at(at[first + r * OWN + k]), 0))

    shape = (OWN, rank, width)
    if copies:
        outs = [(shape, features.dtype, constant_spec(shape))] * (parts - 1 + copies)
    else:
        outs = [((parts * OWN, rank, width), features.dtype, pl.BlockSpec(shape, lambda r, *_: (r, 0, 0)))]
    return call(
        kernel,
        (codes,),
        (parts,),
        [whole(array) for array in ranks]
        + [(features, rows_spec(k)) for k in range(OWN)]
        + [(features, pl.BlockSpec((BLOCK, width), lambda r, *_: (blocks - 1, 0), pipeline_mode=pl.Buffered(1)))],
        outs,
        tokens,
        us,
    )


def outputs_of(lengths, codes, parts, base, ranks, features, maps, last_map):
    rows, width = base[0].shape
    blocks = rows // BLOCK
    rank = maps.shape[1]

    def kernel(lengths_ref, codes_ref, one, two, three, *refs):
        terms, refs = refs[: len(ranks)], refs[len(ranks) :]
        rows_ref, maps_ref, last_ref, out_ref, *outs = refs
        late = summed(terms, blocks - 1)
        for k in range(blocks):
            at = slice(k * BLOCK, (k + 1) * BLOCK)
            adapter = maps_ref[k] if k < blocks - 1 else last_ref[0]
            added = lax.dot_general(
                summed(terms, k) if k < blocks - 1 else late,
                adapter,
                (((0,), (0,)), ((), ())),
                preferred_element_type=jnp.float32,
            )
            frozen = one[at].astype(jnp.float32) + two[at].astype(jnp.float32) + three[at].astype(jnp.float32)
            live = lax.broadcasted_iota(jnp.int32, frozen.shape, 0) < lengths_ref[k]
            values = jnp.where(live, frozen + ADAPTER_SCALE * added, 0.0).astype(out_ref.dtype)
            out_ref[at] = values
            if k == blocks - 1:
                for count, out in zip(parts, outs):
                    out[count * rank :] = values
        late_rows = jnp.dot(late, rows_ref[(blocks - 1) * BLOCK :], preferred_element_type=jnp.float32)
        done = 0
        for count, out in zip(parts, outs):

            def one_row(r, carry, out=out, done=done):
                code = codes_ref[done + r]
                at = jnp.maximum((code >> 1) - 1, 0)
                mine = summed(terms, at)
                mine = jnp.where(code > 1, mine, jnp.zeros_like(mine))
                mine_rows = rows_ref[pl.ds(pl.multiple_of(at * BLOCK, BLOCK), BLOCK), :]
                total = jnp.dot(mine, mine_rows, preferred_element_type=jnp.float32)
                total = total + jnp.where((code & 1) > 0, late_rows, 0.0)
                to = r * rank if isinstance(r, int) else pl.ds(pl.multiple_of(r * rank, rank), rank)
                to = slice(to, to + rank) if isinstance(r, int) else to
                out[to] = (ADAPTER_SCALE * total).astype(out.dtype)
                return carry

            if count <= OWN:
                for r in range(count):
                    one_row(r, 0)
            else:
                lax.fori_loop(0, count, one_row, 0)
            done += count

    return call(
        kernel,
        (lengths, codes),
        (1,),
        [whole(array) for array in (*base, *ranks, features, maps, last_map)],
        [((rows, width), maps.dtype, constant_spec((rows, width)))]
        + [
            ((count * rank + BLOCK, width), maps.dtype, constant_spec((count * rank + BLOCK, width)))
            for count in parts
        ],
    )


def finish(pick, values, own, arrived, tokens):
    width = values.shape[1]
    block = values.shape[0] // BLOCK - 1
    rows = own.shape[0] - BLOCK

    def kernel(pick_ref, *refs):
        choices, table_ref, last_ref = refs[:-3], refs[-2], refs[-1]
        table_ref[...] = sum(choice[:rows].astype(jnp.float32) for choice in choices).astype(own.dtype)
        for k, choice in enumerate(choices):

            @pl.when(pick_ref[0] == k)
            def _():
                last_ref[...] = choice[rows:]

    return call(
        kernel,
        (pick,),
        (1,),
        [whole(choice) for choice in (own, *arrived)] + [(values, ANYWHERE)],
        [
            ((rows, width), own.dtype, constant_spec((rows, width))),
            (values.shape, values.dtype, pl.BlockSpec((BLOCK, width), lambda i, *_: (block, 0))),
        ],
        tokens,
        aliases={2 + len(arrived): 1},
    )


def base_terms(columns, hidden, weight, tokens=()):
    rows, depth = hidden.shape
    width = weight.shape[1] // 4
    tile = rows // 4

    def kernel(columns_ref, rows_ref, *refs):
        for k in range(4):
            out_ref = refs[4 + k]
            out_ref[...] = jnp.dot(rows_ref[...], refs[k][...], preferred_element_type=jnp.float32).astype(out_ref.dtype)

    def column(k):
        return pl.BlockSpec((depth, width), lambda i, at: (0, at[k]), pipeline_mode=pl.Buffered(1))

    return call(
        kernel,
        (columns,),
        (rows // tile,),
        [(hidden, pl.BlockSpec((tile, depth), lambda i, *_: (i, 0)))]
        + [(weight, column(k)) for k in range(4)],
        [((rows, width), hidden.dtype, pl.BlockSpec((tile, width), lambda i, *_: (i, 0)))] * 4,
        tokens,
        100.0,
    )


def shift(array, by):
    size = lax.axis_size("dp")
    return lax.ppermute(array, "dp", [(i, (i + by) % size) for i in range(size)])


def shifted(array, source):
    size = lax.axis_size("dp")
    me = lax.axis_index("dp")
    if size > 4:
        taken = lax.dynamic_index_in_dim(lax.all_gather(array, "dp"), source, 0, keepdims=False)
        return [taken], jnp.zeros((1,), jnp.int32)
    choices = [array] + [shift(array, by) for by in range(1, size)]
    return choices, ((me - source) % size).reshape(1)


def add(*arrays):
    return sum(array.astype(jnp.float32) for array in arrays).astype(arrays[0].dtype)


def crossed(array, by):
    return lax.ppermute(array, "tensor", [(i, i ^ by) for i in range(lax.axis_size("tensor"))])


def near(array):
    return crossed(array, 1)


def far(array):
    return crossed(array, 2)


def exchanged(array):
    array = add(array, near(array))
    return array, far(array)


def spread(array):
    return [array] + [crossed(array, by) for by in range(1, lax.axis_size("tensor"))]


def line_reduce_scatter(table):
    size = lax.axis_size("dp")
    me = lax.axis_index("dp")

    def entry(index):
        return lax.dynamic_index_in_dim(table, jnp.clip(index, 0, size - 1), 0, keepdims=False)

    from_left = from_right = None
    for step in range(size - 1):
        right = entry(size - 1 - step + me)
        left = entry(step - (size - 1 - me))
        if step > 0:
            right = add(right, from_left)
            left = add(left, from_right)
        from_left = lax.ppermute(right, "dp", [(i, i + 1) for i in range(step + 1)])
        from_right = lax.ppermute(left, "dp", [(i, i - 1) for i in range(size - 1 - step, size)])
    return entry(me) if size == 1 else add(entry(me), from_left, from_right)


ROLES = ((3, 2, 1, 0), (0, 3, 2, 1), (3, 0, 1, 2), (0, 1, 2, 3))


def body(
    partner,
    block_tenant_index,
    block_live_length,
    tenant_table_row,
    hidden,
    cotangent,
    frozen_value_weight,
    adapter_down_rows,
    adapter_up_matrix,
):
    blocks = block_tenant_index.shape[0]
    kept = blocks - SW
    devices = lax.axis_size("dp")
    me = lax.axis_index("dp")
    column = lax.axis_index("tensor")
    lengths = block_live_length
    line = devices == 4
    order = jnp.arange(devices, dtype=jnp.int32)
    holder = jnp.sum(jnp.where(partner == me, order, 0))

    up_own = adapter_up_matrix[kept:]
    up_choices, up_pick = shifted(up_own, holder)
    cot_terms, down_own = kept_ranks(lengths, adapter_up_matrix, cotangent, adapter_down_rows, [up_own])
    cot_terms, up_last = with_last_rank(lengths, up_pick, up_choices, cotangent, cot_terms)
    rank_cot = exchanged(cot_terms)
    down_choices, down_pick = shifted(after(down_own, rank_cot[0]), holder)

    table_rows = jnp.sum(
        jnp.where(
            block_tenant_index[:, None] == jnp.arange(tenant_table_row.shape[0], dtype=jnp.int32)[None, :],
            tenant_table_row[None, :],
            0,
        ),
        axis=1,
    )
    weights = jnp.where(jnp.arange(blocks) < kept, 2 * (jnp.arange(blocks, dtype=jnp.int32) + 1), 1)

    def codes_of(owners):
        rows = (owners[:, None] * OWN + jnp.arange(OWN, dtype=jnp.int32)[None, :]).reshape(-1)
        return jnp.sum(jnp.where(rows[:, None] == table_rows[None, :], weights[None, :], 0), axis=1)

    columns = jnp.stack([column ^ 3, column ^ 2, column ^ 1, column]).astype(jnp.int32)

    def base(*tokens):
        return base_terms(columns, hidden, frozen_value_weight, tokens)

    def base_parts(terms, *tokens):
        sent, away, given, mine = terms
        away = add(after(away, *tokens), near(sent))
        return (mine, near(given), far(away)), away

    def inputs(*tokens):
        return spread(
            streamed_ranks(lengths, adapter_down_rows, down_pick, down_choices, hidden, 4, tokens, 100.0)
        )

    def outputs(codes, parts, base_sums, rank_in):
        return outputs_of(
            lengths, codes, parts, base_sums, rank_in, cotangent, adapter_up_matrix, up_last
        )

    if line:
        inner = (me == 1) | (me == 2)
        codes = codes_of(jnp.array(ROLES, jnp.int32)[me])
        (first,) = down_rows(codes, 0, 1, 1, rank_cot, hidden)
        from_first = lax.ppermute(first, "dp", [(0, 1), (3, 2), (1, 0), (2, 3)])
        second, third, own = down_rows(codes, OWN, 3, 1, rank_cot, hidden, [first], 1.0)
        terms = base(second, *down_choices[1:])
        second = add(after(second, terms[0]), jnp.where(inner, from_first, jnp.zeros((), first.dtype)))
        from_second = lax.ppermute(second, "dp", [(0, 1), (3, 2), (1, 3), (2, 0)])
        base_sums, away = base_parts(terms, second)
        rank_in = inputs(away)
        third = add(after(third, rank_in[0]), jnp.where(inner, from_second, jnp.zeros((), first.dtype)))
        from_inner = lax.ppermute(third, "dp", [(1, 2), (2, 1)])
        from_third = lax.ppermute(third, "dp", [(0, 1), (3, 2)])
        near_total = lax.optimization_barrier(
            after(own, third).astype(jnp.float32)
            + jnp.where(inner, 0.0, from_first.astype(jnp.float32) + from_second.astype(jnp.float32))
        )
        down_out = (near_total + from_inner.astype(jnp.float32) + from_third.astype(jnp.float32)).astype(own.dtype)

        up_codes = codes_of((me + jnp.array([1, 2, 3, 0], jnp.int32)) % devices)
        values, *sent, kept_here = outputs(up_codes, [OWN] * 4, base_sums, rank_in)
        arrived = [shift(array, by + 1) for by, array in enumerate(sent)]
        value_pick = ((me - partner[me]) % devices).reshape(1)
        up_out, values = finish(value_pick, values, kept_here, arrived, [down_out])
    else:
        codes = codes_of(order)
        (table,) = down_rows(codes, 0, devices, 0, rank_cot, hidden)
        down_out = line_reduce_scatter(table.reshape(devices, OWN, *table.shape[1:]))
        values, table = outputs(codes, [devices * OWN], base_parts(base(table))[0], inputs(table))
        up_table, last_values = table[:-BLOCK], table[-BLOCK:]
        up_out = line_reduce_scatter(up_table.reshape(devices, OWN, -1, values.shape[1]))
        (last_values,), _ = shifted(last_values, partner[me])
        values = jnp.concatenate([values[: kept * BLOCK], last_values], axis=0)
    return (values, down_out, up_out.reshape(OWN, -1, values.shape[1]))


def solution(mesh):
    in_specs = (
        P("groups"),
        P(("groups", "dp")),
        P(("groups", "dp")),
        P("groups"),
        P(("groups", "dp"), "tensor"),
        P(("groups", "dp"), "tensor"),
        P("tensor", None),
        P(("groups", "dp"), None, "tensor"),
        P(("groups", "dp"), None, "tensor"),
    )
    out_specs = (
        P(("groups", "dp"), "tensor"),
        P(("groups", "dp"), None, "tensor"),
        P(("groups", "dp"), None, "tensor"),
    )
    return jax.shard_map(body, mesh=mesh, in_specs=in_specs, out_specs=out_specs, check_vma=False)
```

```python
import jax
import jax.numpy as jnp
from jax import lax
from jax.experimental import pallas as pl
from jax.experimental.pallas import tpu as pltpu
from jax.sharding import PartitionSpec as P

BLOCK = 128
SW = 1
OWN = 4


ADAPTER_SCALE = 0.5

ANYWHERE = pl.BlockSpec(memory_space=pl.ANY)
ROW_PRODUCT = (((1,), (1,)), ((), ()))


def call(kernel, scalars, grid, inputs, outputs, tokens=(), us=1.0, scratch=(), aliases=None):
    def run(*refs):
        cut = len(scalars) + len(inputs)
        return kernel(*refs[:cut], *refs[cut + len(tokens) :])

    return pl.pallas_call(
        run,
        grid_spec=pltpu.PrefetchScalarGridSpec(
            num_scalar_prefetch=len(scalars),
            grid=grid,
            in_specs=[spec for _, spec in inputs] + [ANYWHERE] * len(tokens),
            out_specs=[spec for _, _, spec in outputs],
            scratch_shapes=scratch,
        ),
        out_shape=[jax.ShapeDtypeStruct(shape, kind) for shape, kind, _ in outputs],
        input_output_aliases=aliases or {},
        compiler_params=pltpu.CompilerParams(vmem_limit_bytes=16 * 1024 * 1024),
        cost_estimate=pl.CostEstimate(flops=int(us * 1e9), bytes_accessed=int(us * 3.6e5), transcendentals=0),
    )(*scalars, *[array for array, _ in inputs], *tokens)


def constant_spec(shape):
    return pl.BlockSpec(shape, lambda *_: (0,) * len(shape), pipeline_mode=pl.Buffered(1))


def whole(array):
    return (array, constant_spec(array.shape))


def nothing(*refs):
    pass


def after(array, *tokens):
    return call(
        nothing, (), (1,), [(array, ANYWHERE)], [(array.shape, array.dtype, ANYWHERE)], tokens, 0.1, aliases={0: 0}
    )[0]


def masked_rank(adapter, rows, length):
    ranks = lax.dot_general(adapter, rows, ROW_PRODUCT, preferred_element_type=jnp.float32)
    live = lax.broadcasted_iota(jnp.int32, ranks.shape, 1) < length
    return jnp.where(live, ranks, 0.0).astype(rows.dtype)


def kept_ranks(lengths, maps, features, others, tokens=()):
    blocks, rank, width = maps.shape
    kept = blocks - SW
    last_shape = (SW, *others.shape[1:])

    def kernel(lengths_ref, maps_ref, rows_ref, others_ref, out_ref, last_other, last_again):
        last_other[...] = others_ref[...]
        last_again[...] = others_ref[...]
        for k in range(kept):
            out_ref[k] = masked_rank(maps_ref[k], rows_ref[k * BLOCK : (k + 1) * BLOCK], lengths_ref[k])

    return call(
        kernel,
        (lengths,),
        (1,),
        [
            (maps, pl.BlockSpec((kept, rank, width), lambda i, *_: (0, 0, 0), pipeline_mode=pl.Buffered(1))),
            (features, pl.BlockSpec((kept * BLOCK, width), lambda i, *_: (0, 0), pipeline_mode=pl.Buffered(1))),
            (others, pl.BlockSpec(last_shape, lambda i, *_: (kept, 0, 0), pipeline_mode=pl.Buffered(1))),
        ],
        [
            ((blocks, rank, BLOCK), features.dtype, pl.BlockSpec((kept, rank, BLOCK), lambda i, *_: (0, 0, 0))),
            (last_shape, features.dtype, constant_spec(last_shape)),
            (last_shape, features.dtype, constant_spec(last_shape)),
        ],
        tokens,
    )


def with_last_rank(lengths, partner, me, choices, features, ranks):
    shape = choices[0].shape
    block = ranks.shape[0] - 1
    size = partner.shape[0]

    def kernel(lengths_ref, partner_ref, me_ref, *refs):
        rows_ref, _, out_ref, chosen_ref = refs[-4:]
        for k, choice in enumerate(refs[:-4]):
            if len(choices) == 1:
                chosen_ref[...] = choice[...]
                continue

            @pl.when(partner_ref[lax.rem(me_ref[0] + (size - k), size)] == me_ref[0])
            def _():
                chosen_ref[...] = choice[...]

        out_ref[0] = masked_rank(chosen_ref[0], rows_ref[...], lengths_ref[block])

    return call(
        kernel,
        (lengths, partner, me.reshape(1)),
        (1,),
        [whole(choice) for choice in choices]
        + [(features, pl.BlockSpec((BLOCK, shape[2]), lambda i, *_: (block, 0), pipeline_mode=pl.Buffered(1)))]
        + [(ranks, ANYWHERE)],
        [
            (ranks.shape, ranks.dtype, pl.BlockSpec((1, *ranks.shape[1:]), lambda i, *_: (block, 0, 0))),
            (shape, features.dtype, constant_spec(shape)),
        ],
        aliases={4 + len(choices): 0},
    )


def streamed_ranks(lengths, maps, pick, choices, features, each, tokens=(), us=1.0):
    blocks, rank, width = maps.shape
    steps = pl.cdiv(blocks, each)
    end = blocks - 1 - (steps - 1) * each

    def kernel(lengths_ref, pick_ref, *refs):
        maps_refs, rows_refs, choices_refs, out_ref = refs[:each], refs[each : 2 * each], refs[2 * each : -1], refs[-1]
        step = pl.program_id(0)

        def one(k):
            block = step * each + k
            out_ref[block] = masked_rank(maps_refs[k][0], rows_refs[k][...], lengths_ref[block])

        @pl.when(step < steps - 1)
        def _():
            for k in range(each):
                one(k)

        @pl.when(step == steps - 1)
        def _():
            for k in range(end):
                one(k)
            for j, choice in enumerate(choices_refs):

                @pl.when(pick_ref[0] == j)
                def _():
                    out_ref[blocks - 1] = masked_rank(choice[0], rows_refs[end][...], lengths_ref[blocks - 1])

    def at(i, k):
        block = i * each + k
        return jnp.where(block < blocks, block, block - each)

    return call(
        kernel,
        (lengths, pick),
        (steps,),
        [(maps, pl.BlockSpec((1, rank, width), lambda i, *_, k=k: (at(i, k), 0, 0))) for k in range(each)]
        + [(features, pl.BlockSpec((BLOCK, width), lambda i, *_, k=k: (at(i, k), 0))) for k in range(each)]
        + [whole(choice) for choice in choices],
        [((blocks, rank, BLOCK), features.dtype, constant_spec((blocks, rank, BLOCK)))],
        tokens,
        us,
    )[0]


def summed(terms, at):
    return sum(term[at].astype(jnp.float32) for term in terms).astype(terms[0].dtype)


def down_rows(codes, first, parts, copies, ranks, features, tokens=(), us=1.0):
    blocks, rank, _ = ranks[0].shape
    width = features.shape[1]
    piece = min(width, 512)

    def block_at(code):
        return jnp.maximum((code >> 1) - 1, 0)

    def kernel(codes_ref, a, b, *refs):
        rows_refs, last_ref, outs = refs[:OWN], refs[OWN], refs[OWN + 1 :]
        step = pl.program_id(0)

        def fill(to):
            for k in range(OWN):
                code = codes_ref[first + step * OWN + k]
                mine = summed((a, b), block_at(code))
                mine = jnp.where(code > 1, mine, jnp.zeros_like(mine))

                def put(at, total):
                    value = (ADAPTER_SCALE * total).astype(features.dtype)
                    for out_ref in to:
                        out_ref[k, :, at] = value

                for at in [slice(c, c + piece) for c in range(0, width, piece)]:
                    put(at, jnp.dot(mine, rows_refs[k][:, at], preferred_element_type=jnp.float32))

                @pl.when((code & 1) > 0)
                def _():
                    late = summed((a, b), blocks - 1)
                    for at in [slice(c, c + piece) for c in range(0, width, piece)]:
                        put(
                            at,
                            jnp.dot(mine, rows_refs[k][:, at], preferred_element_type=jnp.float32)
                            + jnp.dot(late, last_ref[:, at], preferred_element_type=jnp.float32),
                        )

        if not copies or parts == 1:
            fill(outs)
        else:
            for part in range(parts):

                @pl.when(step == part)
                def _():
                    fill(outs[part:] if part == parts - 1 else outs[part : part + 1])

    def rows_spec(k):
        return pl.BlockSpec((BLOCK, width), lambda r, at: (block_at(at[first + r * OWN + k]), 0))

    shape = (OWN, rank, width)
    if copies:
        outs = [(shape, features.dtype, constant_spec(shape))] * (parts - 1 + copies)
    else:
        outs = [((parts * OWN, rank, width), features.dtype, pl.BlockSpec(shape, lambda r, *_: (r, 0, 0)))]
    return call(
        kernel,
        (codes,),
        (parts,),
        [whole(array) for array in ranks]
        + [(features, rows_spec(k)) for k in range(OWN)]
        + [(features, pl.BlockSpec((BLOCK, width), lambda r, *_: (blocks - 1, 0), pipeline_mode=pl.Buffered(1)))],
        outs,
        tokens,
        us,
    )


def outputs_of(lengths, codes, parts, base, ranks, features, maps, last_map):
    rows, width = base[0].shape
    blocks = rows // BLOCK
    rank = maps.shape[1]

    def kernel(lengths_ref, codes_ref, one, two, three, *refs):
        terms, refs = refs[: len(ranks)], refs[len(ranks) :]
        rows_ref, maps_ref, last_ref, out_ref, *outs = refs
        late = summed(terms, blocks - 1)
        for k in range(blocks):
            at = slice(k * BLOCK, (k + 1) * BLOCK)
            adapter = maps_ref[k] if k < blocks - 1 else last_ref[0]
            added = lax.dot_general(
                summed(terms, k) if k < blocks - 1 else late,
                adapter,
                (((0,), (0,)), ((), ())),
                preferred_element_type=jnp.float32,
            )
            frozen = one[at].astype(jnp.float32) + two[at].astype(jnp.float32) + three[at].astype(jnp.float32)
            live = lax.broadcasted_iota(jnp.int32, frozen.shape, 0) < lengths_ref[k]
            values = jnp.where(live, frozen + ADAPTER_SCALE * added, 0.0).astype(out_ref.dtype)
            out_ref[at] = values
            if k == blocks - 1:
                for count, out in zip(parts, outs):
                    out[count * rank :] = values
        late_rows = jnp.dot(late, rows_ref[(blocks - 1) * BLOCK :], preferred_element_type=jnp.float32)
        done = 0
        for count, out in zip(parts, outs):

            def one_row(r, carry, out=out, done=done):
                code = codes_ref[done + r]
                at = jnp.maximum((code >> 1) - 1, 0)
                mine = summed(terms, at)
                mine = jnp.where(code > 1, mine, jnp.zeros_like(mine))
                mine_rows = rows_ref[pl.ds(pl.multiple_of(at * BLOCK, BLOCK), BLOCK), :]
                total = jnp.dot(mine, mine_rows, preferred_element_type=jnp.float32)
                total = total + jnp.where((code & 1) > 0, late_rows, 0.0)
                to = r * rank if isinstance(r, int) else pl.ds(pl.multiple_of(r * rank, rank), rank)
                to = slice(to, to + rank) if isinstance(r, int) else to
                out[to] = (ADAPTER_SCALE * total).astype(out.dtype)
                return carry

            if count <= OWN:
                for r in range(count):
                    one_row(r, 0)
            else:
                lax.fori_loop(0, count, one_row, 0)
            done += count

    return call(
        kernel,
        (lengths, codes),
        (1,),
        [whole(array) for array in (*base, *ranks, features, maps, last_map)],
        [((rows, width), maps.dtype, constant_spec((rows, width)))]
        + [
            ((count * rank + BLOCK, width), maps.dtype, constant_spec((count * rank + BLOCK, width)))
            for count in parts
        ],
    )


def finish(pick, values, own, arrived, tokens):
    width = values.shape[1]
    block = values.shape[0] // BLOCK - 1
    rows = own.shape[0] - BLOCK

    def kernel(pick_ref, *refs):
        choices, table_ref, last_ref = refs[:-3], refs[-2], refs[-1]
        table_ref[...] = sum(choice[:rows].astype(jnp.float32) for choice in choices).astype(own.dtype)
        for k, choice in enumerate(choices):

            @pl.when(pick_ref[0] == k)
            def _():
                last_ref[...] = choice[rows:]

    return call(
        kernel,
        (pick,),
        (1,),
        [whole(choice) for choice in (own, *arrived)] + [(values, ANYWHERE)],
        [
            ((rows, width), own.dtype, constant_spec((rows, width))),
            (values.shape, values.dtype, pl.BlockSpec((BLOCK, width), lambda i, *_: (block, 0))),
        ],
        tokens,
        aliases={2 + len(arrived): 1},
    )


def base_terms(columns, hidden, weight, tokens=()):
    rows, depth = hidden.shape
    width = weight.shape[1] // 4
    tile = rows // 4

    def kernel(columns_ref, rows_ref, *refs):
        for k in range(4):
            out_ref = refs[4 + k]
            out_ref[...] = jnp.dot(rows_ref[...], refs[k][...], preferred_element_type=jnp.float32).astype(out_ref.dtype)

    def column(k):
        return pl.BlockSpec((depth, width), lambda i, at: (0, at[k]), pipeline_mode=pl.Buffered(1))

    return call(
        kernel,
        (columns,),
        (rows // tile,),
        [(hidden, pl.BlockSpec((tile, depth), lambda i, *_: (i, 0)))]
        + [(weight, column(k)) for k in range(4)],
        [((rows, width), hidden.dtype, pl.BlockSpec((tile, width), lambda i, *_: (i, 0)))] * 4,
        tokens,
        100.0,
    )


def shift(array, by):
    size = lax.axis_size("dp")
    return lax.ppermute(array, "dp", [(i, (i + by) % size) for i in range(size)])


def shifted(array, source):
    size = lax.axis_size("dp")
    me = lax.axis_index("dp")
    if size > 4:
        taken = lax.dynamic_index_in_dim(lax.all_gather(array, "dp"), source, 0, keepdims=False)
        return [taken], jnp.zeros((1,), jnp.int32)
    choices = [array] + [shift(array, by) for by in range(1, size)]
    return choices, ((me - source) % size).reshape(1)


def add(*arrays):
    return sum(array.astype(jnp.float32) for array in arrays).astype(arrays[0].dtype)


def crossed(array, by):
    return lax.ppermute(array, "tensor", [(i, i ^ by) for i in range(lax.axis_size("tensor"))])


def near(array):
    return crossed(array, 1)


def far(array):
    return crossed(array, 2)


def exchanged(array):
    array = add(array, near(array))
    return array, far(array)


def spread(array):
    return [array] + [crossed(array, by) for by in range(1, lax.axis_size("tensor"))]


def line_reduce_scatter(table):
    size = lax.axis_size("dp")
    me = lax.axis_index("dp")

    def entry(index):
        return lax.dynamic_index_in_dim(table, jnp.clip(index, 0, size - 1), 0, keepdims=False)

    from_left = from_right = None
    for step in range(size - 1):
        right = entry(size - 1 - step + me)
        left = entry(step - (size - 1 - me))
        if step > 0:
            right = add(right, from_left)
            left = add(left, from_right)
        from_left = lax.ppermute(right, "dp", [(i, i + 1) for i in range(step + 1)])
        from_right = lax.ppermute(left, "dp", [(i, i - 1) for i in range(size - 1 - step, size)])
    return entry(me) if size == 1 else add(entry(me), from_left, from_right)


ROLES = ((3, 2, 1, 0), (0, 3, 2, 1), (3, 0, 1, 2), (0, 1, 2, 3))


def body(
    partner,
    block_tenant_index,
    block_live_length,
    tenant_table_row,
    hidden,
    cotangent,
    frozen_value_weight,
    adapter_down_rows,
    adapter_up_matrix,
):
    blocks = block_tenant_index.shape[0]
    kept = blocks - SW
    devices = lax.axis_size("dp")
    me = lax.axis_index("dp")
    column = lax.axis_index("tensor")
    lengths = block_live_length
    line = devices == 4
    order = jnp.arange(devices, dtype=jnp.int32)
    holders = jnp.sum(jnp.where(partner[None, :] == order[:, None], order[None, :], 0), axis=1)
    holder = holders[me]

    up_own = adapter_up_matrix[kept:]
    cot_terms, down_own, down_kept = kept_ranks(lengths, adapter_up_matrix, cotangent, adapter_down_rows, [up_own])
    up_choices, _ = shifted(up_own, holder)
    cot_terms, up_last = with_last_rank(lengths, partner, me, up_choices, cotangent, cot_terms)
    rank_cot = exchanged(cot_terms)
    me = after(me.reshape(1), rank_cot[0])[0]
    down_own = after(down_own, rank_cot[0])

    table_rows = jnp.sum(
        jnp.where(
            block_tenant_index[:, None] == jnp.arange(tenant_table_row.shape[0], dtype=jnp.int32)[None, :],
            tenant_table_row[None, :],
            0,
        ),
        axis=1,
    )
    weights = jnp.where(jnp.arange(blocks) < kept, 2 * (jnp.arange(blocks, dtype=jnp.int32) + 1), 1)

    def codes_of(owners):
        rows = (owners[:, None] * OWN + jnp.arange(OWN, dtype=jnp.int32)[None, :]).reshape(-1)
        return jnp.sum(jnp.where(rows[:, None] == table_rows[None, :], weights[None, :], 0), axis=1)

    columns = jnp.stack([column ^ 3, column ^ 2, column ^ 1, column]).astype(jnp.int32)

    def base(*tokens):
        return base_terms(columns, hidden, frozen_value_weight, tokens)

    def base_parts(terms, *tokens):
        sent, away, given, mine = terms
        away = add(after(away, *tokens), near(sent))
        return (mine, near(given), far(away)), away

    def inputs(down_pick, down_choices, *tokens):
        return spread(
            streamed_ranks(lengths, adapter_down_rows, down_pick, down_choices, hidden, 4, tokens, 100.0)
        )

    def outputs(codes, parts, base_sums, rank_in):
        return outputs_of(
            lengths, codes, parts, base_sums, rank_in, cotangent, adapter_up_matrix, up_last
        )

    if line:
        inner = (me == 1) | (me == 2)
        codes = codes_of(jnp.array(ROLES, jnp.int32)[me])
        (first,) = down_rows(codes, 0, 1, 1, rank_cot, hidden)
        from_first = lax.ppermute(first, "dp", [(0, 1), (3, 2), (1, 0), (2, 3)])
        from_left = lax.ppermute(down_own, "dp", [(0, 1), (1, 2)])
        from_right = lax.ppermute(down_own, "dp", [(3, 2), (2, 1)])
        second, third, own = down_rows(codes, OWN, 3, 1, rank_cot, hidden, [first])
        passing = jnp.where(after(me.reshape(1), second)[0] == 1, from_left, from_right)
        passed = lax.ppermute(passing, "dp", [(1, 2), (2, 1)])
        terms = base(second, passing)
        second = add(after(second, terms[0]), jnp.where(inner, from_first, jnp.zeros((), first.dtype)))
        from_second = lax.ppermute(second, "dp", [(0, 1), (3, 2), (1, 3), (2, 0)])
        down_kept = after(down_kept, second)

        def place(wanted):
            return jnp.where(wanted == me, 0, jnp.where(wanted == me - 1, 1, jnp.where(wanted == me + 1, 2, 3)))

        wanted = place(jnp.where(me == 1, holders[0], holders[3]))
        outward = jnp.where(wanted == 1, from_left, jnp.where(wanted == 2, from_right, passed))
        outward = lax.ppermute(jnp.where(wanted == 0, down_kept, outward), "dp", [(2, 3), (1, 0)])
        down_choices = [down_kept, from_left, from_right, passed, outward]
        down_pick = jnp.where(inner | (holder == me), place(holder), 4).reshape(1).astype(jnp.int32)
        base_sums, away = base_parts(terms, second)
        rank_in = inputs(down_pick, down_choices, away)
        third = add(after(third, rank_in[0]), jnp.where(inner, from_second, jnp.zeros((), first.dtype)))
        from_inner = lax.ppermute(third, "dp", [(1, 2), (2, 1)])
        from_third = lax.ppermute(third, "dp", [(0, 1), (3, 2)])
        near_total = lax.optimization_barrier(
            after(own, third).astype(jnp.float32)
            + jnp.where(inner, 0.0, from_first.astype(jnp.float32) + from_second.astype(jnp.float32))
        )
        down_out = (near_total + from_inner.astype(jnp.float32) + from_third.astype(jnp.float32)).astype(own.dtype)

        up_codes = codes_of((me + jnp.array([1, 2, 3, 0], jnp.int32)) % devices)
        values, *sent, kept_here = outputs(up_codes, [OWN] * 4, base_sums, rank_in)
        arrived = [shift(array, by + 1) for by, array in enumerate(sent)]
        value_pick = ((me - partner[me]) % devices).reshape(1)
        up_out, values = finish(value_pick, values, kept_here, arrived, [down_out])
    else:
        codes = codes_of(order)
        (table,) = down_rows(codes, 0, devices, 0, rank_cot, hidden)
        down_choices, down_pick = shifted(down_kept, holder)
        down_out = line_reduce_scatter(table.reshape(devices, OWN, *table.shape[1:]))
        values, table = outputs(codes, [devices * OWN], base_parts(base(table))[0], inputs(down_pick, down_choices, table))
        up_table, last_values = table[:-BLOCK], table[-BLOCK:]
        up_out = line_reduce_scatter(up_table.reshape(devices, OWN, -1, values.shape[1]))
        (last_values,), _ = shifted(last_values, partner[me])
        values = jnp.concatenate([values[: kept * BLOCK], last_values], axis=0)
    return (values, down_out, up_out.reshape(OWN, -1, values.shape[1]))


def solution(mesh):
    in_specs = (
        P("groups"),
        P(("groups", "dp")),
        P(("groups", "dp")),
        P("groups"),
        P(("groups", "dp"), "tensor"),
        P(("groups", "dp"), "tensor"),
        P("tensor", None),
        P(("groups", "dp"), None, "tensor"),
        P(("groups", "dp"), None, "tensor"),
    )
    out_specs = (
        P(("groups", "dp"), "tensor"),
        P(("groups", "dp"), None, "tensor"),
        P(("groups", "dp"), None, "tensor"),
    )
    return jax.shard_map(body, mesh=mesh, in_specs=in_specs, out_specs=out_specs, check_vma=False)
```

```python
import jax
import jax.numpy as jnp
from jax import lax
from jax.experimental import pallas as pl
from jax.experimental.pallas import tpu as pltpu
from jax.sharding import PartitionSpec as P

BLOCK = 128
SW = 1
OWN = 4


ADAPTER_SCALE = 0.5

ANYWHERE = pl.BlockSpec(memory_space=pl.ANY)
ROW_PRODUCT = (((1,), (1,)), ((), ()))


def call(kernel, scalars, grid, inputs, outputs, tokens=(), us=1.0, scratch=(), aliases=None, vmem=16):
    def run(*refs):
        cut = len(scalars) + len(inputs)
        return kernel(*refs[:cut], *refs[cut + len(tokens) :])

    return pl.pallas_call(
        run,
        grid_spec=pltpu.PrefetchScalarGridSpec(
            num_scalar_prefetch=len(scalars),
            grid=grid,
            in_specs=[spec for _, spec in inputs] + [ANYWHERE] * len(tokens),
            out_specs=[spec for _, _, spec in outputs],
            scratch_shapes=scratch,
        ),
        out_shape=[jax.ShapeDtypeStruct(shape, kind) for shape, kind, _ in outputs],
        input_output_aliases=aliases or {},
        compiler_params=pltpu.CompilerParams(vmem_limit_bytes=vmem * 1024 * 1024),
        cost_estimate=pl.CostEstimate(flops=int(us * 1e9), bytes_accessed=int(us * 3.6e5), transcendentals=0),
    )(*scalars, *[array for array, _ in inputs], *tokens)


def constant_spec(shape):
    return pl.BlockSpec(shape, lambda *_: (0,) * len(shape), pipeline_mode=pl.Buffered(1))


def whole(array):
    return (array, constant_spec(array.shape))


def nothing(*refs):
    pass


def after(array, *tokens):
    return call(
        nothing, (), (1,), [(array, ANYWHERE)], [(array.shape, array.dtype, ANYWHERE)], tokens, 0.1, aliases={0: 0}
    )[0]


def masked_rank(adapter, rows, length):
    ranks = lax.dot_general(adapter, rows, ROW_PRODUCT, preferred_element_type=jnp.float32)
    live = lax.broadcasted_iota(jnp.int32, ranks.shape, 1) < length
    return jnp.where(live, ranks, 0.0).astype(rows.dtype)


def kept_ranks(lengths, maps, features, others, tokens=()):
    blocks, rank, width = maps.shape
    kept = blocks - SW
    last_shape = (SW, *others.shape[1:])
    in_hbm = pl.BlockSpec(memory_space=pltpu.HBM)

    def kernel(lengths_ref, maps_ref, rows_ref, others_ref, out_ref, one_ref, two_ref, done):
        copies = [
            pltpu.make_async_copy(others_ref.at[kept:], to, done.at[k]) for k, to in enumerate((one_ref, two_ref))
        ]
        for copy in copies:
            copy.start()
        for k in range(kept):
            out_ref[k] = masked_rank(maps_ref[k], rows_ref[k * BLOCK : (k + 1) * BLOCK], lengths_ref[k])
        for copy in copies:
            copy.wait()

    return call(
        kernel,
        (lengths,),
        (1,),
        [
            (maps, pl.BlockSpec((kept, rank, width), lambda i, *_: (0, 0, 0), pipeline_mode=pl.Buffered(1))),
            (features, pl.BlockSpec((kept * BLOCK, width), lambda i, *_: (0, 0), pipeline_mode=pl.Buffered(1))),
            (others, in_hbm),
        ],
        [((blocks, rank, BLOCK), features.dtype, pl.BlockSpec((kept, rank, BLOCK), lambda i, *_: (0, 0, 0)))]
        + [(last_shape, features.dtype, in_hbm)] * 2,
        tokens,
        scratch=[pltpu.SemaphoreType.DMA((2,))],
        vmem=40,
    )


def chosen(pick, choices, tokens):
    shape = choices[0].shape

    def kernel(pick_ref, *refs):
        for k, choice in enumerate(refs[:-1]):

            @pl.when(pick_ref[0] == k)
            def _():
                refs[-1][...] = choice[...]

    return call(
        kernel,
        (pick,),
        (1,),
        [whole(choice) for choice in choices],
        [(shape, choices[0].dtype, constant_spec(shape))],
        tokens,
    )[0]


def with_last_rank(lengths, partner, me, choices, features, ranks):
    shape = choices[0].shape
    block = ranks.shape[0] - 1
    size = partner.shape[0]

    def kernel(lengths_ref, partner_ref, me_ref, *refs):
        rows_ref, _, out_ref, chosen_ref = refs[-4:]
        for k, choice in enumerate(refs[:-4]):
            if len(choices) == 1:
                chosen_ref[...] = choice[...]
                continue

            @pl.when(partner_ref[lax.rem(me_ref[0] + (size - k), size)] == me_ref[0])
            def _():
                chosen_ref[...] = choice[...]

        out_ref[0] = masked_rank(chosen_ref[0], rows_ref[...], lengths_ref[block])

    return call(
        kernel,
        (lengths, partner, me.reshape(1)),
        (1,),
        [whole(choice) for choice in choices]
        + [(features, pl.BlockSpec((BLOCK, shape[2]), lambda i, *_: (block, 0), pipeline_mode=pl.Buffered(1)))]
        + [(ranks, ANYWHERE)],
        [
            (ranks.shape, ranks.dtype, pl.BlockSpec((1, *ranks.shape[1:]), lambda i, *_: (block, 0, 0))),
            (shape, features.dtype, constant_spec(shape)),
        ],
        aliases={4 + len(choices): 0},
    )


def streamed_ranks(lengths, maps, pick, choices, features, each, tokens=(), us=1.0):
    blocks, rank, width = maps.shape
    steps = pl.cdiv(blocks, each)
    end = blocks - 1 - (steps - 1) * each

    def kernel(lengths_ref, pick_ref, *refs):
        maps_refs, rows_refs, choices_refs, out_ref = refs[:each], refs[each : 2 * each], refs[2 * each : -1], refs[-1]
        step = pl.program_id(0)

        def one(k):
            block = step * each + k
            out_ref[block] = masked_rank(maps_refs[k][0], rows_refs[k][...], lengths_ref[block])

        @pl.when(step < steps - 1)
        def _():
            for k in range(each):
                one(k)

        @pl.when(step == steps - 1)
        def _():
            for k in range(end):
                one(k)
            for j, choice in enumerate(choices_refs):

                @pl.when(pick_ref[0] == j)
                def _():
                    out_ref[blocks - 1] = masked_rank(choice[0], rows_refs[end][...], lengths_ref[blocks - 1])

    def at(i, k):
        block = i * each + k
        return jnp.where(block < blocks, block, block - each)

    return call(
        kernel,
        (lengths, pick),
        (steps,),
        [(maps, pl.BlockSpec((1, rank, width), lambda i, *_, k=k: (at(i, k), 0, 0))) for k in range(each)]
        + [(features, pl.BlockSpec((BLOCK, width), lambda i, *_, k=k: (at(i, k), 0))) for k in range(each)]
        + [whole(choice) for choice in choices],
        [((blocks, rank, BLOCK), features.dtype, constant_spec((blocks, rank, BLOCK)))],
        tokens,
        us,
    )[0]


def summed(terms, at):
    return sum(term[at].astype(jnp.float32) for term in terms).astype(terms[0].dtype)


def down_rows(codes, first, parts, copies, ranks, features, tokens=(), us=1.0):
    blocks, rank, _ = ranks[0].shape
    width = features.shape[1]
    piece = min(width, 512)

    def block_at(code):
        return jnp.maximum((code >> 1) - 1, 0)

    def kernel(codes_ref, a, b, *refs):
        rows_refs, last_ref, outs = refs[:OWN], refs[OWN], refs[OWN + 1 :]
        step = pl.program_id(0)

        def fill(to):
            for k in range(OWN):
                code = codes_ref[first + step * OWN + k]
                mine = summed((a, b), block_at(code))
                mine = jnp.where(code > 1, mine, jnp.zeros_like(mine))

                def put(at, total):
                    value = (ADAPTER_SCALE * total).astype(features.dtype)
                    for out_ref in to:
                        out_ref[k, :, at] = value

                for at in [slice(c, c + piece) for c in range(0, width, piece)]:
                    put(at, jnp.dot(mine, rows_refs[k][:, at], preferred_element_type=jnp.float32))

                @pl.when((code & 1) > 0)
                def _():
                    late = summed((a, b), blocks - 1)
                    for at in [slice(c, c + piece) for c in range(0, width, piece)]:
                        put(
                            at,
                            jnp.dot(mine, rows_refs[k][:, at], preferred_element_type=jnp.float32)
                            + jnp.dot(late, last_ref[:, at], preferred_element_type=jnp.float32),
                        )

        if not copies or parts == 1:
            fill(outs)
        else:
            for part in range(parts):

                @pl.when(step == part)
                def _():
                    fill(outs[part:] if part == parts - 1 else outs[part : part + 1])

    def rows_spec(k):
        return pl.BlockSpec((BLOCK, width), lambda r, at: (block_at(at[first + r * OWN + k]), 0))

    shape = (OWN, rank, width)
    if copies:
        outs = [(shape, features.dtype, constant_spec(shape))] * (parts - 1 + copies)
    else:
        outs = [((parts * OWN, rank, width), features.dtype, pl.BlockSpec(shape, lambda r, *_: (r, 0, 0)))]
    return call(
        kernel,
        (codes,),
        (parts,),
        [whole(array) for array in ranks]
        + [(features, rows_spec(k)) for k in range(OWN)]
        + [(features, pl.BlockSpec((BLOCK, width), lambda r, *_: (blocks - 1, 0), pipeline_mode=pl.Buffered(1)))],
        outs,
        tokens,
        us,
    )


def outputs_of(lengths, codes, parts, base, ranks, features, maps, last_map):
    rows, width = base[0].shape
    blocks = rows // BLOCK
    rank = maps.shape[1]

    def kernel(lengths_ref, codes_ref, one, two, three, *refs):
        terms, refs = refs[: len(ranks)], refs[len(ranks) :]
        rows_ref, maps_ref, last_ref, out_ref, *outs = refs
        late = summed(terms, blocks - 1)
        for k in range(blocks):
            at = slice(k * BLOCK, (k + 1) * BLOCK)
            adapter = maps_ref[k] if k < blocks - 1 else last_ref[0]
            added = lax.dot_general(
                summed(terms, k) if k < blocks - 1 else late,
                adapter,
                (((0,), (0,)), ((), ())),
                preferred_element_type=jnp.float32,
            )
            frozen = one[at].astype(jnp.float32) + two[at].astype(jnp.float32) + three[at].astype(jnp.float32)
            live = lax.broadcasted_iota(jnp.int32, frozen.shape, 0) < lengths_ref[k]
            values = jnp.where(live, frozen + ADAPTER_SCALE * added, 0.0).astype(out_ref.dtype)
            out_ref[at] = values
            if k == blocks - 1:
                for count, out in zip(parts, outs):
                    out[count * rank :] = values
        late_rows = jnp.dot(late, rows_ref[(blocks - 1) * BLOCK :], preferred_element_type=jnp.float32)
        done = 0
        for count, out in zip(parts, outs):

            def one_row(r, carry, out=out, done=done):
                code = codes_ref[done + r]
                at = jnp.maximum((code >> 1) - 1, 0)
                mine = summed(terms, at)
                mine = jnp.where(code > 1, mine, jnp.zeros_like(mine))
                mine_rows = rows_ref[pl.ds(pl.multiple_of(at * BLOCK, BLOCK), BLOCK), :]
                total = jnp.dot(mine, mine_rows, preferred_element_type=jnp.float32)
                total = total + jnp.where((code & 1) > 0, late_rows, 0.0)
                to = r * rank if isinstance(r, int) else pl.ds(pl.multiple_of(r * rank, rank), rank)
                to = slice(to, to + rank) if isinstance(r, int) else to
                out[to] = (ADAPTER_SCALE * total).astype(out.dtype)
                return carry

            if count <= OWN:
                for r in range(count):
                    one_row(r, 0)
            else:
                lax.fori_loop(0, count, one_row, 0)
            done += count

    return call(
        kernel,
        (lengths, codes),
        (1,),
        [whole(array) for array in (*base, *ranks, features, maps, last_map)],
        [((rows, width), maps.dtype, constant_spec((rows, width)))]
        + [
            ((count * rank + BLOCK, width), maps.dtype, constant_spec((count * rank + BLOCK, width)))
            for count in parts
        ],
    )


def finish(pick, values, own, arrived, tokens):
    width = values.shape[1]
    block = values.shape[0] // BLOCK - 1
    rows = own.shape[0] - BLOCK

    def kernel(pick_ref, *refs):
        choices, table_ref, last_ref = refs[:-3], refs[-2], refs[-1]
        table_ref[...] = sum(choice[:rows].astype(jnp.float32) for choice in choices).astype(own.dtype)
        for k, choice in enumerate(choices):

            @pl.when(pick_ref[0] == k)
            def _():
                last_ref[...] = choice[rows:]

    return call(
        kernel,
        (pick,),
        (1,),
        [whole(choice) for choice in (own, *arrived)] + [(values, ANYWHERE)],
        [
            ((rows, width), own.dtype, constant_spec((rows, width))),
            (values.shape, values.dtype, pl.BlockSpec((BLOCK, width), lambda i, *_: (block, 0))),
        ],
        tokens,
        aliases={2 + len(arrived): 1},
    )


def base_terms(columns, hidden, weight, tokens=()):
    rows, depth = hidden.shape
    width = weight.shape[1] // 4
    tile = rows // 4

    def kernel(columns_ref, rows_ref, *refs):
        for k in range(4):
            out_ref = refs[4 + k]
            out_ref[...] = jnp.dot(rows_ref[...], refs[k][...], preferred_element_type=jnp.float32).astype(out_ref.dtype)

    def column(k):
        return pl.BlockSpec((depth, width), lambda i, at: (0, at[k]), pipeline_mode=pl.Buffered(1))

    return call(
        kernel,
        (columns,),
        (rows // tile,),
        [(hidden, pl.BlockSpec((tile, depth), lambda i, *_: (i, 0)))]
        + [(weight, column(k)) for k in range(4)],
        [((rows, width), hidden.dtype, pl.BlockSpec((tile, width), lambda i, *_: (i, 0)))] * 4,
        tokens,
        100.0,
    )


def shift(array, by):
    size = lax.axis_size("dp")
    return lax.ppermute(array, "dp", [(i, (i + by) % size) for i in range(size)])


def shifted(array, source):
    size = lax.axis_size("dp")
    me = lax.axis_index("dp")
    if size > 4:
        taken = lax.dynamic_index_in_dim(lax.all_gather(array, "dp"), source, 0, keepdims=False)
        return [taken], jnp.zeros((1,), jnp.int32)
    choices = [array] + [shift(array, by) for by in range(1, size)]
    return choices, ((me - source) % size).reshape(1)


def add(*arrays):
    return sum(array.astype(jnp.float32) for array in arrays).astype(arrays[0].dtype)


def crossed(array, by):
    return lax.ppermute(array, "tensor", [(i, i ^ by) for i in range(lax.axis_size("tensor"))])


def near(array):
    return crossed(array, 1)


def far(array):
    return crossed(array, 2)


def exchanged(array):
    array = add(array, near(array))
    return array, far(array)


def spread(array):
    return [array] + [crossed(array, by) for by in range(1, lax.axis_size("tensor"))]


def line_reduce_scatter(table):
    size = lax.axis_size("dp")
    me = lax.axis_index("dp")

    def entry(index):
        return lax.dynamic_index_in_dim(table, jnp.clip(index, 0, size - 1), 0, keepdims=False)

    from_left = from_right = None
    for step in range(size - 1):
        right = entry(size - 1 - step + me)
        left = entry(step - (size - 1 - me))
        if step > 0:
            right = add(right, from_left)
            left = add(left, from_right)
        from_left = lax.ppermute(right, "dp", [(i, i + 1) for i in range(step + 1)])
        from_right = lax.ppermute(left, "dp", [(i, i - 1) for i in range(size - 1 - step, size)])
    return entry(me) if size == 1 else add(entry(me), from_left, from_right)


ROLES = ((3, 2, 1, 0), (0, 3, 2, 1), (3, 0, 1, 2), (0, 1, 2, 3))


def body(
    partner,
    block_tenant_index,
    block_live_length,
    tenant_table_row,
    hidden,
    cotangent,
    frozen_value_weight,
    adapter_down_rows,
    adapter_up_matrix,
):
    blocks = block_tenant_index.shape[0]
    kept = blocks - SW
    devices = lax.axis_size("dp")
    me = lax.axis_index("dp")
    column = lax.axis_index("tensor")
    lengths = block_live_length
    line = devices == 4
    order = jnp.arange(devices, dtype=jnp.int32)
    holders = jnp.sum(jnp.where(partner[None, :] == order[:, None], order[None, :], 0), axis=1)
    holder = holders[me]

    up_own = adapter_up_matrix[kept:]
    cot_terms, down_own, down_kept = kept_ranks(lengths, adapter_up_matrix, cotangent, adapter_down_rows, [up_own])
    up_choices, _ = shifted(up_own, holder)
    cot_terms, up_last = with_last_rank(lengths, partner, me, up_choices, cotangent, cot_terms)
    rank_cot = exchanged(cot_terms)
    down_own = after(down_own, rank_cot[0])

    table_rows = jnp.sum(
        jnp.where(
            block_tenant_index[:, None] == jnp.arange(tenant_table_row.shape[0], dtype=jnp.int32)[None, :],
            tenant_table_row[None, :],
            0,
        ),
        axis=1,
    )
    weights = jnp.where(jnp.arange(blocks) < kept, 2 * (jnp.arange(blocks, dtype=jnp.int32) + 1), 1)

    def codes_of(owners):
        rows = (owners[:, None] * OWN + jnp.arange(OWN, dtype=jnp.int32)[None, :]).reshape(-1)
        return jnp.sum(jnp.where(rows[:, None] == table_rows[None, :], weights[None, :], 0), axis=1)

    columns = jnp.stack([column ^ 3, column ^ 2, column ^ 1, column]).astype(jnp.int32)

    def base(*tokens):
        return base_terms(columns, hidden, frozen_value_weight, tokens)

    def base_parts(terms, *tokens):
        sent, away, given, mine = terms
        away = add(after(away, *tokens), near(sent))
        return (mine, near(given), far(away)), away

    def inputs(down_pick, down_choices, *tokens):
        return spread(
            streamed_ranks(lengths, adapter_down_rows, down_pick, down_choices, hidden, 4, tokens, 100.0)
        )

    def outputs(codes, parts, base_sums, rank_in):
        return outputs_of(
            lengths, codes, parts, base_sums, rank_in, cotangent, adapter_up_matrix, up_last
        )

    if line:
        inner = (me == 1) | (me == 2)
        codes = codes_of(jnp.array(ROLES, jnp.int32)[me])
        (first,) = down_rows(codes, 0, 1, 1, rank_cot, hidden)
        from_first = lax.ppermute(first, "dp", [(0, 1), (3, 2), (1, 0), (2, 3)])
        from_left = lax.ppermute(down_own, "dp", [(0, 1), (1, 2)])
        from_right = lax.ppermute(down_own, "dp", [(3, 2), (2, 1)])
        second, third, own = down_rows(codes, OWN, 3, 1, rank_cot, hidden, [first])
        def place(wanted):
            place = jnp.where(wanted == me, 0, jnp.where(wanted == me - 1, 1, jnp.where(wanted == me + 1, 2, 3)))
            return place.reshape(1).astype(jnp.int32)

        passed = chosen(jnp.where(me == 1, 0, 1).reshape(1), [from_left, from_right], [second])
        terms = base(second, passed)
        passed = lax.ppermute(passed, "dp", [(1, 2), (2, 1)])
        choices = [down_kept, from_left, from_right, passed]
        outward = chosen(place(jnp.where(me == 1, holders[0], holders[3])), choices, [terms[0]])
        second = add(after(second, terms[0], outward), jnp.where(inner, from_first, jnp.zeros((), first.dtype)))
        from_second = lax.ppermute(second, "dp", [(0, 1), (3, 2), (1, 3), (2, 0)])
        down_choices = [*choices, lax.ppermute(outward, "dp", [(2, 3), (1, 0)])]
        down_pick = jnp.where(inner | (holder == me), place(holder), 4)
        base_sums, away = base_parts(terms, second)
        rank_in = inputs(down_pick, down_choices, away)
        third = add(after(third, rank_in[0]), jnp.where(inner, from_second, jnp.zeros((), first.dtype)))
        from_inner = lax.ppermute(third, "dp", [(1, 2), (2, 1)])
        from_third = lax.ppermute(third, "dp", [(0, 1), (3, 2)])
        near_total = lax.optimization_barrier(
            after(own, third).astype(jnp.float32)
            + jnp.where(inner, 0.0, from_first.astype(jnp.float32) + from_second.astype(jnp.float32))
        )
        down_out = (near_total + from_inner.astype(jnp.float32) + from_third.astype(jnp.float32)).astype(own.dtype)

        up_codes = codes_of((me + jnp.array([1, 2, 3, 0], jnp.int32)) % devices)
        values, *sent, kept_here = outputs(up_codes, [OWN] * 4, base_sums, rank_in)
        arrived = [shift(array, by + 1) for by, array in enumerate(sent)]
        value_pick = ((me - partner[me]) % devices).reshape(1)
        up_out, values = finish(value_pick, values, kept_here, arrived, [down_out])
    else:
        codes = codes_of(order)
        (table,) = down_rows(codes, 0, devices, 0, rank_cot, hidden)
        down_choices, down_pick = shifted(down_kept, holder)
        down_out = line_reduce_scatter(table.reshape(devices, OWN, *table.shape[1:]))
        values, table = outputs(codes, [devices * OWN], base_parts(base(table))[0], inputs(down_pick, down_choices, table))
        up_table, last_values = table[:-BLOCK], table[-BLOCK:]
        up_out = line_reduce_scatter(up_table.reshape(devices, OWN, -1, values.shape[1]))
        (last_values,), _ = shifted(last_values, partner[me])
        values = jnp.concatenate([values[: kept * BLOCK], last_values], axis=0)
    return (values, down_out, up_out.reshape(OWN, -1, values.shape[1]))


def solution(mesh):
    in_specs = (
        P("groups"),
        P(("groups", "dp")),
        P(("groups", "dp")),
        P("groups"),
        P(("groups", "dp"), "tensor"),
        P(("groups", "dp"), "tensor"),
        P("tensor", None),
        P(("groups", "dp"), None, "tensor"),
        P(("groups", "dp"), None, "tensor"),
    )
    out_specs = (
        P(("groups", "dp"), "tensor"),
        P(("groups", "dp"), None, "tensor"),
        P(("groups", "dp"), None, "tensor"),
    )
    return jax.shard_map(body, mesh=mesh, in_specs=in_specs, out_specs=out_specs, check_vma=False)
```

```python
import jax
import jax.numpy as jnp
from jax import lax
from jax.experimental import pallas as pl
from jax.experimental.pallas import tpu as pltpu
from jax.sharding import PartitionSpec as P

BLOCK = 128
SW = 1
OWN = 4


ADAPTER_SCALE = 0.5

ANYWHERE = pl.BlockSpec(memory_space=pl.ANY)
ROW_PRODUCT = (((1,), (1,)), ((), ()))


def call(kernel, scalars, grid, inputs, outputs, tokens=(), us=1.0, scratch=(), aliases=None, vmem=16):
    def run(*refs):
        cut = len(scalars) + len(inputs)
        return kernel(*refs[:cut], *refs[cut + len(tokens) :])

    return pl.pallas_call(
        run,
        grid_spec=pltpu.PrefetchScalarGridSpec(
            num_scalar_prefetch=len(scalars),
            grid=grid,
            in_specs=[spec for _, spec in inputs] + [ANYWHERE] * len(tokens),
            out_specs=[spec for _, _, spec in outputs],
            scratch_shapes=scratch,
        ),
        out_shape=[jax.ShapeDtypeStruct(shape, kind) for shape, kind, _ in outputs],
        input_output_aliases=aliases or {},
        compiler_params=pltpu.CompilerParams(vmem_limit_bytes=vmem * 1024 * 1024),
        cost_estimate=pl.CostEstimate(flops=int(us * 1e9), bytes_accessed=int(us * 3.6e5), transcendentals=0),
    )(*scalars, *[array for array, _ in inputs], *tokens)


def constant_spec(shape):
    return pl.BlockSpec(shape, lambda *_: (0,) * len(shape), pipeline_mode=pl.Buffered(1))


def whole(array):
    return (array, constant_spec(array.shape))


def nothing(*refs):
    pass


def after(array, *tokens):
    return call(
        nothing, (), (1,), [(array, ANYWHERE)], [(array.shape, array.dtype, ANYWHERE)], tokens, 0.1, aliases={0: 0}
    )[0]


def masked_rank(adapter, rows, length):
    ranks = lax.dot_general(adapter, rows, ROW_PRODUCT, preferred_element_type=jnp.float32)
    live = lax.broadcasted_iota(jnp.int32, ranks.shape, 1) < length
    return jnp.where(live, ranks, 0.0).astype(rows.dtype)


def kept_ranks(lengths, maps, features, others, tokens=()):
    blocks, rank, width = maps.shape
    kept = blocks - SW
    last_shape = (SW, *others.shape[1:])
    in_hbm = pl.BlockSpec(memory_space=pltpu.HBM)

    def kernel(lengths_ref, maps_ref, rows_ref, others_ref, out_ref, one_ref, two_ref, done):
        copies = [
            pltpu.make_async_copy(others_ref.at[kept:], to, done.at[k]) for k, to in enumerate((one_ref, two_ref))
        ]
        for copy in copies:
            copy.start()
        for k in range(kept):
            out_ref[k] = masked_rank(maps_ref[k], rows_ref[k * BLOCK : (k + 1) * BLOCK], lengths_ref[k])
        for copy in copies:
            copy.wait()

    return call(
        kernel,
        (lengths,),
        (1,),
        [
            (maps, pl.BlockSpec((kept, rank, width), lambda i, *_: (0, 0, 0), pipeline_mode=pl.Buffered(1))),
            (features, pl.BlockSpec((kept * BLOCK, width), lambda i, *_: (0, 0), pipeline_mode=pl.Buffered(1))),
            (others, in_hbm),
        ],
        [((blocks, rank, BLOCK), features.dtype, pl.BlockSpec((kept, rank, BLOCK), lambda i, *_: (0, 0, 0)))]
        + [(last_shape, features.dtype, in_hbm)] * 2,
        tokens,
        scratch=[pltpu.SemaphoreType.DMA((2,))],
        vmem=60,
    )


def chosen(pick, choices, tokens):
    shape = choices[0].shape

    def kernel(pick_ref, *refs):
        for k, choice in enumerate(refs[:-1]):

            @pl.when(pick_ref[0] == k)
            def _():
                refs[-1][...] = choice[...]

    return call(
        kernel,
        (pick,),
        (1,),
        [whole(choice) for choice in choices],
        [(shape, choices[0].dtype, constant_spec(shape))],
        tokens,
        1.0,
    )[0]


def with_last_rank(lengths, partner, me, choices, features, ranks):
    shape = choices[0].shape
    block = ranks.shape[0] - 1
    size = partner.shape[0]

    def kernel(lengths_ref, partner_ref, me_ref, *refs):
        rows_ref, _, out_ref, chosen_ref = refs[-4:]
        for k, choice in enumerate(refs[:-4]):
            if len(choices) == 1:
                chosen_ref[...] = choice[...]
                continue

            @pl.when(partner_ref[lax.rem(me_ref[0] + (size - k), size)] == me_ref[0])
            def _():
                chosen_ref[...] = choice[...]

        out_ref[0] = masked_rank(chosen_ref[0], rows_ref[...], lengths_ref[block])

    return call(
        kernel,
        (lengths, partner, me.reshape(1)),
        (1,),
        [whole(choice) for choice in choices]
        + [(features, pl.BlockSpec((BLOCK, shape[2]), lambda i, *_: (block, 0), pipeline_mode=pl.Buffered(1)))]
        + [(ranks, ANYWHERE)],
        [
            (ranks.shape, ranks.dtype, pl.BlockSpec((1, *ranks.shape[1:]), lambda i, *_: (block, 0, 0))),
            (shape, features.dtype, constant_spec(shape)),
        ],
        aliases={4 + len(choices): 0},
    )


def streamed_ranks(lengths, maps, pick, choices, features, each, tokens=(), us=1.0):
    blocks, rank, width = maps.shape
    steps = pl.cdiv(blocks, each)
    end = blocks - 1 - (steps - 1) * each

    def kernel(lengths_ref, pick_ref, *refs):
        maps_refs, rows_refs, choices_refs, out_ref = refs[:each], refs[each : 2 * each], refs[2 * each : -1], refs[-1]
        step = pl.program_id(0)

        def one(k):
            block = step * each + k
            out_ref[block] = masked_rank(maps_refs[k][0], rows_refs[k][...], lengths_ref[block])

        @pl.when(step < steps - 1)
        def _():
            for k in range(each):
                one(k)

        @pl.when(step == steps - 1)
        def _():
            for k in range(end):
                one(k)
            for j, choice in enumerate(choices_refs):

                @pl.when(pick_ref[0] == j)
                def _():
                    out_ref[blocks - 1] = masked_rank(choice[0], rows_refs[end][...], lengths_ref[blocks - 1])

    def at(i, k):
        block = i * each + k
        return jnp.where(block < blocks, block, block - each)

    return call(
        kernel,
        (lengths, pick),
        (steps,),
        [(maps, pl.BlockSpec((1, rank, width), lambda i, *_, k=k: (at(i, k), 0, 0))) for k in range(each)]
        + [(features, pl.BlockSpec((BLOCK, width), lambda i, *_, k=k: (at(i, k), 0))) for k in range(each)]
        + [whole(choice) for choice in choices],
        [((blocks, rank, BLOCK), features.dtype, constant_spec((blocks, rank, BLOCK)))],
        tokens,
        us,
    )[0]


def summed(terms, at):
    return sum(term[at].astype(jnp.float32) for term in terms).astype(terms[0].dtype)


def down_rows(codes, first, parts, copies, ranks, features, tokens=(), us=1.0):
    blocks, rank, _ = ranks[0].shape
    width = features.shape[1]
    piece = min(width, 512)

    def block_at(code):
        return jnp.maximum((code >> 1) - 1, 0)

    def kernel(codes_ref, a, b, *refs):
        rows_refs, last_ref, outs = refs[:OWN], refs[OWN], refs[OWN + 1 :]
        step = pl.program_id(0)

        def fill(to):
            for k in range(OWN):
                code = codes_ref[first + step * OWN + k]
                mine = summed((a, b), block_at(code))
                mine = jnp.where(code > 1, mine, jnp.zeros_like(mine))

                def put(at, total):
                    value = (ADAPTER_SCALE * total).astype(features.dtype)
                    for out_ref in to:
                        out_ref[k, :, at] = value

                for at in [slice(c, c + piece) for c in range(0, width, piece)]:
                    put(at, jnp.dot(mine, rows_refs[k][:, at], preferred_element_type=jnp.float32))

                @pl.when((code & 1) > 0)
                def _():
                    late = summed((a, b), blocks - 1)
                    for at in [slice(c, c + piece) for c in range(0, width, piece)]:
                        put(
                            at,
                            jnp.dot(mine, rows_refs[k][:, at], preferred_element_type=jnp.float32)
                            + jnp.dot(late, last_ref[:, at], preferred_element_type=jnp.float32),
                        )

        if not copies or parts == 1:
            fill(outs)
        else:
            for part in range(parts):

                @pl.when(step == part)
                def _():
                    fill(outs[part:] if part == parts - 1 else outs[part : part + 1])

    def rows_spec(k):
        return pl.BlockSpec((BLOCK, width), lambda r, at: (block_at(at[first + r * OWN + k]), 0))

    shape = (OWN, rank, width)
    if copies:
        outs = [(shape, features.dtype, constant_spec(shape))] * (parts - 1 + copies)
    else:
        outs = [((parts * OWN, rank, width), features.dtype, pl.BlockSpec(shape, lambda r, *_: (r, 0, 0)))]
    return call(
        kernel,
        (codes,),
        (parts,),
        [whole(array) for array in ranks]
        + [(features, rows_spec(k)) for k in range(OWN)]
        + [(features, pl.BlockSpec((BLOCK, width), lambda r, *_: (blocks - 1, 0), pipeline_mode=pl.Buffered(1)))],
        outs,
        tokens,
        us,
    )


def outputs_of(lengths, codes, parts, base, ranks, features, maps, last_map):
    rows, width = base[0].shape
    blocks = rows // BLOCK
    rank = maps.shape[1]

    def kernel(lengths_ref, codes_ref, one, two, three, *refs):
        terms, refs = refs[: len(ranks)], refs[len(ranks) :]
        rows_ref, maps_ref, last_ref, out_ref, *outs = refs
        late = summed(terms, blocks - 1)
        for k in range(blocks):
            at = slice(k * BLOCK, (k + 1) * BLOCK)
            adapter = maps_ref[k] if k < blocks - 1 else last_ref[0]
            added = lax.dot_general(
                summed(terms, k) if k < blocks - 1 else late,
                adapter,
                (((0,), (0,)), ((), ())),
                preferred_element_type=jnp.float32,
            )
            frozen = one[at].astype(jnp.float32) + two[at].astype(jnp.float32) + three[at].astype(jnp.float32)
            live = lax.broadcasted_iota(jnp.int32, frozen.shape, 0) < lengths_ref[k]
            values = jnp.where(live, frozen + ADAPTER_SCALE * added, 0.0).astype(out_ref.dtype)
            out_ref[at] = values
            if k == blocks - 1:
                for count, out in zip(parts, outs):
                    out[count * rank :] = values
        late_rows = jnp.dot(late, rows_ref[(blocks - 1) * BLOCK :], preferred_element_type=jnp.float32)
        done = 0
        for count, out in zip(parts, outs):

            def one_row(r, carry, out=out, done=done):
                code = codes_ref[done + r]
                at = jnp.maximum((code >> 1) - 1, 0)
                mine = summed(terms, at)
                mine = jnp.where(code > 1, mine, jnp.zeros_like(mine))
                mine_rows = rows_ref[pl.ds(pl.multiple_of(at * BLOCK, BLOCK), BLOCK), :]
                total = jnp.dot(mine, mine_rows, preferred_element_type=jnp.float32)
                total = total + jnp.where((code & 1) > 0, late_rows, 0.0)
                to = r * rank if isinstance(r, int) else pl.ds(pl.multiple_of(r * rank, rank), rank)
                to = slice(to, to + rank) if isinstance(r, int) else to
                out[to] = (ADAPTER_SCALE * total).astype(out.dtype)
                return carry

            if count <= OWN:
                for r in range(count):
                    one_row(r, 0)
            else:
                lax.fori_loop(0, count, one_row, 0)
            done += count

    return call(
        kernel,
        (lengths, codes),
        (1,),
        [whole(array) for array in (*base, *ranks, features, maps, last_map)],
        [((rows, width), maps.dtype, constant_spec((rows, width)))]
        + [
            ((count * rank + BLOCK, width), maps.dtype, constant_spec((count * rank + BLOCK, width)))
            for count in parts
        ],
        vmem=60,
    )


def finish(pick, values, own, arrived, tokens):
    width = values.shape[1]
    block = values.shape[0] // BLOCK - 1
    rows = own.shape[0] - BLOCK

    def kernel(pick_ref, *refs):
        choices, table_ref, last_ref = refs[:-3], refs[-2], refs[-1]
        table_ref[...] = sum(choice[:rows].astype(jnp.float32) for choice in choices).astype(own.dtype)
        for k, choice in enumerate(choices):

            @pl.when(pick_ref[0] == k)
            def _():
                last_ref[...] = choice[rows:]

    return call(
        kernel,
        (pick,),
        (1,),
        [whole(choice) for choice in (own, *arrived)] + [(values, ANYWHERE)],
        [
            ((rows, width), own.dtype, constant_spec((rows, width))),
            (values.shape, values.dtype, pl.BlockSpec((BLOCK, width), lambda i, *_: (block, 0))),
        ],
        tokens,
        aliases={2 + len(arrived): 1},
    )


def base_terms(columns, hidden, weight, tokens=()):
    rows, depth = hidden.shape
    width = weight.shape[1] // 4
    tile = rows // 4

    def kernel(columns_ref, rows_ref, *refs):
        for k in range(4):
            out_ref = refs[4 + k]
            out_ref[...] = jnp.dot(rows_ref[...], refs[k][...], preferred_element_type=jnp.float32).astype(out_ref.dtype)

    def column(k):
        return pl.BlockSpec((depth, width), lambda i, at: (0, at[k]), pipeline_mode=pl.Buffered(1))

    return call(
        kernel,
        (columns,),
        (rows // tile,),
        [(hidden, pl.BlockSpec((tile, depth), lambda i, *_: (i, 0)))]
        + [(weight, column(k)) for k in range(4)],
        [((rows, width), hidden.dtype, pl.BlockSpec((tile, width), lambda i, *_: (i, 0)))] * 4,
        tokens,
        100.0,
    )


def shift(array, by):
    size = lax.axis_size("dp")
    return lax.ppermute(array, "dp", [(i, (i + by) % size) for i in range(size)])


def shifted(array, source):
    size = lax.axis_size("dp")
    me = lax.axis_index("dp")
    if size > 4:
        taken = lax.dynamic_index_in_dim(lax.all_gather(array, "dp"), source, 0, keepdims=False)
        return [taken], jnp.zeros((1,), jnp.int32)
    choices = [array] + [shift(array, by) for by in range(1, size)]
    return choices, ((me - source) % size).reshape(1)


def add(*arrays):
    return sum(array.astype(jnp.float32) for array in arrays).astype(arrays[0].dtype)


def crossed(array, by):
    return lax.ppermute(array, "tensor", [(i, i ^ by) for i in range(lax.axis_size("tensor"))])


def near(array):
    return crossed(array, 1)


def far(array):
    return crossed(array, 2)


def exchanged(array):
    array = add(array, near(array))
    return array, far(array)


def spread(array):
    return [array] + [crossed(array, by) for by in range(1, lax.axis_size("tensor"))]


def line_reduce_scatter(table):
    size = lax.axis_size("dp")
    me = lax.axis_index("dp")

    def entry(index):
        return lax.dynamic_index_in_dim(table, jnp.clip(index, 0, size - 1), 0, keepdims=False)

    from_left = from_right = None
    for step in range(size - 1):
        right = entry(size - 1 - step + me)
        left = entry(step - (size - 1 - me))
        if step > 0:
            right = add(right, from_left)
            left = add(left, from_right)
        from_left = lax.ppermute(right, "dp", [(i, i + 1) for i in range(step + 1)])
        from_right = lax.ppermute(left, "dp", [(i, i - 1) for i in range(size - 1 - step, size)])
    return entry(me) if size == 1 else add(entry(me), from_left, from_right)


ROLES = ((3, 2, 1, 0), (0, 3, 2, 1), (3, 0, 1, 2), (0, 1, 2, 3))


def body(
    partner,
    block_tenant_index,
    block_live_length,
    tenant_table_row,
    hidden,
    cotangent,
    frozen_value_weight,
    adapter_down_rows,
    adapter_up_matrix,
):
    blocks = block_tenant_index.shape[0]
    kept = blocks - SW
    devices = lax.axis_size("dp")
    me = lax.axis_index("dp")
    column = lax.axis_index("tensor")
    lengths = block_live_length
    line = devices == 4
    order = jnp.arange(devices, dtype=jnp.int32)
    holders = jnp.sum(jnp.where(partner[None, :] == order[:, None], order[None, :], 0), axis=1)
    holder = holders[me]

    up_own = adapter_up_matrix[kept:]
    cot_terms, down_own, down_kept = kept_ranks(lengths, adapter_up_matrix, cotangent, adapter_down_rows, [up_own])
    up_choices, _ = shifted(up_own, holder)
    cot_terms, up_last = with_last_rank(lengths, partner, me, up_choices, cotangent, cot_terms)
    rank_cot = exchanged(cot_terms)
    down_own = after(down_own, rank_cot[0])

    table_rows = jnp.sum(
        jnp.where(
            block_tenant_index[:, None] == jnp.arange(tenant_table_row.shape[0], dtype=jnp.int32)[None, :],
            tenant_table_row[None, :],
            0,
        ),
        axis=1,
    )
    weights = jnp.where(jnp.arange(blocks) < kept, 2 * (jnp.arange(blocks, dtype=jnp.int32) + 1), 1)

    def codes_of(owners):
        rows = (owners[:, None] * OWN + jnp.arange(OWN, dtype=jnp.int32)[None, :]).reshape(-1)
        return jnp.sum(jnp.where(rows[:, None] == table_rows[None, :], weights[None, :], 0), axis=1)

    columns = jnp.stack([column ^ 3, column ^ 2, column ^ 1, column]).astype(jnp.int32)

    def base(*tokens):
        return base_terms(columns, hidden, frozen_value_weight, tokens)

    def base_parts(terms, *tokens):
        sent, away, given, mine = terms
        away = add(after(away, *tokens), near(sent))
        return (mine, near(given), far(away)), away

    def inputs(down_pick, down_choices, *tokens):
        return spread(
            streamed_ranks(lengths, adapter_down_rows, down_pick, down_choices, hidden, 4, tokens, 100.0)
        )

    def outputs(codes, parts, base_sums, rank_in):
        return outputs_of(
            lengths, codes, parts, base_sums, rank_in, cotangent, adapter_up_matrix, up_last
        )

    if line:
        inner = (me == 1) | (me == 2)
        codes = codes_of(jnp.array(ROLES, jnp.int32)[me])
        (first,) = down_rows(codes, 0, 1, 1, rank_cot, hidden)
        from_first = lax.ppermute(first, "dp", [(0, 1), (3, 2), (1, 0), (2, 3)])
        from_left = lax.ppermute(down_own, "dp", [(0, 1), (1, 2)])
        from_right = lax.ppermute(down_own, "dp", [(3, 2), (2, 1)])
        def place(wanted):
            place = jnp.where(wanted == me, 0, jnp.where(wanted == me - 1, 1, jnp.where(wanted == me + 1, 2, 3)))
            return place.reshape(1).astype(jnp.int32)

        passed = chosen(jnp.where(me == 1, 0, 1).reshape(1), [from_left, from_right], [first])
        second, third, own = down_rows(codes, OWN, 3, 1, rank_cot, hidden, [passed], 100.0)
        passed = lax.ppermute(passed, "dp", [(1, 2), (2, 1)])
        choices = [down_kept, from_left, from_right, passed]
        outward = chosen(place(jnp.where(me == 1, holders[0], holders[3])), choices, [second])
        terms = base(second, outward)
        second = add(after(second, terms[0]), jnp.where(inner, from_first, jnp.zeros((), first.dtype)))
        from_second = lax.ppermute(second, "dp", [(0, 1), (3, 2), (1, 3), (2, 0)])
        down_choices = [*choices, lax.ppermute(outward, "dp", [(2, 3), (1, 0)])]
        down_pick = jnp.where(inner | (holder == me), place(holder), 4)
        base_sums, away = base_parts(terms, second)
        rank_in = inputs(down_pick, down_choices, away)
        third = add(after(third, rank_in[0]), jnp.where(inner, from_second, jnp.zeros((), first.dtype)))
        from_inner = lax.ppermute(third, "dp", [(1, 2), (2, 1)])
        from_third = lax.ppermute(third, "dp", [(0, 1), (3, 2)])
        near_total = lax.optimization_barrier(
            after(own, third).astype(jnp.float32)
            + jnp.where(inner, 0.0, from_first.astype(jnp.float32) + from_second.astype(jnp.float32))
        )
        down_out = (near_total + from_inner.astype(jnp.float32) + from_third.astype(jnp.float32)).astype(own.dtype)

        up_codes = codes_of((me + jnp.array([1, 2, 3, 0], jnp.int32)) % devices)
        values, *sent, kept_here = outputs(up_codes, [OWN] * 4, base_sums, rank_in)
        arrived = [shift(array, by + 1) for by, array in enumerate(sent)]
        value_pick = ((me - partner[me]) % devices).reshape(1)
        up_out, values = finish(value_pick, values, kept_here, arrived, [down_out])
    else:
        codes = codes_of(order)
        (table,) = down_rows(codes, 0, devices, 0, rank_cot, hidden)
        down_choices, down_pick = shifted(down_kept, holder)
        down_out = line_reduce_scatter(table.reshape(devices, OWN, *table.shape[1:]))
        values, table = outputs(codes, [devices * OWN], base_parts(base(table))[0], inputs(down_pick, down_choices, table))
        up_table, last_values = table[:-BLOCK], table[-BLOCK:]
        up_out = line_reduce_scatter(up_table.reshape(devices, OWN, -1, values.shape[1]))
        (last_values,), _ = shifted(last_values, partner[me])
        values = jnp.concatenate([values[: kept * BLOCK], last_values], axis=0)
    return (values, down_out, up_out.reshape(OWN, -1, values.shape[1]))


def solution(mesh):
    in_specs = (
        P("groups"),
        P(("groups", "dp")),
        P(("groups", "dp")),
        P("groups"),
        P(("groups", "dp"), "tensor"),
        P(("groups", "dp"), "tensor"),
        P("tensor", None),
        P(("groups", "dp"), None, "tensor"),
        P(("groups", "dp"), None, "tensor"),
    )
    out_specs = (
        P(("groups", "dp"), "tensor"),
        P(("groups", "dp"), None, "tensor"),
        P(("groups", "dp"), None, "tensor"),
    )
    return jax.shard_map(body, mesh=mesh, in_specs=in_specs, out_specs=out_specs, check_vma=False)
```

```python
import jax
import jax.numpy as jnp
from jax import lax
from jax.experimental import pallas as pl
from jax.experimental.pallas import tpu as pltpu
from jax.sharding import PartitionSpec as P

BLOCK = 128
SW = 1
OWN = 4


ADAPTER_SCALE = 0.5

ANYWHERE = pl.BlockSpec(memory_space=pl.ANY)
ROW_PRODUCT = (((1,), (1,)), ((), ()))


def call(kernel, scalars, grid, inputs, outputs, tokens=(), us=1.0, scratch=(), aliases=None, vmem=16):
    def run(*refs):
        cut = len(scalars) + len(inputs)
        return kernel(*refs[:cut], *refs[cut + len(tokens) :])

    return pl.pallas_call(
        run,
        grid_spec=pltpu.PrefetchScalarGridSpec(
            num_scalar_prefetch=len(scalars),
            grid=grid,
            in_specs=[spec for _, spec in inputs] + [ANYWHERE] * len(tokens),
            out_specs=[spec for _, _, spec in outputs],
            scratch_shapes=scratch,
        ),
        out_shape=[jax.ShapeDtypeStruct(shape, kind) for shape, kind, _ in outputs],
        input_output_aliases=aliases or {},
        compiler_params=pltpu.CompilerParams(vmem_limit_bytes=vmem * 1024 * 1024),
        cost_estimate=pl.CostEstimate(flops=int(us * 1e9), bytes_accessed=int(us * 3.6e5), transcendentals=0),
    )(*scalars, *[array for array, _ in inputs], *tokens)


def constant_spec(shape):
    return pl.BlockSpec(shape, lambda *_: (0,) * len(shape), pipeline_mode=pl.Buffered(1))


def whole(array):
    return (array, constant_spec(array.shape))


def nothing(*refs):
    pass


def after(array, *tokens):
    return call(
        nothing, (), (1,), [(array, ANYWHERE)], [(array.shape, array.dtype, ANYWHERE)], tokens, 0.1, aliases={0: 0}
    )[0]


def masked_rank(adapter, rows, length):
    ranks = lax.dot_general(adapter, rows, ROW_PRODUCT, preferred_element_type=jnp.float32)
    live = lax.broadcasted_iota(jnp.int32, ranks.shape, 1) < length
    return jnp.where(live, ranks, 0.0).astype(rows.dtype)


def kept_ranks(lengths, maps, features, others, tokens=()):
    blocks, rank, width = maps.shape
    kept = blocks - SW
    last_shape = (SW, *others.shape[1:])

    def kernel(lengths_ref, maps_ref, rows_ref, others_ref, out_ref, last_other):
        last_other[...] = others_ref[...]
        for k in range(kept):
            out_ref[k] = masked_rank(maps_ref[k], rows_ref[k * BLOCK : (k + 1) * BLOCK], lengths_ref[k])

    return call(
        kernel,
        (lengths,),
        (1,),
        [
            (maps, pl.BlockSpec((kept, rank, width), lambda i, *_: (0, 0, 0), pipeline_mode=pl.Buffered(1))),
            (features, pl.BlockSpec((kept * BLOCK, width), lambda i, *_: (0, 0), pipeline_mode=pl.Buffered(1))),
            (others, pl.BlockSpec(last_shape, lambda i, *_: (kept, 0, 0), pipeline_mode=pl.Buffered(1))),
        ],
        [
            ((blocks, rank, BLOCK), features.dtype, pl.BlockSpec((kept, rank, BLOCK), lambda i, *_: (0, 0, 0))),
            (last_shape, features.dtype, constant_spec(last_shape)),
        ],
        tokens,
        vmem=60,
    )


def passed_on(partner, me, own, from_left, from_right, tokens):
    shape = own.shape

    def kernel(partner_ref, me_ref, own_ref, left_ref, right_ref, inner_ref, outer_ref):
        left = me_ref[0] == 1

        @pl.when(left)
        def _():
            inner_ref[...] = left_ref[...]
            outer_ref[...] = left_ref[...]

        @pl.when(jnp.logical_not(left))
        def _():
            inner_ref[...] = right_ref[...]
            outer_ref[...] = right_ref[...]

        @pl.when(partner_ref[me_ref[0]] == jnp.where(left, 3, 0))
        def _():
            outer_ref[...] = own_ref[...]

    return call(
        kernel,
        (partner, me.reshape(1)),
        (1,),
        [whole(array) for array in (own, from_left, from_right)],
        [(shape, own.dtype, constant_spec(shape))] * 2,
        tokens,
        1.0,
    )


def with_last_rank(lengths, partner, me, choices, features, ranks):
    shape = choices[0].shape
    block = ranks.shape[0] - 1
    size = partner.shape[0]

    def kernel(lengths_ref, partner_ref, me_ref, *refs):
        rows_ref, _, out_ref, chosen_ref = refs[-4:]
        for k, choice in enumerate(refs[:-4]):
            if len(choices) == 1:
                chosen_ref[...] = choice[...]
                continue

            @pl.when(partner_ref[lax.rem(me_ref[0] + (size - k), size)] == me_ref[0])
            def _():
                chosen_ref[...] = choice[...]

        out_ref[0] = masked_rank(chosen_ref[0], rows_ref[...], lengths_ref[block])

    return call(
        kernel,
        (lengths, partner, me.reshape(1)),
        (1,),
        [whole(choice) for choice in choices]
        + [(features, pl.BlockSpec((BLOCK, shape[2]), lambda i, *_: (block, 0), pipeline_mode=pl.Buffered(1)))]
        + [(ranks, ANYWHERE)],
        [
            (ranks.shape, ranks.dtype, pl.BlockSpec((1, *ranks.shape[1:]), lambda i, *_: (block, 0, 0))),
            (shape, features.dtype, constant_spec(shape)),
        ],
        aliases={4 + len(choices): 0},
    )


def streamed_ranks(lengths, partner, me, maps, choices, features, each, tokens=(), us=1.0):
    blocks, rank, width = maps.shape
    steps = pl.cdiv(blocks, each)
    end = blocks - 1 - (steps - 1) * each

    def picked(partner_ref, at):
        if len(choices) == 1:
            return [at == at]
        held = [
            partner_ref[at] == at,
            (partner_ref[jnp.maximum(at - 1, 0)] == at) & (at > 0),
            (partner_ref[jnp.minimum(at + 1, 3)] == at) & (at < 3),
        ]
        other = jnp.logical_not(held[0] | held[1] | held[2])
        inner = (at == 1) | (at == 2)
        return [*held, other & inner, other & jnp.logical_not(inner)]

    def kernel(lengths_ref, partner_ref, me_ref, *refs):
        maps_refs, rows_refs, choices_refs, out_ref = refs[:each], refs[each : 2 * each], refs[2 * each : -1], refs[-1]
        step = pl.program_id(0)

        def one(k):
            block = step * each + k
            out_ref[block] = masked_rank(maps_refs[k][0], rows_refs[k][...], lengths_ref[block])

        @pl.when(step < steps - 1)
        def _():
            for k in range(each):
                one(k)

        @pl.when(step == steps - 1)
        def _():
            for k in range(end):
                one(k)
            for choice, use in zip(choices_refs, picked(partner_ref, me_ref[0])):

                @pl.when(use)
                def _():
                    out_ref[blocks - 1] = masked_rank(choice[0], rows_refs[end][...], lengths_ref[blocks - 1])

    def at(i, k):
        block = i * each + k
        return jnp.where(block < blocks, block, block - each)

    return call(
        kernel,
        (lengths, partner, me.reshape(1)),
        (steps,),
        [(maps, pl.BlockSpec((1, rank, width), lambda i, *_, k=k: (at(i, k), 0, 0))) for k in range(each)]
        + [(features, pl.BlockSpec((BLOCK, width), lambda i, *_, k=k: (at(i, k), 0))) for k in range(each)]
        + [whole(choice) for choice in choices],
        [((blocks, rank, BLOCK), features.dtype, constant_spec((blocks, rank, BLOCK)))],
        tokens,
        us,
    )[0]


def summed(terms, at):
    return sum(term[at].astype(jnp.float32) for term in terms).astype(terms[0].dtype)


def down_rows(codes, first, parts, copies, ranks, features, tokens=(), us=1.0):
    blocks, rank, _ = ranks[0].shape
    width = features.shape[1]
    piece = min(width, 512)

    def block_at(code):
        return jnp.maximum((code >> 1) - 1, 0)

    def kernel(codes_ref, a, b, *refs):
        rows_refs, last_ref, outs = refs[:OWN], refs[OWN], refs[OWN + 1 :]
        step = pl.program_id(0)

        def fill(to):
            for k in range(OWN):
                code = codes_ref[first + step * OWN + k]
                mine = summed((a, b), block_at(code))
                mine = jnp.where(code > 1, mine, jnp.zeros_like(mine))

                def put(at, total):
                    value = (ADAPTER_SCALE * total).astype(features.dtype)
                    for out_ref in to:
                        out_ref[k, :, at] = value

                for at in [slice(c, c + piece) for c in range(0, width, piece)]:
                    put(at, jnp.dot(mine, rows_refs[k][:, at], preferred_element_type=jnp.float32))

                @pl.when((code & 1) > 0)
                def _():
                    late = summed((a, b), blocks - 1)
                    for at in [slice(c, c + piece) for c in range(0, width, piece)]:
                        put(
                            at,
                            jnp.dot(mine, rows_refs[k][:, at], preferred_element_type=jnp.float32)
                            + jnp.dot(late, last_ref[:, at], preferred_element_type=jnp.float32),
                        )

        if not copies or parts == 1:
            fill(outs)
        else:
            for part in range(parts):

                @pl.when(step == part)
                def _():
                    fill(outs[part:] if part == parts - 1 else outs[part : part + 1])

    def rows_spec(k):
        return pl.BlockSpec((BLOCK, width), lambda r, at: (block_at(at[first + r * OWN + k]), 0))

    shape = (OWN, rank, width)
    if copies:
        outs = [(shape, features.dtype, constant_spec(shape))] * (parts - 1 + copies)
    else:
        outs = [((parts * OWN, rank, width), features.dtype, pl.BlockSpec(shape, lambda r, *_: (r, 0, 0)))]
    return call(
        kernel,
        (codes,),
        (parts,),
        [whole(array) for array in ranks]
        + [(features, rows_spec(k)) for k in range(OWN)]
        + [(features, pl.BlockSpec((BLOCK, width), lambda r, *_: (blocks - 1, 0), pipeline_mode=pl.Buffered(1)))],
        outs,
        tokens,
        us,
    )


def outputs_of(lengths, codes, parts, base, ranks, features, maps, last_map):
    rows, width = base[0].shape
    blocks = rows // BLOCK
    rank = maps.shape[1]

    def kernel(lengths_ref, codes_ref, one, two, three, *refs):
        terms, refs = refs[: len(ranks)], refs[len(ranks) :]
        rows_ref, maps_ref, last_ref, out_ref, *outs = refs
        late = summed(terms, blocks - 1)
        for k in range(blocks):
            at = slice(k * BLOCK, (k + 1) * BLOCK)
            adapter = maps_ref[k] if k < blocks - 1 else last_ref[0]
            added = lax.dot_general(
                summed(terms, k) if k < blocks - 1 else late,
                adapter,
                (((0,), (0,)), ((), ())),
                preferred_element_type=jnp.float32,
            )
            frozen = one[at].astype(jnp.float32) + two[at].astype(jnp.float32) + three[at].astype(jnp.float32)
            live = lax.broadcasted_iota(jnp.int32, frozen.shape, 0) < lengths_ref[k]
            values = jnp.where(live, frozen + ADAPTER_SCALE * added, 0.0).astype(out_ref.dtype)
            out_ref[at] = values
            if k == blocks - 1:
                for count, out in zip(parts, outs):
                    out[count * rank :] = values
        late_rows = jnp.dot(late, rows_ref[(blocks - 1) * BLOCK :], preferred_element_type=jnp.float32)
        done = 0
        for count, out in zip(parts, outs):

            def one_row(r, carry, out=out, done=done):
                code = codes_ref[done + r]
                at = jnp.maximum((code >> 1) - 1, 0)
                mine = summed(terms, at)
                mine = jnp.where(code > 1, mine, jnp.zeros_like(mine))
                mine_rows = rows_ref[pl.ds(pl.multiple_of(at * BLOCK, BLOCK), BLOCK), :]
                total = jnp.dot(mine, mine_rows, preferred_element_type=jnp.float32)
                total = total + jnp.where((code & 1) > 0, late_rows, 0.0)
                to = r * rank if isinstance(r, int) else pl.ds(pl.multiple_of(r * rank, rank), rank)
                to = slice(to, to + rank) if isinstance(r, int) else to
                out[to] = (ADAPTER_SCALE * total).astype(out.dtype)
                return carry

            if count <= OWN:
                for r in range(count):
                    one_row(r, 0)
            else:
                lax.fori_loop(0, count, one_row, 0)
            done += count

    return call(
        kernel,
        (lengths, codes),
        (1,),
        [whole(array) for array in (*base, *ranks, features, maps, last_map)],
        [((rows, width), maps.dtype, constant_spec((rows, width)))]
        + [
            ((count * rank + BLOCK, width), maps.dtype, constant_spec((count * rank + BLOCK, width)))
            for count in parts
        ],
        vmem=60,
    )


def finish(pick, values, own, arrived, tokens):
    width = values.shape[1]
    block = values.shape[0] // BLOCK - 1
    rows = own.shape[0] - BLOCK

    def kernel(pick_ref, *refs):
        choices, table_ref, last_ref = refs[:-3], refs[-2], refs[-1]
        table_ref[...] = sum(choice[:rows].astype(jnp.float32) for choice in choices).astype(own.dtype)
        for k, choice in enumerate(choices):

            @pl.when(pick_ref[0] == k)
            def _():
                last_ref[...] = choice[rows:]

    return call(
        kernel,
        (pick,),
        (1,),
        [whole(choice) for choice in (own, *arrived)] + [(values, ANYWHERE)],
        [
            ((rows, width), own.dtype, constant_spec((rows, width))),
            (values.shape, values.dtype, pl.BlockSpec((BLOCK, width), lambda i, *_: (block, 0))),
        ],
        tokens,
        aliases={2 + len(arrived): 1},
    )


def base_terms(columns, hidden, weight, tokens=()):
    rows, depth = hidden.shape
    width = weight.shape[1] // 4
    tile = rows // 4

    def kernel(columns_ref, rows_ref, *refs):
        for k in range(4):
            out_ref = refs[4 + k]
            out_ref[...] = jnp.dot(rows_ref[...], refs[k][...], preferred_element_type=jnp.float32).astype(out_ref.dtype)

    def column(k):
        return pl.BlockSpec((depth, width), lambda i, at: (0, at[k]), pipeline_mode=pl.Buffered(1))

    return call(
        kernel,
        (columns,),
        (rows // tile,),
        [(hidden, pl.BlockSpec((tile, depth), lambda i, *_: (i, 0)))]
        + [(weight, column(k)) for k in range(4)],
        [((rows, width), hidden.dtype, pl.BlockSpec((tile, width), lambda i, *_: (i, 0)))] * 4,
        tokens,
        100.0,
    )


def shift(array, by):
    size = lax.axis_size("dp")
    return lax.ppermute(array, "dp", [(i, (i + by) % size) for i in range(size)])


def shifted(array, source):
    size = lax.axis_size("dp")
    me = lax.axis_index("dp")
    if size > 4:
        taken = lax.dynamic_index_in_dim(lax.all_gather(array, "dp"), source, 0, keepdims=False)
        return [taken], jnp.zeros((1,), jnp.int32)
    choices = [array] + [shift(array, by) for by in range(1, size)]
    return choices, ((me - source) % size).reshape(1)


def add(*arrays):
    return sum(array.astype(jnp.float32) for array in arrays).astype(arrays[0].dtype)


def crossed(array, by):
    return lax.ppermute(array, "tensor", [(i, i ^ by) for i in range(lax.axis_size("tensor"))])


def near(array):
    return crossed(array, 1)


def far(array):
    return crossed(array, 2)


def exchanged(array):
    array = add(array, near(array))
    return array, far(array)


def spread(array):
    return [array] + [crossed(array, by) for by in range(1, lax.axis_size("tensor"))]


def line_reduce_scatter(table):
    size = lax.axis_size("dp")
    me = lax.axis_index("dp")

    def entry(index):
        return lax.dynamic_index_in_dim(table, jnp.clip(index, 0, size - 1), 0, keepdims=False)

    from_left = from_right = None
    for step in range(size - 1):
        right = entry(size - 1 - step + me)
        left = entry(step - (size - 1 - me))
        if step > 0:
            right = add(right, from_left)
            left = add(left, from_right)
        from_left = lax.ppermute(right, "dp", [(i, i + 1) for i in range(step + 1)])
        from_right = lax.ppermute(left, "dp", [(i, i - 1) for i in range(size - 1 - step, size)])
    return entry(me) if size == 1 else add(entry(me), from_left, from_right)


ROLES = ((3, 2, 1, 0), (0, 3, 2, 1), (3, 0, 1, 2), (0, 1, 2, 3))


def body(
    partner,
    block_tenant_index,
    block_live_length,
    tenant_table_row,
    hidden,
    cotangent,
    frozen_value_weight,
    adapter_down_rows,
    adapter_up_matrix,
):
    blocks = block_tenant_index.shape[0]
    kept = blocks - SW
    devices = lax.axis_size("dp")
    me = lax.axis_index("dp")
    column = lax.axis_index("tensor")
    lengths = block_live_length
    line = devices == 4
    order = jnp.arange(devices, dtype=jnp.int32)
    holder = jnp.sum(jnp.where(partner == me, order, 0))

    up_own = adapter_up_matrix[kept:]
    cot_terms, down_own = kept_ranks(lengths, adapter_up_matrix, cotangent, adapter_down_rows, [up_own])
    up_choices, _ = shifted(up_own, holder)
    cot_terms, up_last = with_last_rank(lengths, partner, me, up_choices, cotangent, cot_terms)
    rank_cot = exchanged(cot_terms)
    down_own = after(down_own, rank_cot[0])

    table_rows = jnp.sum(
        jnp.where(
            block_tenant_index[:, None] == jnp.arange(tenant_table_row.shape[0], dtype=jnp.int32)[None, :],
            tenant_table_row[None, :],
            0,
        ),
        axis=1,
    )
    weights = jnp.where(jnp.arange(blocks) < kept, 2 * (jnp.arange(blocks, dtype=jnp.int32) + 1), 1)

    def codes_of(owners):
        rows = (owners[:, None] * OWN + jnp.arange(OWN, dtype=jnp.int32)[None, :]).reshape(-1)
        return jnp.sum(jnp.where(rows[:, None] == table_rows[None, :], weights[None, :], 0), axis=1)

    columns = jnp.stack([column ^ 3, column ^ 2, column ^ 1, column]).astype(jnp.int32)

    def base(*tokens):
        return base_terms(columns, hidden, frozen_value_weight, tokens)

    def base_parts(terms, *tokens):
        sent, away, given, mine = terms
        away = add(after(away, *tokens), near(sent))
        return (mine, near(given), far(away)), away

    def inputs(down_choices, *tokens):
        return spread(
            streamed_ranks(lengths, partner, me, adapter_down_rows, down_choices, hidden, 4, tokens, 100.0)
        )

    def outputs(codes, parts, base_sums, rank_in):
        return outputs_of(
            lengths, codes, parts, base_sums, rank_in, cotangent, adapter_up_matrix, up_last
        )

    if line:
        inner = (me == 1) | (me == 2)
        codes = codes_of(jnp.array(ROLES, jnp.int32)[me])
        (first,) = down_rows(codes, 0, 1, 1, rank_cot, hidden)
        from_first = lax.ppermute(first, "dp", [(0, 1), (3, 2), (1, 0), (2, 3)])
        from_left = lax.ppermute(down_own, "dp", [(0, 1), (1, 2), (2, 3)])
        from_right = lax.ppermute(down_own, "dp", [(3, 2), (2, 1), (1, 0)])
        passed, outward = passed_on(partner, me, down_own, from_left, from_right, [first])
        terms = base(first, passed)
        passed = lax.ppermute(passed, "dp", [(1, 2), (2, 1)])
        outward = lax.ppermute(outward, "dp", [(1, 3), (2, 0)])
        down_choices = [down_own, from_left, from_right, passed, outward]
        second, third, own = down_rows(codes, OWN, 3, 1, rank_cot, hidden, [terms[0], passed, outward], 100.0)
        second = add(second, jnp.where(inner, from_first, jnp.zeros((), first.dtype)))
        from_second = lax.ppermute(second, "dp", [(0, 1), (3, 2), (1, 3), (2, 0)])
        base_sums, away = base_parts(terms, second)
        rank_in = inputs(down_choices, away)
        third = add(after(third, rank_in[0]), jnp.where(inner, from_second, jnp.zeros((), first.dtype)))
        from_inner = lax.ppermute(third, "dp", [(1, 2), (2, 1)])
        from_third = lax.ppermute(third, "dp", [(0, 1), (3, 2)])
        near_total = lax.optimization_barrier(
            after(own, third).astype(jnp.float32)
            + jnp.where(inner, 0.0, from_first.astype(jnp.float32) + from_second.astype(jnp.float32))
        )
        down_out = (near_total + from_inner.astype(jnp.float32) + from_third.astype(jnp.float32)).astype(own.dtype)

        up_codes = codes_of((me + jnp.array([1, 2, 3, 0], jnp.int32)) % devices)
        values, *sent, kept_here = outputs(up_codes, [OWN] * 4, base_sums, rank_in)
        arrived = [shift(array, by + 1) for by, array in enumerate(sent)]
        value_pick = ((me - partner[me]) % devices).reshape(1)
        up_out, values = finish(value_pick, values, kept_here, arrived, [down_out])
    else:
        codes = codes_of(order)
        (table,) = down_rows(codes, 0, devices, 0, rank_cot, hidden)
        down_choices, _ = shifted(down_own, holder)
        down_out = line_reduce_scatter(table.reshape(devices, OWN, *table.shape[1:]))
        values, table = outputs(codes, [devices * OWN], base_parts(base(table))[0], inputs(down_choices, table))
        up_table, last_values = table[:-BLOCK], table[-BLOCK:]
        up_out = line_reduce_scatter(up_table.reshape(devices, OWN, -1, values.shape[1]))
        (last_values,), _ = shifted(last_values, partner[me])
        values = jnp.concatenate([values[: kept * BLOCK], last_values], axis=0)
    return (values, down_out, up_out.reshape(OWN, -1, values.shape[1]))


def solution(mesh):
    in_specs = (
        P("groups"),
        P(("groups", "dp")),
        P(("groups", "dp")),
        P("groups"),
        P(("groups", "dp"), "tensor"),
        P(("groups", "dp"), "tensor"),
        P("tensor", None),
        P(("groups", "dp"), None, "tensor"),
        P(("groups", "dp"), None, "tensor"),
    )
    out_specs = (
        P(("groups", "dp"), "tensor"),
        P(("groups", "dp"), None, "tensor"),
        P(("groups", "dp"), None, "tensor"),
    )
    return jax.shard_map(body, mesh=mesh, in_specs=in_specs, out_specs=out_specs, check_vma=False)
```

```python
import jax
import jax.numpy as jnp
from jax import lax
from jax.experimental import pallas as pl
from jax.experimental.pallas import tpu as pltpu
from jax.sharding import PartitionSpec as P

BLOCK = 128
SW = 1
OWN = 4


ADAPTER_SCALE = 0.5

ANYWHERE = pl.BlockSpec(memory_space=pl.ANY)
ROW_PRODUCT = (((1,), (1,)), ((), ()))


def call(kernel, scalars, grid, inputs, outputs, tokens=(), us=1.0, scratch=(), aliases=None, vmem=16):
    def run(*refs):
        cut = len(scalars) + len(inputs)
        return kernel(*refs[:cut], *refs[cut + len(tokens) :])

    return pl.pallas_call(
        run,
        grid_spec=pltpu.PrefetchScalarGridSpec(
            num_scalar_prefetch=len(scalars),
            grid=grid,
            in_specs=[spec for _, spec in inputs] + [ANYWHERE] * len(tokens),
            out_specs=[spec for _, _, spec in outputs],
            scratch_shapes=scratch,
        ),
        out_shape=[jax.ShapeDtypeStruct(shape, kind) for shape, kind, _ in outputs],
        input_output_aliases=aliases or {},
        compiler_params=pltpu.CompilerParams(vmem_limit_bytes=vmem * 1024 * 1024),
        cost_estimate=pl.CostEstimate(flops=int(us * 1e9), bytes_accessed=int(us * 3.6e5), transcendentals=0),
    )(*scalars, *[array for array, _ in inputs], *tokens)


def constant_spec(shape):
    return pl.BlockSpec(shape, lambda *_: (0,) * len(shape), pipeline_mode=pl.Buffered(1))


def whole(array):
    return (array, constant_spec(array.shape))


def nothing(*refs):
    pass


def after(array, *tokens):
    return call(
        nothing, (), (1,), [(array, ANYWHERE)], [(array.shape, array.dtype, ANYWHERE)], tokens, 0.1, aliases={0: 0}
    )[0]


def masked_rank(adapter, rows, length):
    ranks = lax.dot_general(adapter, rows, ROW_PRODUCT, preferred_element_type=jnp.float32)
    live = lax.broadcasted_iota(jnp.int32, ranks.shape, 1) < length
    return jnp.where(live, ranks, 0.0).astype(rows.dtype)


def kept_ranks(lengths, maps, features, others):
    blocks, rank, width = maps.shape
    kept = blocks - SW
    last_shapes = [(SW, rank, width), (SW, *others.shape[1:])]

    def kernel(lengths_ref, maps_ref, rows_ref, others_ref, out_ref, last_ref, last_other):
        last_ref[...] = maps_ref[kept:]
        last_other[...] = others_ref[...]
        for k in range(kept):
            out_ref[k] = masked_rank(maps_ref[k], rows_ref[k * BLOCK : (k + 1) * BLOCK], lengths_ref[k])

    return call(
        kernel,
        (lengths,),
        (1,),
        [
            whole(maps),
            (features, pl.BlockSpec((kept * BLOCK, width), lambda i, *_: (0, 0), pipeline_mode=pl.Buffered(1))),
            (others, pl.BlockSpec(last_shapes[1], lambda i, *_: (kept, 0, 0), pipeline_mode=pl.Buffered(1))),
        ],
        [((blocks, rank, BLOCK), features.dtype, pl.BlockSpec((kept, rank, BLOCK), lambda i, *_: (0, 0, 0)))]
        + [(shape, features.dtype, constant_spec(shape)) for shape in last_shapes],
        vmem=60,
    )


def passed_on(partner, me, own, from_left, from_right, tokens):
    shape = own.shape

    def kernel(partner_ref, me_ref, own_ref, left_ref, right_ref, inner_ref, outer_ref):
        left = me_ref[0] == 1

        @pl.when(left)
        def _():
            inner_ref[...] = left_ref[...]
            outer_ref[...] = left_ref[...]

        @pl.when(jnp.logical_not(left))
        def _():
            inner_ref[...] = right_ref[...]
            outer_ref[...] = right_ref[...]

        @pl.when(partner_ref[me_ref[0]] == jnp.where(left, 3, 0))
        def _():
            outer_ref[...] = own_ref[...]

    return call(
        kernel,
        (partner, me.reshape(1)),
        (1,),
        [whole(array) for array in (own, from_left, from_right)],
        [(shape, own.dtype, constant_spec(shape))] * 2,
        tokens,
        1.0,
    )


def with_last_rank(lengths, partner, me, choices, features, ranks):
    shape = choices[0].shape
    block = ranks.shape[0] - 1
    size = partner.shape[0]

    def kernel(lengths_ref, partner_ref, me_ref, *refs):
        rows_ref, _, out_ref, chosen_ref = refs[-4:]
        for k, choice in enumerate(refs[:-4]):
            if len(choices) == 1:
                chosen_ref[...] = choice[...]
                continue

            @pl.when(partner_ref[lax.rem(me_ref[0] + (size - k), size)] == me_ref[0])
            def _():
                chosen_ref[...] = choice[...]

        out_ref[0] = masked_rank(chosen_ref[0], rows_ref[...], lengths_ref[block])

    return call(
        kernel,
        (lengths, partner, me.reshape(1)),
        (1,),
        [whole(choice) for choice in choices]
        + [(features, pl.BlockSpec((BLOCK, shape[2]), lambda i, *_: (block, 0), pipeline_mode=pl.Buffered(1)))]
        + [(ranks, ANYWHERE)],
        [
            (ranks.shape, ranks.dtype, pl.BlockSpec((1, *ranks.shape[1:]), lambda i, *_: (block, 0, 0))),
            (shape, features.dtype, constant_spec(shape)),
        ],
        aliases={4 + len(choices): 0},
    )


def streamed_ranks(lengths, partner, me, maps, choices, features, each, tokens=(), us=1.0):
    blocks, rank, width = maps.shape
    steps = pl.cdiv(blocks, each)
    end = blocks - 1 - (steps - 1) * each

    def picked(partner_ref, at):
        if len(choices) == 1:
            return [at == at]
        held = [
            partner_ref[at] == at,
            (partner_ref[jnp.maximum(at - 1, 0)] == at) & (at > 0),
            (partner_ref[jnp.minimum(at + 1, 3)] == at) & (at < 3),
        ]
        other = jnp.logical_not(held[0] | held[1] | held[2])
        inner = (at == 1) | (at == 2)
        return [*held, other & inner, other & jnp.logical_not(inner)]

    def kernel(lengths_ref, partner_ref, me_ref, *refs):
        maps_refs, rows_refs, choices_refs, out_ref = refs[:each], refs[each : 2 * each], refs[2 * each : -1], refs[-1]
        step = pl.program_id(0)

        def one(k):
            block = step * each + k
            out_ref[block] = masked_rank(maps_refs[k][0], rows_refs[k][...], lengths_ref[block])

        @pl.when(step < steps - 1)
        def _():
            for k in range(each):
                one(k)

        @pl.when(step == steps - 1)
        def _():
            for k in range(end):
                one(k)
            for choice, use in zip(choices_refs, picked(partner_ref, me_ref[0])):

                @pl.when(use)
                def _():
                    out_ref[blocks - 1] = masked_rank(choice[0], rows_refs[end][...], lengths_ref[blocks - 1])

    def at(i, k):
        block = i * each + k
        return jnp.where(block < blocks, block, block - each)

    return call(
        kernel,
        (lengths, partner, me.reshape(1)),
        (steps,),
        [(maps, pl.BlockSpec((1, rank, width), lambda i, *_, k=k: (at(i, k), 0, 0))) for k in range(each)]
        + [(features, pl.BlockSpec((BLOCK, width), lambda i, *_, k=k: (at(i, k), 0))) for k in range(each)]
        + [whole(choice) for choice in choices],
        [((blocks, rank, BLOCK), features.dtype, constant_spec((blocks, rank, BLOCK)))],
        tokens,
        us,
    )[0]


def summed(terms, at):
    return sum(term[at].astype(jnp.float32) for term in terms).astype(terms[0].dtype)


def down_rows(codes, first, parts, copies, ranks, features, tokens=(), us=1.0):
    blocks, rank, _ = ranks[0].shape
    width = features.shape[1]
    piece = min(width, 512)

    def block_at(code):
        return jnp.maximum((code >> 1) - 1, 0)

    def kernel(codes_ref, a, b, *refs):
        rows_refs, last_ref, outs = refs[:OWN], refs[OWN], refs[OWN + 1 :]
        step = pl.program_id(0)

        def fill(to):
            for k in range(OWN):
                code = codes_ref[first + step * OWN + k]
                mine = summed((a, b), block_at(code))
                mine = jnp.where(code > 1, mine, jnp.zeros_like(mine))

                def put(at, total):
                    value = (ADAPTER_SCALE * total).astype(features.dtype)
                    for out_ref in to:
                        out_ref[k, :, at] = value

                for at in [slice(c, c + piece) for c in range(0, width, piece)]:
                    put(at, jnp.dot(mine, rows_refs[k][:, at], preferred_element_type=jnp.float32))

                @pl.when((code & 1) > 0)
                def _():
                    late = summed((a, b), blocks - 1)
                    for at in [slice(c, c + piece) for c in range(0, width, piece)]:
                        put(
                            at,
                            jnp.dot(mine, rows_refs[k][:, at], preferred_element_type=jnp.float32)
                            + jnp.dot(late, last_ref[:, at], preferred_element_type=jnp.float32),
                        )

        if not copies or parts == 1:
            fill(outs)
        else:
            for part in range(parts):

                @pl.when(step == part)
                def _():
                    fill(outs[part:] if part == parts - 1 else outs[part : part + 1])

    def rows_spec(k):
        return pl.BlockSpec((BLOCK, width), lambda r, at: (block_at(at[first + r * OWN + k]), 0))

    shape = (OWN, rank, width)
    if copies:
        outs = [(shape, features.dtype, constant_spec(shape))] * (parts - 1 + copies)
    else:
        outs = [((parts * OWN, rank, width), features.dtype, pl.BlockSpec(shape, lambda r, *_: (r, 0, 0)))]
    return call(
        kernel,
        (codes,),
        (parts,),
        [whole(array) for array in ranks]
        + [(features, rows_spec(k)) for k in range(OWN)]
        + [(features, pl.BlockSpec((BLOCK, width), lambda r, *_: (blocks - 1, 0), pipeline_mode=pl.Buffered(1)))],
        outs,
        tokens,
        us,
    )


def outputs_of(lengths, codes, parts, base, ranks, features, maps, last_map):
    rows, width = base[0].shape
    blocks = rows // BLOCK
    rank = maps.shape[1]

    def kernel(lengths_ref, codes_ref, one, two, three, *refs):
        terms, refs = refs[: len(ranks)], refs[len(ranks) :]
        rows_ref, maps_ref, last_ref, out_ref, *outs = refs
        late = summed(terms, blocks - 1)
        for k in range(blocks):
            at = slice(k * BLOCK, (k + 1) * BLOCK)
            adapter = maps_ref[k] if k < blocks - 1 else last_ref[0]
            added = lax.dot_general(
                summed(terms, k) if k < blocks - 1 else late,
                adapter,
                (((0,), (0,)), ((), ())),
                preferred_element_type=jnp.float32,
            )
            frozen = one[at].astype(jnp.float32) + two[at].astype(jnp.float32) + three[at].astype(jnp.float32)
            live = lax.broadcasted_iota(jnp.int32, frozen.shape, 0) < lengths_ref[k]
            values = jnp.where(live, frozen + ADAPTER_SCALE * added, 0.0).astype(out_ref.dtype)
            out_ref[at] = values
            if k == blocks - 1:
                for count, out in zip(parts, outs):
                    out[count * rank :] = values
        late_rows = jnp.dot(late, rows_ref[(blocks - 1) * BLOCK :], preferred_element_type=jnp.float32)
        done = 0
        for count, out in zip(parts, outs):

            def one_row(r, carry, out=out, done=done):
                code = codes_ref[done + r]
                at = jnp.maximum((code >> 1) - 1, 0)
                mine = summed(terms, at)
                mine = jnp.where(code > 1, mine, jnp.zeros_like(mine))
                mine_rows = rows_ref[pl.ds(pl.multiple_of(at * BLOCK, BLOCK), BLOCK), :]
                total = jnp.dot(mine, mine_rows, preferred_element_type=jnp.float32)
                total = total + jnp.where((code & 1) > 0, late_rows, 0.0)
                to = r * rank if isinstance(r, int) else pl.ds(pl.multiple_of(r * rank, rank), rank)
                to = slice(to, to + rank) if isinstance(r, int) else to
                out[to] = (ADAPTER_SCALE * total).astype(out.dtype)
                return carry

            if count <= OWN:
                for r in range(count):
                    one_row(r, 0)
            else:
                lax.fori_loop(0, count, one_row, 0)
            done += count

    return call(
        kernel,
        (lengths, codes),
        (1,),
        [whole(array) for array in (*base, *ranks, features, maps, last_map)],
        [((rows, width), maps.dtype, constant_spec((rows, width)))]
        + [
            ((count * rank + BLOCK, width), maps.dtype, constant_spec((count * rank + BLOCK, width)))
            for count in parts
        ],
        vmem=60,
    )


def finish(pick, values, own, arrived, tokens):
    width = values.shape[1]
    block = values.shape[0] // BLOCK - 1
    rows = own.shape[0] - BLOCK

    def kernel(pick_ref, *refs):
        choices, table_ref, last_ref = refs[:-3], refs[-2], refs[-1]
        table_ref[...] = sum(choice[:rows].astype(jnp.float32) for choice in choices).astype(own.dtype)
        for k, choice in enumerate(choices):

            @pl.when(pick_ref[0] == k)
            def _():
                last_ref[...] = choice[rows:]

    return call(
        kernel,
        (pick,),
        (1,),
        [whole(choice) for choice in (own, *arrived)] + [(values, ANYWHERE)],
        [
            ((rows, width), own.dtype, constant_spec((rows, width))),
            (values.shape, values.dtype, pl.BlockSpec((BLOCK, width), lambda i, *_: (block, 0))),
        ],
        tokens,
        aliases={2 + len(arrived): 1},
    )


def base_terms(columns, hidden, weight, tokens=()):
    rows, depth = hidden.shape
    width = weight.shape[1] // 4
    tile = rows // 4

    def kernel(columns_ref, rows_ref, *refs):
        for k in range(4):
            out_ref = refs[4 + k]
            out_ref[...] = jnp.dot(rows_ref[...], refs[k][...], preferred_element_type=jnp.float32).astype(out_ref.dtype)

    def column(k):
        return pl.BlockSpec((depth, width), lambda i, at: (0, at[k]), pipeline_mode=pl.Buffered(1))

    return call(
        kernel,
        (columns,),
        (rows // tile,),
        [(hidden, pl.BlockSpec((tile, depth), lambda i, *_: (i, 0)))]
        + [(weight, column(k)) for k in range(4)],
        [((rows, width), hidden.dtype, pl.BlockSpec((tile, width), lambda i, *_: (i, 0)))] * 4,
        tokens,
        100.0,
    )


def shift(array, by):
    size = lax.axis_size("dp")
    return lax.ppermute(array, "dp", [(i, (i + by) % size) for i in range(size)])


def shifted(array, source):
    size = lax.axis_size("dp")
    me = lax.axis_index("dp")
    if size > 4:
        taken = lax.dynamic_index_in_dim(lax.all_gather(array, "dp"), source, 0, keepdims=False)
        return [taken], jnp.zeros((1,), jnp.int32)
    choices = [array] + [shift(array, by) for by in range(1, size)]
    return choices, ((me - source) % size).reshape(1)


def add(*arrays):
    return sum(array.astype(jnp.float32) for array in arrays).astype(arrays[0].dtype)


def crossed(array, by):
    return lax.ppermute(array, "tensor", [(i, i ^ by) for i in range(lax.axis_size("tensor"))])


def near(array):
    return crossed(array, 1)


def far(array):
    return crossed(array, 2)


def exchanged(array):
    array = add(array, near(array))
    return array, far(array)


def spread(array):
    return [array] + [crossed(array, by) for by in range(1, lax.axis_size("tensor"))]


def line_reduce_scatter(table):
    size = lax.axis_size("dp")
    me = lax.axis_index("dp")

    def entry(index):
        return lax.dynamic_index_in_dim(table, jnp.clip(index, 0, size - 1), 0, keepdims=False)

    from_left = from_right = None
    for step in range(size - 1):
        right = entry(size - 1 - step + me)
        left = entry(step - (size - 1 - me))
        if step > 0:
            right = add(right, from_left)
            left = add(left, from_right)
        from_left = lax.ppermute(right, "dp", [(i, i + 1) for i in range(step + 1)])
        from_right = lax.ppermute(left, "dp", [(i, i - 1) for i in range(size - 1 - step, size)])
    return entry(me) if size == 1 else add(entry(me), from_left, from_right)


ROLES = ((3, 2, 1, 0), (2, 3, 0, 1), (1, 0, 3, 2), (0, 1, 2, 3))


def body(
    partner,
    block_tenant_index,
    block_live_length,
    tenant_table_row,
    hidden,
    cotangent,
    frozen_value_weight,
    adapter_down_rows,
    adapter_up_matrix,
):
    blocks = block_tenant_index.shape[0]
    kept = blocks - SW
    devices = lax.axis_size("dp")
    me = lax.axis_index("dp")
    column = lax.axis_index("tensor")
    lengths = block_live_length
    line = devices == 4
    order = jnp.arange(devices, dtype=jnp.int32)
    holder = jnp.sum(jnp.where(partner == me, order, 0))

    cot_terms, up_own, down_own = kept_ranks(lengths, adapter_up_matrix, cotangent, adapter_down_rows)
    up_choices, _ = shifted(up_own, holder)
    cot_terms, up_last = with_last_rank(lengths, partner, me, up_choices, cotangent, cot_terms)
    rank_cot = exchanged(cot_terms)
    down_own = after(down_own, rank_cot[0])

    table_rows = jnp.sum(
        jnp.where(
            block_tenant_index[:, None] == jnp.arange(tenant_table_row.shape[0], dtype=jnp.int32)[None, :],
            tenant_table_row[None, :],
            0,
        ),
        axis=1,
    )
    weights = jnp.where(jnp.arange(blocks) < kept, 2 * (jnp.arange(blocks, dtype=jnp.int32) + 1), 1)

    def codes_of(owners):
        rows = (owners[:, None] * OWN + jnp.arange(OWN, dtype=jnp.int32)[None, :]).reshape(-1)
        return jnp.sum(jnp.where(rows[:, None] == table_rows[None, :], weights[None, :], 0), axis=1)

    columns = jnp.stack([column ^ 3, column ^ 2, column ^ 1, column]).astype(jnp.int32)

    def base(*tokens):
        return base_terms(columns, hidden, frozen_value_weight, tokens)

    def base_parts(terms, *tokens):
        sent, away, given, mine = terms
        away = add(after(away, *tokens), near(sent))
        return (mine, near(given), far(away)), away

    def inputs(down_choices, *tokens):
        return spread(
            streamed_ranks(lengths, partner, me, adapter_down_rows, down_choices, hidden, 4, tokens, 100.0)
        )

    def outputs(codes, parts, base_sums, rank_in):
        return outputs_of(
            lengths, codes, parts, base_sums, rank_in, cotangent, adapter_up_matrix, up_last
        )

    if line:
        inner = (me == 1) | (me == 2)
        codes = codes_of(jnp.array(ROLES, jnp.int32)[me])
        (first,) = down_rows(codes, 0, 1, 1, rank_cot, hidden)
        from_end = lax.ppermute(first, "dp", [(0, 1), (3, 2)])
        from_left = lax.ppermute(down_own, "dp", [(0, 1), (1, 2), (2, 3)])
        from_right = lax.ppermute(down_own, "dp", [(3, 2), (2, 1), (1, 0)])
        passed, outward = passed_on(partner, me, down_own, from_left, from_right, [first])
        terms = base(first, passed)
        passed = lax.ppermute(passed, "dp", [(1, 2), (2, 1)])
        outward = lax.ppermute(outward, "dp", [(1, 3), (2, 0)])
        down_choices = [down_own, from_left, from_right, passed, outward]
        second, third, own = down_rows(codes, OWN, 3, 1, rank_cot, hidden, [terms[0], passed, outward], 100.0)
        second = add(second, jnp.where(inner, from_end, jnp.zeros((), first.dtype)))
        from_second = lax.ppermute(second, "dp", [(0, 1), (3, 2), (1, 3), (2, 0)])
        rank_in = inputs(down_choices, second)
        base_sums, _ = base_parts(terms, rank_in[0])
        middle = add(after(first, *rank_in[1:]), from_second)
        from_inner = lax.ppermute(middle, "dp", [(1, 2), (2, 1)])
        from_third = lax.ppermute(after(third, middle), "dp", [(0, 1), (3, 2), (1, 0), (2, 3)])
        near_total = lax.optimization_barrier(
            after(own, middle).astype(jnp.float32) + jnp.where(inner, 0.0, from_second.astype(jnp.float32))
        )
        down_out = (near_total + from_inner.astype(jnp.float32) + from_third.astype(jnp.float32)).astype(own.dtype)

        up_codes = codes_of((me + jnp.array([1, 2, 3, 0], jnp.int32)) % devices)
        values, *sent, kept_here = outputs(up_codes, [OWN] * 4, base_sums, rank_in)
        arrived = [shift(array, by + 1) for by, array in enumerate(sent)]
        value_pick = ((me - partner[me]) % devices).reshape(1)
        up_out, values = finish(value_pick, values, kept_here, arrived, [down_out])
    else:
        codes = codes_of(order)
        (table,) = down_rows(codes, 0, devices, 0, rank_cot, hidden)
        down_choices, _ = shifted(down_own, holder)
        down_out = line_reduce_scatter(table.reshape(devices, OWN, *table.shape[1:]))
        values, table = outputs(codes, [devices * OWN], base_parts(base(table))[0], inputs(down_choices, table))
        up_table, last_values = table[:-BLOCK], table[-BLOCK:]
        up_out = line_reduce_scatter(up_table.reshape(devices, OWN, -1, values.shape[1]))
        (last_values,), _ = shifted(last_values, partner[me])
        values = jnp.concatenate([values[: kept * BLOCK], last_values], axis=0)
    return (values, down_out, up_out.reshape(OWN, -1, values.shape[1]))


def solution(mesh):
    in_specs = (
        P("groups"),
        P(("groups", "dp")),
        P(("groups", "dp")),
        P("groups"),
        P(("groups", "dp"), "tensor"),
        P(("groups", "dp"), "tensor"),
        P("tensor", None),
        P(("groups", "dp"), None, "tensor"),
        P(("groups", "dp"), None, "tensor"),
    )
    out_specs = (
        P(("groups", "dp"), "tensor"),
        P(("groups", "dp"), None, "tensor"),
        P(("groups", "dp"), None, "tensor"),
    )
    return jax.shard_map(body, mesh=mesh, in_specs=in_specs, out_specs=out_specs, check_vma=False)
```

```python
import jax
import jax.numpy as jnp
from jax import lax
from jax.experimental import pallas as pl
from jax.experimental.pallas import tpu as pltpu
from jax.sharding import PartitionSpec as P

BLOCK = 128
SW = 1
OWN = 4


ADAPTER_SCALE = 0.5

ANYWHERE = pl.BlockSpec(memory_space=pl.ANY)
ROW_PRODUCT = (((1,), (1,)), ((), ()))


def call(kernel, scalars, grid, inputs, outputs, tokens=(), us=1.0, scratch=(), aliases=None, vmem=16):
    def run(*refs):
        cut = len(scalars) + len(inputs)
        return kernel(*refs[:cut], *refs[cut + len(tokens) :])

    return pl.pallas_call(
        run,
        grid_spec=pltpu.PrefetchScalarGridSpec(
            num_scalar_prefetch=len(scalars),
            grid=grid,
            in_specs=[spec for _, spec in inputs] + [ANYWHERE] * len(tokens),
            out_specs=[spec for _, _, spec in outputs],
            scratch_shapes=scratch,
        ),
        out_shape=[jax.ShapeDtypeStruct(shape, kind) for shape, kind, _ in outputs],
        input_output_aliases=aliases or {},
        compiler_params=pltpu.CompilerParams(vmem_limit_bytes=vmem * 1024 * 1024),
        cost_estimate=pl.CostEstimate(flops=int(us * 1e9), bytes_accessed=int(us * 3.6e5), transcendentals=0),
    )(*scalars, *[array for array, _ in inputs], *tokens)


def constant_spec(shape):
    return pl.BlockSpec(shape, lambda *_: (0,) * len(shape), pipeline_mode=pl.Buffered(1))


def whole(array):
    return (array, constant_spec(array.shape))


def nothing(*refs):
    pass


def after(array, *tokens):
    return call(
        nothing, (), (1,), [(array, ANYWHERE)], [(array.shape, array.dtype, ANYWHERE)], tokens, 0.1, aliases={0: 0}
    )[0]


def masked_rank(adapter, rows, length):
    ranks = lax.dot_general(adapter, rows, ROW_PRODUCT, preferred_element_type=jnp.float32)
    live = lax.broadcasted_iota(jnp.int32, ranks.shape, 1) < length
    return jnp.where(live, ranks, 0.0).astype(rows.dtype)


def kept_ranks(lengths, maps, features, others):
    blocks, rank, width = maps.shape
    kept = blocks - SW
    last_shapes = [(SW, rank, width), (SW, *others.shape[1:])]

    def kernel(lengths_ref, maps_ref, rows_ref, others_ref, out_ref, last_ref, last_other):
        last_ref[...] = maps_ref[kept:]
        last_other[...] = others_ref[...]
        for k in range(kept):
            out_ref[k] = masked_rank(maps_ref[k], rows_ref[k * BLOCK : (k + 1) * BLOCK], lengths_ref[k])

    return call(
        kernel,
        (lengths,),
        (1,),
        [
            whole(maps),
            (features, pl.BlockSpec((kept * BLOCK, width), lambda i, *_: (0, 0), pipeline_mode=pl.Buffered(1))),
            (others, pl.BlockSpec(last_shapes[1], lambda i, *_: (kept, 0, 0), pipeline_mode=pl.Buffered(1))),
        ],
        [((blocks, rank, BLOCK), features.dtype, pl.BlockSpec((kept, rank, BLOCK), lambda i, *_: (0, 0, 0)))]
        + [(shape, features.dtype, constant_spec(shape)) for shape in last_shapes],
        vmem=60,
    )


def passed_on(partner, me, own, from_left, from_right, tokens):
    shape = own.shape

    def kernel(partner_ref, me_ref, own_ref, left_ref, right_ref, inner_ref, outer_ref):
        left = me_ref[0] == 1

        @pl.when(left)
        def _():
            inner_ref[...] = left_ref[...]
            outer_ref[...] = left_ref[...]

        @pl.when(jnp.logical_not(left))
        def _():
            inner_ref[...] = right_ref[...]
            outer_ref[...] = right_ref[...]

        @pl.when(partner_ref[me_ref[0]] == jnp.where(left, 3, 0))
        def _():
            outer_ref[...] = own_ref[...]

    return call(
        kernel,
        (partner, me.reshape(1)),
        (1,),
        [whole(array) for array in (own, from_left, from_right)],
        [(shape, own.dtype, constant_spec(shape))] * 2,
        tokens,
        1.0,
    )


def with_last_rank(lengths, partner, me, choices, features, ranks):
    shape = choices[0].shape
    block = ranks.shape[0] - 1
    size = partner.shape[0]

    def kernel(lengths_ref, partner_ref, me_ref, *refs):
        rows_ref, _, out_ref, chosen_ref = refs[-4:]
        for k, choice in enumerate(refs[:-4]):
            if len(choices) == 1:
                chosen_ref[...] = choice[...]
                continue

            @pl.when(partner_ref[lax.rem(me_ref[0] + (size - k), size)] == me_ref[0])
            def _():
                chosen_ref[...] = choice[...]

        out_ref[0] = masked_rank(chosen_ref[0], rows_ref[...], lengths_ref[block])

    return call(
        kernel,
        (lengths, partner, me.reshape(1)),
        (1,),
        [whole(choice) for choice in choices]
        + [(features, pl.BlockSpec((BLOCK, shape[2]), lambda i, *_: (block, 0), pipeline_mode=pl.Buffered(1)))]
        + [(ranks, ANYWHERE)],
        [
            (ranks.shape, ranks.dtype, pl.BlockSpec((1, *ranks.shape[1:]), lambda i, *_: (block, 0, 0))),
            (shape, features.dtype, constant_spec(shape)),
        ],
        aliases={4 + len(choices): 0},
    )


def streamed_ranks(lengths, partner, me, maps, choices, features, each, tokens=(), us=1.0):
    blocks, rank, width = maps.shape
    steps = pl.cdiv(blocks, each)
    end = blocks - 1 - (steps - 1) * each

    def picked(partner_ref, at):
        if len(choices) == 1:
            return [at == at]
        held = [
            partner_ref[at] == at,
            (partner_ref[jnp.maximum(at - 1, 0)] == at) & (at > 0),
            (partner_ref[jnp.minimum(at + 1, 3)] == at) & (at < 3),
        ]
        other = jnp.logical_not(held[0] | held[1] | held[2])
        inner = (at == 1) | (at == 2)
        return [*held, other & inner, other & jnp.logical_not(inner)]

    def kernel(lengths_ref, partner_ref, me_ref, *refs):
        maps_refs, rows_refs, choices_refs, out_ref = refs[:each], refs[each : 2 * each], refs[2 * each : -1], refs[-1]
        step = pl.program_id(0)

        def one(k):
            block = step * each + k
            out_ref[block] = masked_rank(maps_refs[k][0], rows_refs[k][...], lengths_ref[block])

        @pl.when(step < steps - 1)
        def _():
            for k in range(each):
                one(k)

        @pl.when(step == steps - 1)
        def _():
            for k in range(end):
                one(k)
            for choice, use in zip(choices_refs, picked(partner_ref, me_ref[0])):

                @pl.when(use)
                def _():
                    out_ref[blocks - 1] = masked_rank(choice[0], rows_refs[end][...], lengths_ref[blocks - 1])

    def at(i, k):
        block = i * each + k
        return jnp.where(block < blocks, block, block - each)

    return call(
        kernel,
        (lengths, partner, me.reshape(1)),
        (steps,),
        [(maps, pl.BlockSpec((1, rank, width), lambda i, *_, k=k: (at(i, k), 0, 0))) for k in range(each)]
        + [(features, pl.BlockSpec((BLOCK, width), lambda i, *_, k=k: (at(i, k), 0))) for k in range(each)]
        + [whole(choice) for choice in choices],
        [((blocks, rank, BLOCK), features.dtype, constant_spec((blocks, rank, BLOCK)))],
        tokens,
        us,
    )[0]


def summed(terms, at):
    return sum(term[at].astype(jnp.float32) for term in terms).astype(terms[0].dtype)


def down_rows(codes, first, parts, copies, ranks, features, tokens=(), us=1.0):
    blocks, rank, _ = ranks[0].shape
    width = features.shape[1]
    piece = min(width, 512)

    def block_at(code):
        return jnp.maximum((code >> 1) - 1, 0)

    def kernel(codes_ref, a, b, *refs):
        rows_refs, last_ref, outs = refs[:OWN], refs[OWN], refs[OWN + 1 :]
        step = pl.program_id(0)

        def fill(to):
            for k in range(OWN):
                code = codes_ref[first + step * OWN + k]
                mine = summed((a, b), block_at(code))
                mine = jnp.where(code > 1, mine, jnp.zeros_like(mine))

                def put(at, total):
                    value = (ADAPTER_SCALE * total).astype(features.dtype)
                    for out_ref in to:
                        out_ref[k, :, at] = value

                for at in [slice(c, c + piece) for c in range(0, width, piece)]:
                    put(at, jnp.dot(mine, rows_refs[k][:, at], preferred_element_type=jnp.float32))

                @pl.when((code & 1) > 0)
                def _():
                    late = summed((a, b), blocks - 1)
                    for at in [slice(c, c + piece) for c in range(0, width, piece)]:
                        put(
                            at,
                            jnp.dot(mine, rows_refs[k][:, at], preferred_element_type=jnp.float32)
                            + jnp.dot(late, last_ref[:, at], preferred_element_type=jnp.float32),
                        )

        if not copies or parts == 1:
            fill(outs)
        else:
            for part in range(parts):

                @pl.when(step == part)
                def _():
                    fill(outs[part:] if part == parts - 1 else outs[part : part + 1])

    def rows_spec(k):
        return pl.BlockSpec((BLOCK, width), lambda r, at: (block_at(at[first + r * OWN + k]), 0))

    shape = (OWN, rank, width)
    if copies:
        outs = [(shape, features.dtype, constant_spec(shape))] * (parts - 1 + copies)
    else:
        outs = [((parts * OWN, rank, width), features.dtype, pl.BlockSpec(shape, lambda r, *_: (r, 0, 0)))]
    return call(
        kernel,
        (codes,),
        (parts,),
        [whole(array) for array in ranks]
        + [(features, rows_spec(k)) for k in range(OWN)]
        + [(features, pl.BlockSpec((BLOCK, width), lambda r, *_: (blocks - 1, 0), pipeline_mode=pl.Buffered(1)))],
        outs,
        tokens,
        us,
    )


def up_rows(codes, parts, ranks, features):
    blocks, rank, _ = ranks[0].shape
    width = features.shape[1]

    def kernel(codes_ref, *refs):
        terms, rows_ref, outs = refs[: len(ranks)], refs[len(ranks)], refs[len(ranks) + 1 :]
        late = jnp.dot(
            summed(terms, blocks - 1), rows_ref[(blocks - 1) * BLOCK :], preferred_element_type=jnp.float32
        )
        done = 0
        for count, out in zip(parts, outs):

            def one_row(r, carry, out=out, done=done):
                code = codes_ref[done + r]
                at = jnp.maximum((code >> 1) - 1, 0)
                mine = summed(terms, at)
                mine = jnp.where(code > 1, mine, jnp.zeros_like(mine))
                mine_rows = rows_ref[pl.ds(pl.multiple_of(at * BLOCK, BLOCK), BLOCK), :]
                total = jnp.dot(mine, mine_rows, preferred_element_type=jnp.float32)
                total = total + jnp.where((code & 1) > 0, late, 0.0)
                out[r] = (ADAPTER_SCALE * total).astype(out.dtype)
                return carry

            if count <= OWN:
                for r in range(count):
                    one_row(r, 0)
            else:
                lax.fori_loop(0, count, one_row, 0)
            done += count

    return call(
        kernel,
        (codes,),
        (1,),
        [whole(array) for array in (*ranks, features)],
        [((count, rank, width), features.dtype, constant_spec((count, rank, width))) for count in parts],
    )


def values_of(lengths, base, ranks, maps, last_map, tokens=()):
    rows, width = base[0].shape
    blocks = rows // BLOCK

    def kernel(lengths_ref, one, two, three, *refs):
        terms, (maps_ref, last_ref, out_ref, last_out) = refs[: len(ranks)], refs[len(ranks) :]
        for k in range(blocks):
            at = slice(k * BLOCK, (k + 1) * BLOCK)
            adapter = maps_ref[k] if k < blocks - 1 else last_ref[0]
            added = lax.dot_general(
                summed(terms, k), adapter, (((0,), (0,)), ((), ())), preferred_element_type=jnp.float32
            )
            frozen = one[at].astype(jnp.float32) + two[at].astype(jnp.float32) + three[at].astype(jnp.float32)
            live = lax.broadcasted_iota(jnp.int32, frozen.shape, 0) < lengths_ref[k]
            values = jnp.where(live, frozen + ADAPTER_SCALE * added, 0.0).astype(out_ref.dtype)
            out_ref[at] = values
            if k == blocks - 1:
                last_out[...] = values

    return call(
        kernel,
        (lengths,),
        (1,),
        [whole(array) for array in (*base, *ranks, maps, last_map)],
        [
            ((rows, width), maps.dtype, constant_spec((rows, width))),
            ((BLOCK, width), maps.dtype, constant_spec((BLOCK, width))),
        ],
        tokens,
        100.0,
        vmem=60,
    )


def put_last(partner, me, values, choices, tokens):
    width = values.shape[1]
    block = values.shape[0] // BLOCK - 1
    size = partner.shape[0]

    def kernel(partner_ref, me_ref, *refs):
        for k, choice in enumerate(refs[:-2]):
            if len(choices) == 1:
                refs[-1][...] = choice[...]
                continue

            @pl.when(partner_ref[me_ref[0]] == lax.rem(me_ref[0] + (size - k), size))
            def _():
                refs[-1][...] = choice[...]

    return call(
        kernel,
        (partner, me.reshape(1)),
        (1,),
        [whole(choice) for choice in choices] + [(values, ANYWHERE)],
        [(values.shape, values.dtype, pl.BlockSpec((BLOCK, width), lambda i, *_: (block, 0)))],
        tokens,
        aliases={2 + len(choices): 0},
    )[0]


def base_terms(columns, hidden, weight, tokens=()):
    rows, depth = hidden.shape
    width = weight.shape[1] // 4
    tile = rows // 4

    def kernel(columns_ref, rows_ref, *refs):
        for k in range(4):
            out_ref = refs[4 + k]
            out_ref[...] = jnp.dot(rows_ref[...], refs[k][...], preferred_element_type=jnp.float32).astype(out_ref.dtype)

    def column(k):
        return pl.BlockSpec((depth, width), lambda i, at: (0, at[k]), pipeline_mode=pl.Buffered(1))

    return call(
        kernel,
        (columns,),
        (rows // tile,),
        [(hidden, pl.BlockSpec((tile, depth), lambda i, *_: (i, 0)))]
        + [(weight, column(k)) for k in range(4)],
        [((rows, width), hidden.dtype, pl.BlockSpec((tile, width), lambda i, *_: (i, 0)))] * 4,
        tokens,
        100.0,
    )


def shift(array, by):
    size = lax.axis_size("dp")
    return lax.ppermute(array, "dp", [(i, (i + by) % size) for i in range(size)])


def shifted(array, source):
    size = lax.axis_size("dp")
    me = lax.axis_index("dp")
    if size > 4:
        taken = lax.dynamic_index_in_dim(lax.all_gather(array, "dp"), source, 0, keepdims=False)
        return [taken], jnp.zeros((1,), jnp.int32)
    choices = [array] + [shift(array, by) for by in range(1, size)]
    return choices, ((me - source) % size).reshape(1)


def add(*arrays):
    return sum(array.astype(jnp.float32) for array in arrays).astype(arrays[0].dtype)


def crossed(array, by):
    return lax.ppermute(array, "tensor", [(i, i ^ by) for i in range(lax.axis_size("tensor"))])


def near(array):
    return crossed(array, 1)


def far(array):
    return crossed(array, 2)


def exchanged(array):
    array = add(array, near(array))
    return array, far(array)


def spread(array):
    return [array] + [crossed(array, by) for by in range(1, lax.axis_size("tensor"))]


def line_reduce_scatter(table):
    size = lax.axis_size("dp")
    me = lax.axis_index("dp")

    def entry(index):
        return lax.dynamic_index_in_dim(table, jnp.clip(index, 0, size - 1), 0, keepdims=False)

    from_left = from_right = None
    for step in range(size - 1):
        right = entry(size - 1 - step + me)
        left = entry(step - (size - 1 - me))
        if step > 0:
            right = add(right, from_left)
            left = add(left, from_right)
        from_left = lax.ppermute(right, "dp", [(i, i + 1) for i in range(step + 1)])
        from_right = lax.ppermute(left, "dp", [(i, i - 1) for i in range(size - 1 - step, size)])
    return entry(me) if size == 1 else add(entry(me), from_left, from_right)


ROLES = ((3, 2, 1, 0), (2, 3, 0, 1), (1, 0, 3, 2), (0, 1, 2, 3))


def body(
    partner,
    block_tenant_index,
    block_live_length,
    tenant_table_row,
    hidden,
    cotangent,
    frozen_value_weight,
    adapter_down_rows,
    adapter_up_matrix,
):
    blocks = block_tenant_index.shape[0]
    kept = blocks - SW
    devices = lax.axis_size("dp")
    me = lax.axis_index("dp")
    column = lax.axis_index("tensor")
    lengths = block_live_length
    line = devices == 4
    order = jnp.arange(devices, dtype=jnp.int32)
    holder = jnp.sum(jnp.where(partner == me, order, 0))

    cot_terms, up_own, down_own = kept_ranks(lengths, adapter_up_matrix, cotangent, adapter_down_rows)
    up_choices, _ = shifted(up_own, holder)
    cot_terms, up_last = with_last_rank(lengths, partner, me, up_choices, cotangent, cot_terms)
    rank_cot = exchanged(cot_terms)
    down_own = after(down_own, rank_cot[0])

    table_rows = jnp.sum(
        jnp.where(
            block_tenant_index[:, None] == jnp.arange(tenant_table_row.shape[0], dtype=jnp.int32)[None, :],
            tenant_table_row[None, :],
            0,
        ),
        axis=1,
    )
    weights = jnp.where(jnp.arange(blocks) < kept, 2 * (jnp.arange(blocks, dtype=jnp.int32) + 1), 1)

    def codes_of(owners):
        rows = (owners[:, None] * OWN + jnp.arange(OWN, dtype=jnp.int32)[None, :]).reshape(-1)
        return jnp.sum(jnp.where(rows[:, None] == table_rows[None, :], weights[None, :], 0), axis=1)

    columns = jnp.stack([column ^ 3, column ^ 2, column ^ 1, column]).astype(jnp.int32)

    def base(*tokens):
        return base_terms(columns, hidden, frozen_value_weight, tokens)

    def base_parts(terms, *tokens):
        sent, away, given, mine = terms
        away = add(after(away, *tokens), near(sent))
        return (mine, near(given), far(away)), away

    def inputs(down_choices, *tokens):
        return spread(
            streamed_ranks(lengths, partner, me, adapter_down_rows, down_choices, hidden, 4, tokens, 100.0)
        )

    if line:
        inner = (me == 1) | (me == 2)
        codes = codes_of(jnp.array(ROLES, jnp.int32)[me])
        (first,) = down_rows(codes, 0, 1, 1, rank_cot, hidden)
        from_end = lax.ppermute(first, "dp", [(0, 1), (3, 2)])
        from_left = lax.ppermute(down_own, "dp", [(0, 1), (1, 2), (2, 3)])
        from_right = lax.ppermute(down_own, "dp", [(3, 2), (2, 1), (1, 0)])
        passed, outward = passed_on(partner, me, down_own, from_left, from_right, [first])
        terms = base(first, passed)
        passed = lax.ppermute(passed, "dp", [(1, 2), (2, 1)])
        outward = lax.ppermute(outward, "dp", [(1, 3), (2, 0)])
        down_choices = [down_own, from_left, from_right, passed, outward]
        second, third, own = down_rows(codes, OWN, 3, 1, rank_cot, hidden, [terms[0], passed, outward], 100.0)
        second = add(second, jnp.where(inner, from_end, jnp.zeros((), first.dtype)))
        from_second = lax.ppermute(second, "dp", [(0, 1), (3, 2), (1, 3), (2, 0)])
        rank_in = inputs(down_choices, second)
        base_sums, _ = base_parts(terms, rank_in[0])
        up_codes = codes_of((me + jnp.array([1, 2, 3, 0], jnp.int32)) % devices)
        *sent, up_kept = up_rows(up_codes, [OWN] * 4, rank_in, cotangent)
        arrived = [shift(array, by + 1) for by, array in enumerate(sent)]
        middle = add(after(first, up_kept), from_second)
        from_inner = lax.ppermute(middle, "dp", [(1, 2), (2, 1)])
        up_out = add(after(up_kept, middle), *arrived)
        from_third = lax.ppermute(after(third, middle), "dp", [(0, 1), (3, 2), (1, 0), (2, 3)])
        near_total = lax.optimization_barrier(
            after(own, middle).astype(jnp.float32) + jnp.where(inner, 0.0, from_second.astype(jnp.float32))
        )
        down_out = (near_total + from_inner.astype(jnp.float32) + from_third.astype(jnp.float32)).astype(own.dtype)

        values, last_values = values_of(lengths, base_sums, rank_in, adapter_up_matrix, up_last, [up_out])
        tokens = [down_out]
    else:
        codes = codes_of(order)
        (table,) = down_rows(codes, 0, devices, 0, rank_cot, hidden)
        down_choices, _ = shifted(down_own, holder)
        down_out = line_reduce_scatter(table.reshape(devices, OWN, *table.shape[1:]))
        rank_in = inputs(down_choices, table)
        values, last_values = values_of(
            lengths, base_parts(base(table))[0], rank_in, adapter_up_matrix, up_last
        )
        (up_table,) = up_rows(codes, [devices * OWN], rank_in, cotangent)
        up_out = line_reduce_scatter(up_table.reshape(devices, OWN, *up_table.shape[1:]))
        tokens = []
    value_choices, _ = shifted(last_values, partner[me])
    values = put_last(partner, me, values, value_choices, tokens)
    return (values, down_out, up_out)


def solution(mesh):
    in_specs = (
        P("groups"),
        P(("groups", "dp")),
        P(("groups", "dp")),
        P("groups"),
        P(("groups", "dp"), "tensor"),
        P(("groups", "dp"), "tensor"),
        P("tensor", None),
        P(("groups", "dp"), None, "tensor"),
        P(("groups", "dp"), None, "tensor"),
    )
    out_specs = (
        P(("groups", "dp"), "tensor"),
        P(("groups", "dp"), None, "tensor"),
        P(("groups", "dp"), None, "tensor"),
    )
    return jax.shard_map(body, mesh=mesh, in_specs=in_specs, out_specs=out_specs, check_vma=False)
```

```python
import jax
import jax.numpy as jnp
from jax import lax
from jax.experimental import pallas as pl
from jax.experimental.pallas import tpu as pltpu
from jax.sharding import PartitionSpec as P

BLOCK = 128
SW = 1
OWN = 4


ADAPTER_SCALE = 0.5

ANYWHERE = pl.BlockSpec(memory_space=pl.ANY)
ROW_PRODUCT = (((1,), (1,)), ((), ()))


def call(kernel, scalars, grid, inputs, outputs, tokens=(), us=1.0, scratch=(), aliases=None, vmem=16):
    def run(*refs):
        cut = len(scalars) + len(inputs)
        return kernel(*refs[:cut], *refs[cut + len(tokens) :])

    return pl.pallas_call(
        run,
        grid_spec=pltpu.PrefetchScalarGridSpec(
            num_scalar_prefetch=len(scalars),
            grid=grid,
            in_specs=[spec for _, spec in inputs] + [ANYWHERE] * len(tokens),
            out_specs=[spec for _, _, spec in outputs],
            scratch_shapes=scratch,
        ),
        out_shape=[jax.ShapeDtypeStruct(shape, kind) for shape, kind, _ in outputs],
        input_output_aliases=aliases or {},
        compiler_params=pltpu.CompilerParams(vmem_limit_bytes=vmem * 1024 * 1024),
        cost_estimate=pl.CostEstimate(flops=int(us * 1e9), bytes_accessed=int(us * 3.6e5), transcendentals=0),
    )(*scalars, *[array for array, _ in inputs], *tokens)


def constant_spec(shape):
    return pl.BlockSpec(shape, lambda *_: (0,) * len(shape), pipeline_mode=pl.Buffered(1))


def whole(array):
    return (array, constant_spec(array.shape))


def nothing(*refs):
    pass


def after(array, *tokens):
    return call(
        nothing, (), (1,), [(array, ANYWHERE)], [(array.shape, array.dtype, ANYWHERE)], tokens, 0.1, aliases={0: 0}
    )[0]


def masked_rank(adapter, rows, length):
    ranks = lax.dot_general(adapter, rows, ROW_PRODUCT, preferred_element_type=jnp.float32)
    live = lax.broadcasted_iota(jnp.int32, ranks.shape, 1) < length
    return jnp.where(live, ranks, 0.0).astype(rows.dtype)


def kept_ranks(lengths, maps, features, others):
    blocks, rank, width = maps.shape
    kept = blocks - SW
    last_shapes = [(SW, rank, width), (SW, *others.shape[1:])]

    def kernel(lengths_ref, maps_ref, rows_ref, others_ref, out_ref, last_ref, last_other):
        last_ref[...] = maps_ref[kept:]
        last_other[...] = others_ref[...]
        for k in range(kept):
            out_ref[k] = masked_rank(maps_ref[k], rows_ref[k * BLOCK : (k + 1) * BLOCK], lengths_ref[k])

    return call(
        kernel,
        (lengths,),
        (1,),
        [
            whole(maps),
            (features, pl.BlockSpec((kept * BLOCK, width), lambda i, *_: (0, 0), pipeline_mode=pl.Buffered(1))),
            (others, pl.BlockSpec(last_shapes[1], lambda i, *_: (kept, 0, 0), pipeline_mode=pl.Buffered(1))),
        ],
        [((blocks, rank, BLOCK), features.dtype, pl.BlockSpec((kept, rank, BLOCK), lambda i, *_: (0, 0, 0)))]
        + [(shape, features.dtype, constant_spec(shape)) for shape in last_shapes],
        vmem=60,
    )


def passed_on(partner, me, own, from_left, from_right, tokens):
    shape = own.shape

    def kernel(partner_ref, me_ref, own_ref, left_ref, right_ref, inner_ref, outer_ref):
        left = me_ref[0] == 1

        @pl.when(left)
        def _():
            inner_ref[...] = left_ref[...]
            outer_ref[...] = left_ref[...]

        @pl.when(jnp.logical_not(left))
        def _():
            inner_ref[...] = right_ref[...]
            outer_ref[...] = right_ref[...]

        @pl.when(partner_ref[me_ref[0]] == jnp.where(left, 3, 0))
        def _():
            outer_ref[...] = own_ref[...]

    return call(
        kernel,
        (partner, me.reshape(1)),
        (1,),
        [whole(array) for array in (own, from_left, from_right)],
        [(shape, own.dtype, constant_spec(shape))] * 2,
        tokens,
        1.0,
    )


def with_last_rank(lengths, partner, me, choices, features, ranks):
    shape = choices[0].shape
    block = ranks.shape[0] - 1
    size = partner.shape[0]

    def kernel(lengths_ref, partner_ref, me_ref, *refs):
        rows_ref, _, out_ref, chosen_ref = refs[-4:]
        for k, choice in enumerate(refs[:-4]):
            if len(choices) == 1:
                chosen_ref[...] = choice[...]
                continue

            @pl.when(partner_ref[lax.rem(me_ref[0] + (size - k), size)] == me_ref[0])
            def _():
                chosen_ref[...] = choice[...]

        out_ref[0] = masked_rank(chosen_ref[0], rows_ref[...], lengths_ref[block])

    return call(
        kernel,
        (lengths, partner, me.reshape(1)),
        (1,),
        [whole(choice) for choice in choices]
        + [(features, pl.BlockSpec((BLOCK, shape[2]), lambda i, *_: (block, 0), pipeline_mode=pl.Buffered(1)))]
        + [(ranks, ANYWHERE)],
        [
            (ranks.shape, ranks.dtype, pl.BlockSpec((1, *ranks.shape[1:]), lambda i, *_: (block, 0, 0))),
            (shape, features.dtype, constant_spec(shape)),
        ],
        aliases={4 + len(choices): 0},
    )


def streamed_ranks(lengths, partner, me, maps, choices, features, each, tokens=(), us=1.0):
    blocks, rank, width = maps.shape
    steps = pl.cdiv(blocks, each)
    end = blocks - 1 - (steps - 1) * each

    def picked(partner_ref, at):
        if len(choices) == 1:
            return [at == at]
        held = [
            partner_ref[at] == at,
            (partner_ref[jnp.maximum(at - 1, 0)] == at) & (at > 0),
            (partner_ref[jnp.minimum(at + 1, 3)] == at) & (at < 3),
        ]
        other = jnp.logical_not(held[0] | held[1] | held[2])
        inner = (at == 1) | (at == 2)
        return [*held, other & inner, other & jnp.logical_not(inner)]

    def kernel(lengths_ref, partner_ref, me_ref, *refs):
        maps_refs, rows_refs, choices_refs, out_ref = refs[:each], refs[each : 2 * each], refs[2 * each : -1], refs[-1]
        step = pl.program_id(0)

        def one(k):
            block = step * each + k
            out_ref[block] = masked_rank(maps_refs[k][0], rows_refs[k][...], lengths_ref[block])

        @pl.when(step < steps - 1)
        def _():
            for k in range(each):
                one(k)

        @pl.when(step == steps - 1)
        def _():
            for k in range(end):
                one(k)
            for choice, use in zip(choices_refs, picked(partner_ref, me_ref[0])):

                @pl.when(use)
                def _():
                    out_ref[blocks - 1] = masked_rank(choice[0], rows_refs[end][...], lengths_ref[blocks - 1])

    def at(i, k):
        block = i * each + k
        return jnp.where(block < blocks, block, block - each)

    return call(
        kernel,
        (lengths, partner, me.reshape(1)),
        (steps,),
        [(maps, pl.BlockSpec((1, rank, width), lambda i, *_, k=k: (at(i, k), 0, 0))) for k in range(each)]
        + [(features, pl.BlockSpec((BLOCK, width), lambda i, *_, k=k: (at(i, k), 0))) for k in range(each)]
        + [whole(choice) for choice in choices],
        [((blocks, rank, BLOCK), features.dtype, constant_spec((blocks, rank, BLOCK)))],
        tokens,
        us,
    )[0]


def summed(terms, at):
    return sum(term[at].astype(jnp.float32) for term in terms).astype(terms[0].dtype)


def down_rows(codes, first, parts, copies, ranks, features, tokens=(), us=1.0):
    blocks, rank, _ = ranks[0].shape
    width = features.shape[1]
    piece = min(width, 512)

    def block_at(code):
        return jnp.maximum((code >> 1) - 1, 0)

    def kernel(codes_ref, a, b, *refs):
        rows_refs, last_ref, outs = refs[:OWN], refs[OWN], refs[OWN + 1 :]
        step = pl.program_id(0)

        def fill(to):
            for k in range(OWN):
                code = codes_ref[first + step * OWN + k]
                mine = summed((a, b), block_at(code))
                mine = jnp.where(code > 1, mine, jnp.zeros_like(mine))

                def put(at, total):
                    value = (ADAPTER_SCALE * total).astype(features.dtype)
                    for out_ref in to:
                        out_ref[k, :, at] = value

                for at in [slice(c, c + piece) for c in range(0, width, piece)]:
                    put(at, jnp.dot(mine, rows_refs[k][:, at], preferred_element_type=jnp.float32))

                @pl.when((code & 1) > 0)
                def _():
                    late = summed((a, b), blocks - 1)
                    for at in [slice(c, c + piece) for c in range(0, width, piece)]:
                        put(
                            at,
                            jnp.dot(mine, rows_refs[k][:, at], preferred_element_type=jnp.float32)
                            + jnp.dot(late, last_ref[:, at], preferred_element_type=jnp.float32),
                        )

        if not copies or parts == 1:
            fill(outs)
        else:
            for part in range(parts):

                @pl.when(step == part)
                def _():
                    fill(outs[part:] if part == parts - 1 else outs[part : part + 1])

    def rows_spec(k):
        return pl.BlockSpec((BLOCK, width), lambda r, at: (block_at(at[first + r * OWN + k]), 0))

    shape = (OWN, rank, width)
    if copies:
        outs = [(shape, features.dtype, constant_spec(shape))] * (parts - 1 + copies)
    else:
        outs = [((parts * OWN, rank, width), features.dtype, pl.BlockSpec(shape, lambda r, *_: (r, 0, 0)))]
    return call(
        kernel,
        (codes,),
        (parts,),
        [whole(array) for array in ranks]
        + [(features, rows_spec(k)) for k in range(OWN)]
        + [(features, pl.BlockSpec((BLOCK, width), lambda r, *_: (blocks - 1, 0), pipeline_mode=pl.Buffered(1)))],
        outs,
        tokens,
        us,
    )


def up_rows(codes, parts, ranks, features):
    blocks, rank, _ = ranks[0].shape
    width = features.shape[1]

    def kernel(codes_ref, *refs):
        terms, rows_ref, outs = refs[: len(ranks)], refs[len(ranks)], refs[len(ranks) + 1 :]
        late = jnp.dot(
            summed(terms, blocks - 1), rows_ref[(blocks - 1) * BLOCK :], preferred_element_type=jnp.float32
        )
        done = 0
        for count, out in zip(parts, outs):

            def one_row(r, carry, out=out, done=done):
                code = codes_ref[done + r]
                at = jnp.maximum((code >> 1) - 1, 0)
                mine = summed(terms, at)
                mine = jnp.where(code > 1, mine, jnp.zeros_like(mine))
                mine_rows = rows_ref[pl.ds(pl.multiple_of(at * BLOCK, BLOCK), BLOCK), :]
                total = jnp.dot(mine, mine_rows, preferred_element_type=jnp.float32)
                total = total + jnp.where((code & 1) > 0, late, 0.0)
                out[r] = (ADAPTER_SCALE * total).astype(out.dtype)
                return carry

            if count <= OWN:
                for r in range(count):
                    one_row(r, 0)
            else:
                lax.fori_loop(0, count, one_row, 0)
            done += count

    return call(
        kernel,
        (codes,),
        (1,),
        [whole(array) for array in (*ranks, features)],
        [((count, rank, width), features.dtype, constant_spec((count, rank, width))) for count in parts],
    )


def values_of(lengths, base, ranks, maps, last_map, tokens=()):
    rows, width = base[0].shape
    blocks = rows // BLOCK

    def kernel(lengths_ref, one, two, three, *refs):
        terms, (maps_ref, last_ref, out_ref, last_out) = refs[: len(ranks)], refs[len(ranks) :]
        for k in range(blocks):
            at = slice(k * BLOCK, (k + 1) * BLOCK)
            adapter = maps_ref[k] if k < blocks - 1 else last_ref[0]
            added = lax.dot_general(
                summed(terms, k), adapter, (((0,), (0,)), ((), ())), preferred_element_type=jnp.float32
            )
            frozen = one[at].astype(jnp.float32) + two[at].astype(jnp.float32) + three[at].astype(jnp.float32)
            live = lax.broadcasted_iota(jnp.int32, frozen.shape, 0) < lengths_ref[k]
            values = jnp.where(live, frozen + ADAPTER_SCALE * added, 0.0).astype(out_ref.dtype)
            out_ref[at] = values
            if k == blocks - 1:
                last_out[...] = values

    return call(
        kernel,
        (lengths,),
        (1,),
        [whole(array) for array in (*base, *ranks, maps, last_map)],
        [
            ((rows, width), maps.dtype, constant_spec((rows, width))),
            ((BLOCK, width), maps.dtype, constant_spec((BLOCK, width))),
        ],
        tokens,
        100.0,
        vmem=60,
    )


def put_last(partner, me, values, choices, tokens):
    width = values.shape[1]
    block = values.shape[0] // BLOCK - 1
    size = partner.shape[0]

    def kernel(partner_ref, me_ref, *refs):
        for k, choice in enumerate(refs[:-2]):
            if len(choices) == 1:
                refs[-1][...] = choice[...]
                continue

            @pl.when(partner_ref[me_ref[0]] == lax.rem(me_ref[0] + (size - k), size))
            def _():
                refs[-1][...] = choice[...]

    return call(
        kernel,
        (partner, me.reshape(1)),
        (1,),
        [whole(choice) for choice in choices] + [(values, ANYWHERE)],
        [(values.shape, values.dtype, pl.BlockSpec((BLOCK, width), lambda i, *_: (block, 0)))],
        tokens,
        aliases={2 + len(choices): 0},
    )[0]


def base_terms(columns, hidden, weight, tokens=()):
    rows, depth = hidden.shape
    width = weight.shape[1] // 4
    tile = rows // 4

    def kernel(columns_ref, rows_ref, *refs):
        for k in range(4):
            out_ref = refs[4 + k]
            out_ref[...] = jnp.dot(rows_ref[...], refs[k][...], preferred_element_type=jnp.float32).astype(out_ref.dtype)

    def column(k):
        return pl.BlockSpec((depth, width), lambda i, at: (0, at[k]), pipeline_mode=pl.Buffered(1))

    return call(
        kernel,
        (columns,),
        (rows // tile,),
        [(hidden, pl.BlockSpec((tile, depth), lambda i, *_: (i, 0)))]
        + [(weight, column(k)) for k in range(4)],
        [((rows, width), hidden.dtype, pl.BlockSpec((tile, width), lambda i, *_: (i, 0)))] * 4,
        tokens,
        100.0,
    )


def shift(array, by):
    size = lax.axis_size("dp")
    return lax.ppermute(array, "dp", [(i, (i + by) % size) for i in range(size)])


def shifted(array, source):
    size = lax.axis_size("dp")
    me = lax.axis_index("dp")
    if size > 4:
        taken = lax.dynamic_index_in_dim(lax.all_gather(array, "dp"), source, 0, keepdims=False)
        return [taken], jnp.zeros((1,), jnp.int32)
    choices = [array] + [shift(array, by) for by in range(1, size)]
    return choices, ((me - source) % size).reshape(1)


def add(*arrays):
    return sum(array.astype(jnp.float32) for array in arrays).astype(arrays[0].dtype)


def crossed(array, by):
    return lax.ppermute(array, "tensor", [(i, i ^ by) for i in range(lax.axis_size("tensor"))])


def near(array):
    return crossed(array, 1)


def far(array):
    return crossed(array, 2)


def exchanged(array):
    array = add(array, near(array))
    return array, far(array)


def spread(array):
    return [array] + [crossed(array, by) for by in range(1, lax.axis_size("tensor"))]


def line_reduce_scatter(table):
    size = lax.axis_size("dp")
    me = lax.axis_index("dp")

    def entry(index):
        return lax.dynamic_index_in_dim(table, jnp.clip(index, 0, size - 1), 0, keepdims=False)

    from_left = from_right = None
    for step in range(size - 1):
        right = entry(size - 1 - step + me)
        left = entry(step - (size - 1 - me))
        if step > 0:
            right = add(right, from_left)
            left = add(left, from_right)
        from_left = lax.ppermute(right, "dp", [(i, i + 1) for i in range(step + 1)])
        from_right = lax.ppermute(left, "dp", [(i, i - 1) for i in range(size - 1 - step, size)])
    return entry(me) if size == 1 else add(entry(me), from_left, from_right)


ROLES = ((3, 2, 1, 0), (2, 3, 0, 1), (1, 0, 3, 2), (0, 1, 2, 3))


def body(
    partner,
    block_tenant_index,
    block_live_length,
    tenant_table_row,
    hidden,
    cotangent,
    frozen_value_weight,
    adapter_down_rows,
    adapter_up_matrix,
):
    blocks = block_tenant_index.shape[0]
    kept = blocks - SW
    devices = lax.axis_size("dp")
    me = lax.axis_index("dp")
    column = lax.axis_index("tensor")
    lengths = block_live_length
    line = devices == 4
    order = jnp.arange(devices, dtype=jnp.int32)
    holder = jnp.sum(jnp.where(partner == me, order, 0))

    cot_terms, up_own, down_own = kept_ranks(lengths, adapter_up_matrix, cotangent, adapter_down_rows)
    up_choices, _ = shifted(up_own, holder)
    cot_terms, up_last = with_last_rank(lengths, partner, me, up_choices, cotangent, cot_terms)
    rank_cot = exchanged(cot_terms)
    down_own = after(down_own, rank_cot[0])

    table_rows = jnp.sum(
        jnp.where(
            block_tenant_index[:, None] == jnp.arange(tenant_table_row.shape[0], dtype=jnp.int32)[None, :],
            tenant_table_row[None, :],
            0,
        ),
        axis=1,
    )
    weights = jnp.where(jnp.arange(blocks) < kept, 2 * (jnp.arange(blocks, dtype=jnp.int32) + 1), 1)

    def codes_of(owners):
        rows = (owners[:, None] * OWN + jnp.arange(OWN, dtype=jnp.int32)[None, :]).reshape(-1)
        return jnp.sum(jnp.where(rows[:, None] == table_rows[None, :], weights[None, :], 0), axis=1)

    columns = jnp.stack([column ^ 3, column ^ 2, column ^ 1, column]).astype(jnp.int32)

    def base(*tokens):
        return base_terms(columns, hidden, frozen_value_weight, tokens)

    def base_parts(terms, *tokens):
        sent, away, given, mine = terms
        away = add(after(away, *tokens), near(sent))
        return (mine, near(given), far(away)), away

    def inputs(down_choices, *tokens):
        return spread(
            streamed_ranks(lengths, partner, me, adapter_down_rows, down_choices, hidden, 4, tokens, 100.0)
        )

    if line:
        inner = (me == 1) | (me == 2)
        codes = codes_of(jnp.array(ROLES, jnp.int32)[me])
        (first,) = down_rows(codes, 0, 1, 1, rank_cot, hidden)
        from_end = lax.ppermute(first, "dp", [(0, 1), (3, 2)])
        from_left = lax.ppermute(down_own, "dp", [(0, 1), (1, 2), (2, 3)])
        from_right = lax.ppermute(down_own, "dp", [(3, 2), (2, 1), (1, 0)])
        passed, outward = passed_on(partner, me, down_own, from_left, from_right, [first])
        terms = base(first, passed)
        passed = lax.ppermute(passed, "dp", [(1, 2), (2, 1)])
        outward = lax.ppermute(outward, "dp", [(1, 3), (2, 0)])
        down_choices = [down_own, from_left, from_right, passed, outward]
        second, third, own = down_rows(codes, OWN, 3, 1, rank_cot, hidden, [terms[0], passed, outward], 100.0)
        second = add(second, jnp.where(inner, from_end, jnp.zeros((), first.dtype)))
        from_second = lax.ppermute(second, "dp", [(0, 1), (3, 2), (1, 3), (2, 0)])
        rank_in = inputs(down_choices, second)
        base_sums, _ = base_parts(terms, rank_in[0])
        up_codes = codes_of((me + jnp.array([1, 2, 3, 0], jnp.int32)) % devices)
        *sent, up_kept = up_rows(up_codes, [OWN] * 4, rank_in, cotangent)
        arrived = [shift(array, by + 1) for by, array in enumerate(sent)]
        middle = add(after(first, up_kept), from_second)
        third = after(third, from_second)
        from_inner = lax.ppermute(after(middle, third), "dp", [(1, 2), (2, 1)])
        up_out = add(after(up_kept, middle), *arrived)
        from_third = lax.ppermute(third, "dp", [(0, 1), (3, 2), (1, 0), (2, 3)])
        near_total = lax.optimization_barrier(
            after(own, middle).astype(jnp.float32) + jnp.where(inner, 0.0, from_second.astype(jnp.float32))
        )
        down_out = (near_total + from_inner.astype(jnp.float32) + from_third.astype(jnp.float32)).astype(own.dtype)

        values, last_values = values_of(lengths, base_sums, rank_in, adapter_up_matrix, up_last)
        last_values = after(last_values, up_out)
        tokens = [down_out]
    else:
        codes = codes_of(order)
        (table,) = down_rows(codes, 0, devices, 0, rank_cot, hidden)
        down_choices, _ = shifted(down_own, holder)
        down_out = line_reduce_scatter(table.reshape(devices, OWN, *table.shape[1:]))
        rank_in = inputs(down_choices, table)
        values, last_values = values_of(
            lengths, base_parts(base(table))[0], rank_in, adapter_up_matrix, up_last
        )
        (up_table,) = up_rows(codes, [devices * OWN], rank_in, cotangent)
        up_out = line_reduce_scatter(up_table.reshape(devices, OWN, *up_table.shape[1:]))
        tokens = []
    value_choices, _ = shifted(last_values, partner[me])
    values = put_last(partner, me, values, value_choices, tokens)
    return (values, down_out, up_out)


def solution(mesh):
    in_specs = (
        P("groups"),
        P(("groups", "dp")),
        P(("groups", "dp")),
        P("groups"),
        P(("groups", "dp"), "tensor"),
        P(("groups", "dp"), "tensor"),
        P("tensor", None),
        P(("groups", "dp"), None, "tensor"),
        P(("groups", "dp"), None, "tensor"),
    )
    out_specs = (
        P(("groups", "dp"), "tensor"),
        P(("groups", "dp"), None, "tensor"),
        P(("groups", "dp"), None, "tensor"),
    )
    return jax.shard_map(body, mesh=mesh, in_specs=in_specs, out_specs=out_specs, check_vma=False)
```

```python
import jax
import jax.numpy as jnp
from jax import lax
from jax.experimental import pallas as pl
from jax.experimental.pallas import tpu as pltpu
from jax.sharding import PartitionSpec as P

BLOCK = 128
SW = 1
OWN = 4


ADAPTER_SCALE = 0.5

ANYWHERE = pl.BlockSpec(memory_space=pl.ANY)
ROW_PRODUCT = (((1,), (1,)), ((), ()))


def call(kernel, scalars, grid, inputs, outputs, tokens=(), us=1.0, scratch=(), aliases=None, vmem=16):
    def run(*refs):
        cut = len(scalars) + len(inputs)
        return kernel(*refs[:cut], *refs[cut + len(tokens) :])

    return pl.pallas_call(
        run,
        grid_spec=pltpu.PrefetchScalarGridSpec(
            num_scalar_prefetch=len(scalars),
            grid=grid,
            in_specs=[spec for _, spec in inputs] + [ANYWHERE] * len(tokens),
            out_specs=[spec for _, _, spec in outputs],
            scratch_shapes=scratch,
        ),
        out_shape=[jax.ShapeDtypeStruct(shape, kind) for shape, kind, _ in outputs],
        input_output_aliases=aliases or {},
        compiler_params=pltpu.CompilerParams(vmem_limit_bytes=vmem * 1024 * 1024),
        cost_estimate=pl.CostEstimate(flops=int(us * 1e9), bytes_accessed=int(us * 3.6e5), transcendentals=0),
    )(*scalars, *[array for array, _ in inputs], *tokens)


def constant_spec(shape):
    return pl.BlockSpec(shape, lambda *_: (0,) * len(shape), pipeline_mode=pl.Buffered(1))


def whole(array):
    return (array, constant_spec(array.shape))


def nothing(*refs):
    pass


def after(array, *tokens):
    return call(
        nothing, (), (1,), [(array, ANYWHERE)], [(array.shape, array.dtype, ANYWHERE)], tokens, 0.1, aliases={0: 0}
    )[0]


def masked_rank(adapter, rows, length):
    ranks = lax.dot_general(adapter, rows, ROW_PRODUCT, preferred_element_type=jnp.float32)
    live = lax.broadcasted_iota(jnp.int32, ranks.shape, 1) < length
    return jnp.where(live, ranks, 0.0).astype(rows.dtype)


def kept_ranks(lengths, maps, features, others):
    blocks, rank, width = maps.shape
    kept = blocks - SW
    last_shapes = [(SW, rank, width), (SW, *others.shape[1:])]

    def kernel(lengths_ref, maps_ref, rows_ref, others_ref, out_ref, last_ref, last_other):
        last_ref[...] = maps_ref[kept:]
        last_other[...] = others_ref[...]
        for k in range(kept):
            out_ref[k] = masked_rank(maps_ref[k], rows_ref[k * BLOCK : (k + 1) * BLOCK], lengths_ref[k])

    return call(
        kernel,
        (lengths,),
        (1,),
        [
            whole(maps),
            (features, pl.BlockSpec((kept * BLOCK, width), lambda i, *_: (0, 0), pipeline_mode=pl.Buffered(1))),
            (others, pl.BlockSpec(last_shapes[1], lambda i, *_: (kept, 0, 0), pipeline_mode=pl.Buffered(1))),
        ],
        [((blocks, rank, BLOCK), features.dtype, pl.BlockSpec((kept, rank, BLOCK), lambda i, *_: (0, 0, 0)))]
        + [(shape, features.dtype, constant_spec(shape)) for shape in last_shapes],
        vmem=60,
    )


def passed_on(partner, me, own, from_left, from_right, tokens):
    shape = own.shape

    def kernel(partner_ref, me_ref, own_ref, left_ref, right_ref, inner_ref, outer_ref):
        left = me_ref[0] == 1

        @pl.when(left)
        def _():
            inner_ref[...] = left_ref[...]
            outer_ref[...] = left_ref[...]

        @pl.when(jnp.logical_not(left))
        def _():
            inner_ref[...] = right_ref[...]
            outer_ref[...] = right_ref[...]

        @pl.when(partner_ref[me_ref[0]] == jnp.where(left, 3, 0))
        def _():
            outer_ref[...] = own_ref[...]

    return call(
        kernel,
        (partner, me.reshape(1)),
        (1,),
        [whole(array) for array in (own, from_left, from_right)],
        [(shape, own.dtype, constant_spec(shape))] * 2,
        tokens,
        1.0,
    )


def with_last_rank(lengths, partner, me, choices, features, ranks):
    shape = choices[0].shape
    block = ranks.shape[0] - 1
    size = partner.shape[0]

    def kernel(lengths_ref, partner_ref, me_ref, *refs):
        rows_ref, _, out_ref, chosen_ref = refs[-4:]
        for k, choice in enumerate(refs[:-4]):
            if len(choices) == 1:
                chosen_ref[...] = choice[...]
                continue

            @pl.when(partner_ref[lax.rem(me_ref[0] + (size - k), size)] == me_ref[0])
            def _():
                chosen_ref[...] = choice[...]

        out_ref[0] = masked_rank(chosen_ref[0], rows_ref[...], lengths_ref[block])

    return call(
        kernel,
        (lengths, partner, me.reshape(1)),
        (1,),
        [whole(choice) for choice in choices]
        + [(features, pl.BlockSpec((BLOCK, shape[2]), lambda i, *_: (block, 0), pipeline_mode=pl.Buffered(1)))]
        + [(ranks, ANYWHERE)],
        [
            (ranks.shape, ranks.dtype, pl.BlockSpec((1, *ranks.shape[1:]), lambda i, *_: (block, 0, 0))),
            (shape, features.dtype, constant_spec(shape)),
        ],
        aliases={4 + len(choices): 0},
    )


def streamed_ranks(lengths, partner, me, maps, choices, features, each, tokens=(), us=1.0):
    blocks, rank, width = maps.shape
    steps = pl.cdiv(blocks, each)
    end = blocks - 1 - (steps - 1) * each

    def picked(partner_ref, at):
        if len(choices) == 1:
            return [at == at]
        held = [
            partner_ref[at] == at,
            (partner_ref[jnp.maximum(at - 1, 0)] == at) & (at > 0),
            (partner_ref[jnp.minimum(at + 1, 3)] == at) & (at < 3),
        ]
        other = jnp.logical_not(held[0] | held[1] | held[2])
        inner = (at == 1) | (at == 2)
        return [*held, other & inner, other & jnp.logical_not(inner)]

    def kernel(lengths_ref, partner_ref, me_ref, *refs):
        maps_refs, rows_refs, choices_refs, out_ref = refs[:each], refs[each : 2 * each], refs[2 * each : -1], refs[-1]
        step = pl.program_id(0)

        def one(k):
            block = step * each + k
            out_ref[block] = masked_rank(maps_refs[k][0], rows_refs[k][...], lengths_ref[block])

        @pl.when(step < steps - 1)
        def _():
            for k in range(each):
                one(k)

        @pl.when(step == steps - 1)
        def _():
            for k in range(end):
                one(k)
            for choice, use in zip(choices_refs, picked(partner_ref, me_ref[0])):

                @pl.when(use)
                def _():
                    out_ref[blocks - 1] = masked_rank(choice[0], rows_refs[end][...], lengths_ref[blocks - 1])

    def at(i, k):
        block = i * each + k
        return jnp.where(block < blocks, block, block - each)

    return call(
        kernel,
        (lengths, partner, me.reshape(1)),
        (steps,),
        [(maps, pl.BlockSpec((1, rank, width), lambda i, *_, k=k: (at(i, k), 0, 0))) for k in range(each)]
        + [(features, pl.BlockSpec((BLOCK, width), lambda i, *_, k=k: (at(i, k), 0))) for k in range(each)]
        + [whole(choice) for choice in choices],
        [((blocks, rank, BLOCK), features.dtype, constant_spec((blocks, rank, BLOCK)))],
        tokens,
        us,
    )[0]


def summed(terms, at):
    return sum(term[at].astype(jnp.float32) for term in terms).astype(terms[0].dtype)


def down_rows(codes, first, parts, copies, ranks, features, tokens=(), us=1.0):
    blocks, rank, _ = ranks[0].shape
    width = features.shape[1]
    piece = min(width, 512)

    def block_at(code):
        return jnp.maximum((code >> 1) - 1, 0)

    def kernel(codes_ref, a, b, *refs):
        rows_refs, last_ref, outs = refs[:OWN], refs[OWN], refs[OWN + 1 :]
        step = pl.program_id(0)

        def fill(to):
            for k in range(OWN):
                code = codes_ref[first + step * OWN + k]
                mine = summed((a, b), block_at(code))
                mine = jnp.where(code > 1, mine, jnp.zeros_like(mine))

                def put(at, total):
                    value = (ADAPTER_SCALE * total).astype(features.dtype)
                    for out_ref in to:
                        out_ref[k, :, at] = value

                for at in [slice(c, c + piece) for c in range(0, width, piece)]:
                    put(at, jnp.dot(mine, rows_refs[k][:, at], preferred_element_type=jnp.float32))

                @pl.when((code & 1) > 0)
                def _():
                    late = summed((a, b), blocks - 1)
                    for at in [slice(c, c + piece) for c in range(0, width, piece)]:
                        put(
                            at,
                            jnp.dot(mine, rows_refs[k][:, at], preferred_element_type=jnp.float32)
                            + jnp.dot(late, last_ref[:, at], preferred_element_type=jnp.float32),
                        )

        if not copies or parts == 1:
            fill(outs)
        else:
            for part in range(parts):

                @pl.when(step == part)
                def _():
                    fill(outs[part:] if part == parts - 1 else outs[part : part + 1])

    def rows_spec(k):
        return pl.BlockSpec((BLOCK, width), lambda r, at: (block_at(at[first + r * OWN + k]), 0))

    shape = (OWN, rank, width)
    if copies:
        outs = [(shape, features.dtype, constant_spec(shape))] * (parts - 1 + copies)
    else:
        outs = [((parts * OWN, rank, width), features.dtype, pl.BlockSpec(shape, lambda r, *_: (r, 0, 0)))]
    return call(
        kernel,
        (codes,),
        (parts,),
        [whole(array) for array in ranks]
        + [(features, rows_spec(k)) for k in range(OWN)]
        + [(features, pl.BlockSpec((BLOCK, width), lambda r, *_: (blocks - 1, 0), pipeline_mode=pl.Buffered(1)))],
        outs,
        tokens,
        us,
    )


def up_rows(codes, parts, ranks, features):
    blocks, rank, _ = ranks[0].shape
    width = features.shape[1]

    def kernel(codes_ref, *refs):
        terms, rows_ref, outs = refs[: len(ranks)], refs[len(ranks)], refs[len(ranks) + 1 :]
        late = jnp.dot(
            summed(terms, blocks - 1), rows_ref[(blocks - 1) * BLOCK :], preferred_element_type=jnp.float32
        )
        done = 0
        for count, out in zip(parts, outs):

            def one_row(r, carry, out=out, done=done):
                code = codes_ref[done + r]
                at = jnp.maximum((code >> 1) - 1, 0)
                mine = summed(terms, at)
                mine = jnp.where(code > 1, mine, jnp.zeros_like(mine))
                mine_rows = rows_ref[pl.ds(pl.multiple_of(at * BLOCK, BLOCK), BLOCK), :]
                total = jnp.dot(mine, mine_rows, preferred_element_type=jnp.float32)
                total = total + jnp.where((code & 1) > 0, late, 0.0)
                out[r] = (ADAPTER_SCALE * total).astype(out.dtype)
                return carry

            if count <= OWN:
                for r in range(count):
                    one_row(r, 0)
            else:
                lax.fori_loop(0, count, one_row, 0)
            done += count

    return call(
        kernel,
        (codes,),
        (1,),
        [whole(array) for array in (*ranks, features)],
        [((count, rank, width), features.dtype, constant_spec((count, rank, width))) for count in parts],
    )


def values_of(lengths, base, ranks, maps, last_map, tokens=()):
    rows, width = base[0].shape
    blocks = rows // BLOCK

    def kernel(lengths_ref, one, two, three, *refs):
        terms, (maps_ref, last_ref, out_ref, last_out) = refs[: len(ranks)], refs[len(ranks) :]
        for k in range(blocks):
            at = slice(k * BLOCK, (k + 1) * BLOCK)
            adapter = maps_ref[k] if k < blocks - 1 else last_ref[0]
            added = lax.dot_general(
                summed(terms, k), adapter, (((0,), (0,)), ((), ())), preferred_element_type=jnp.float32
            )
            frozen = one[at].astype(jnp.float32) + two[at].astype(jnp.float32) + three[at].astype(jnp.float32)
            live = lax.broadcasted_iota(jnp.int32, frozen.shape, 0) < lengths_ref[k]
            values = jnp.where(live, frozen + ADAPTER_SCALE * added, 0.0).astype(out_ref.dtype)
            out_ref[at] = values
            if k == blocks - 1:
                last_out[...] = values

    return call(
        kernel,
        (lengths,),
        (1,),
        [whole(array) for array in (*base, *ranks, maps, last_map)],
        [
            ((rows, width), maps.dtype, constant_spec((rows, width))),
            ((BLOCK, width), maps.dtype, constant_spec((BLOCK, width))),
        ],
        tokens,
        100.0,
        vmem=60,
    )


def put_last(partner, me, values, choices, tokens):
    width = values.shape[1]
    block = values.shape[0] // BLOCK - 1
    size = partner.shape[0]

    def kernel(partner_ref, me_ref, *refs):
        for k, choice in enumerate(refs[:-2]):
            if len(choices) == 1:
                refs[-1][...] = choice[...]
                continue

            @pl.when(partner_ref[me_ref[0]] == lax.rem(me_ref[0] + (size - k), size))
            def _():
                refs[-1][...] = choice[...]

    return call(
        kernel,
        (partner, me.reshape(1)),
        (1,),
        [whole(choice) for choice in choices] + [(values, ANYWHERE)],
        [(values.shape, values.dtype, pl.BlockSpec((BLOCK, width), lambda i, *_: (block, 0)))],
        tokens,
        aliases={2 + len(choices): 0},
    )[0]


def base_terms(columns, hidden, weight, tokens=()):
    rows, depth = hidden.shape
    width = weight.shape[1] // 4
    tile = rows // 4

    def kernel(columns_ref, rows_ref, *refs):
        for k in range(4):
            out_ref = refs[4 + k]
            out_ref[...] = jnp.dot(rows_ref[...], refs[k][...], preferred_element_type=jnp.float32).astype(out_ref.dtype)

    def column(k):
        return pl.BlockSpec((depth, width), lambda i, at: (0, at[k]), pipeline_mode=pl.Buffered(1))

    return call(
        kernel,
        (columns,),
        (rows // tile,),
        [(hidden, pl.BlockSpec((tile, depth), lambda i, *_: (i, 0)))]
        + [(weight, column(k)) for k in range(4)],
        [((rows, width), hidden.dtype, pl.BlockSpec((tile, width), lambda i, *_: (i, 0)))] * 4,
        tokens,
        100.0,
    )


def shift(array, by):
    size = lax.axis_size("dp")
    return lax.ppermute(array, "dp", [(i, (i + by) % size) for i in range(size)])


def shifted(array, source):
    size = lax.axis_size("dp")
    me = lax.axis_index("dp")
    if size > 4:
        taken = lax.dynamic_index_in_dim(lax.all_gather(array, "dp"), source, 0, keepdims=False)
        return [taken], jnp.zeros((1,), jnp.int32)
    choices = [array] + [shift(array, by) for by in range(1, size)]
    return choices, ((me - source) % size).reshape(1)


def add(*arrays):
    return sum(array.astype(jnp.float32) for array in arrays).astype(arrays[0].dtype)


def crossed(array, by):
    return lax.ppermute(array, "tensor", [(i, i ^ by) for i in range(lax.axis_size("tensor"))])


def near(array):
    return crossed(array, 1)


def far(array):
    return crossed(array, 2)


def exchanged(array):
    array = add(array, near(array))
    return array, far(array)


def spread(array):
    return [array] + [crossed(array, by) for by in range(1, lax.axis_size("tensor"))]


def line_reduce_scatter(table):
    size = lax.axis_size("dp")
    me = lax.axis_index("dp")

    def entry(index):
        return lax.dynamic_index_in_dim(table, jnp.clip(index, 0, size - 1), 0, keepdims=False)

    from_left = from_right = None
    for step in range(size - 1):
        right = entry(size - 1 - step + me)
        left = entry(step - (size - 1 - me))
        if step > 0:
            right = add(right, from_left)
            left = add(left, from_right)
        from_left = lax.ppermute(right, "dp", [(i, i + 1) for i in range(step + 1)])
        from_right = lax.ppermute(left, "dp", [(i, i - 1) for i in range(size - 1 - step, size)])
    return entry(me) if size == 1 else add(entry(me), from_left, from_right)


ROLES = ((3, 2, 1, 0), (2, 3, 0, 1), (1, 0, 3, 2), (0, 1, 2, 3))


def body(
    partner,
    block_tenant_index,
    block_live_length,
    tenant_table_row,
    hidden,
    cotangent,
    frozen_value_weight,
    adapter_down_rows,
    adapter_up_matrix,
):
    blocks = block_tenant_index.shape[0]
    kept = blocks - SW
    devices = lax.axis_size("dp")
    me = lax.axis_index("dp")
    column = lax.axis_index("tensor")
    lengths = block_live_length
    line = devices == 4
    order = jnp.arange(devices, dtype=jnp.int32)
    holder = jnp.sum(jnp.where(partner == me, order, 0))

    cot_terms, up_own, down_own = kept_ranks(lengths, adapter_up_matrix, cotangent, adapter_down_rows)
    up_choices, _ = shifted(up_own, holder)
    cot_terms, up_last = with_last_rank(lengths, partner, me, up_choices, cotangent, cot_terms)
    rank_cot = exchanged(cot_terms)
    down_own = after(down_own, rank_cot[0])

    table_rows = jnp.sum(
        jnp.where(
            block_tenant_index[:, None] == jnp.arange(tenant_table_row.shape[0], dtype=jnp.int32)[None, :],
            tenant_table_row[None, :],
            0,
        ),
        axis=1,
    )
    weights = jnp.where(jnp.arange(blocks) < kept, 2 * (jnp.arange(blocks, dtype=jnp.int32) + 1), 1)

    def codes_of(owners):
        rows = (owners[:, None] * OWN + jnp.arange(OWN, dtype=jnp.int32)[None, :]).reshape(-1)
        return jnp.sum(jnp.where(rows[:, None] == table_rows[None, :], weights[None, :], 0), axis=1)

    columns = jnp.stack([column ^ 3, column ^ 2, column ^ 1, column]).astype(jnp.int32)

    def base(*tokens):
        return base_terms(columns, hidden, frozen_value_weight, tokens)

    def base_parts(terms, *tokens):
        sent, away, given, mine = terms
        away = add(after(away, *tokens), near(sent))
        return (mine, near(given), far(away)), away

    def inputs(down_choices, *tokens):
        return spread(
            streamed_ranks(lengths, partner, me, adapter_down_rows, down_choices, hidden, 4, tokens, 100.0)
        )

    if line:
        inner = (me == 1) | (me == 2)
        codes = codes_of(jnp.array(ROLES, jnp.int32)[me])
        (first,) = down_rows(codes, 0, 1, 1, rank_cot, hidden)
        from_end = lax.ppermute(first, "dp", [(0, 1), (3, 2)])
        from_left = lax.ppermute(down_own, "dp", [(0, 1), (1, 2), (2, 3)])
        from_right = lax.ppermute(down_own, "dp", [(3, 2), (2, 1), (1, 0)])
        passed, outward = passed_on(partner, me, down_own, from_left, from_right, [first])
        terms = base(first, passed)
        passed = lax.ppermute(passed, "dp", [(1, 2), (2, 1)])
        outward = lax.ppermute(outward, "dp", [(1, 3), (2, 0)])
        down_choices = [down_own, from_left, from_right, passed, outward]
        second, third, own = down_rows(codes, OWN, 3, 1, rank_cot, hidden, [terms[0], passed, outward], 100.0)
        second = add(second, jnp.where(inner, from_end, jnp.zeros((), first.dtype)))
        from_second = lax.ppermute(second, "dp", [(0, 1), (3, 2), (1, 3), (2, 0)])
        rank_in = inputs(down_choices, second)
        base_sums, _ = base_parts(terms, rank_in[0])
        up_codes = codes_of((me + jnp.array([1, 2, 3, 0], jnp.int32)) % devices)
        *sent, up_kept = up_rows(up_codes, [OWN] * 4, rank_in, cotangent)
        arrived = [shift(array, by + 1) for by, array in enumerate(sent)]
        middle = add(after(first, up_kept), from_second)
        third = after(third, from_second)
        from_inner = lax.ppermute(after(middle, third), "dp", [(1, 2), (2, 1)])
        up_out = add(after(up_kept, middle), *arrived)
        from_third = lax.ppermute(third, "dp", [(0, 1), (3, 2), (1, 0), (2, 3)])
        near_total = lax.optimization_barrier(
            after(own, middle).astype(jnp.float32) + jnp.where(inner, 0.0, from_second.astype(jnp.float32))
        )
        down_out = (near_total + from_inner.astype(jnp.float32) + from_third.astype(jnp.float32)).astype(own.dtype)

        values, last_values = values_of(lengths, base_sums, rank_in, adapter_up_matrix, up_last, [up_out])
        tokens = [down_out]
    else:
        codes = codes_of(order)
        (table,) = down_rows(codes, 0, devices, 0, rank_cot, hidden)
        down_choices, _ = shifted(down_own, holder)
        down_out = line_reduce_scatter(table.reshape(devices, OWN, *table.shape[1:]))
        rank_in = inputs(down_choices, table)
        values, last_values = values_of(
            lengths, base_parts(base(table))[0], rank_in, adapter_up_matrix, up_last
        )
        (up_table,) = up_rows(codes, [devices * OWN], rank_in, cotangent)
        up_out = line_reduce_scatter(up_table.reshape(devices, OWN, *up_table.shape[1:]))
        tokens = []
    value_choices, _ = shifted(last_values, partner[me])
    values = put_last(partner, me, values, value_choices, tokens)
    return (values, down_out, up_out)


def solution(mesh):
    in_specs = (
        P("groups"),
        P(("groups", "dp")),
        P(("groups", "dp")),
        P("groups"),
        P(("groups", "dp"), "tensor"),
        P(("groups", "dp"), "tensor"),
        P("tensor", None),
        P(("groups", "dp"), None, "tensor"),
        P(("groups", "dp"), None, "tensor"),
    )
    out_specs = (
        P(("groups", "dp"), "tensor"),
        P(("groups", "dp"), None, "tensor"),
        P(("groups", "dp"), None, "tensor"),
    )
    return jax.shard_map(body, mesh=mesh, in_specs=in_specs, out_specs=out_specs, check_vma=False)
```

```python
import jax
import jax.numpy as jnp
from jax import lax
from jax.experimental import pallas as pl
from jax.experimental.pallas import tpu as pltpu
from jax.sharding import PartitionSpec as P

BLOCK = 128
SW = 1
OWN = 4


ADAPTER_SCALE = 0.5

ANYWHERE = pl.BlockSpec(memory_space=pl.ANY)
ROW_PRODUCT = (((1,), (1,)), ((), ()))


def call(kernel, scalars, grid, inputs, outputs, tokens=(), us=1.0, scratch=(), aliases=None, vmem=16):
    def run(*refs):
        cut = len(scalars) + len(inputs)
        return kernel(*refs[:cut], *refs[cut + len(tokens) :])

    return pl.pallas_call(
        run,
        grid_spec=pltpu.PrefetchScalarGridSpec(
            num_scalar_prefetch=len(scalars),
            grid=grid,
            in_specs=[spec for _, spec in inputs] + [ANYWHERE] * len(tokens),
            out_specs=[spec for _, _, spec in outputs],
            scratch_shapes=scratch,
        ),
        out_shape=[jax.ShapeDtypeStruct(shape, kind) for shape, kind, _ in outputs],
        input_output_aliases=aliases or {},
        compiler_params=pltpu.CompilerParams(vmem_limit_bytes=vmem * 1024 * 1024),
        cost_estimate=pl.CostEstimate(flops=int(us * 1e9), bytes_accessed=int(us * 3.6e5), transcendentals=0),
    )(*scalars, *[array for array, _ in inputs], *tokens)


def constant_spec(shape):
    return pl.BlockSpec(shape, lambda *_: (0,) * len(shape), pipeline_mode=pl.Buffered(1))


def whole(array):
    return (array, constant_spec(array.shape))


def nothing(*refs):
    pass


def after(array, *tokens):
    return call(
        nothing, (), (1,), [(array, ANYWHERE)], [(array.shape, array.dtype, ANYWHERE)], tokens, 0.1, aliases={0: 0}
    )[0]


def masked_rank(adapter, rows, length):
    ranks = lax.dot_general(adapter, rows, ROW_PRODUCT, preferred_element_type=jnp.float32)
    live = lax.broadcasted_iota(jnp.int32, ranks.shape, 1) < length
    return jnp.where(live, ranks, 0.0).astype(rows.dtype)


def kept_ranks(lengths, maps, features, others):
    blocks, rank, width = maps.shape
    kept = blocks - SW
    last_shapes = [(SW, rank, width), (SW, *others.shape[1:])]

    def kernel(lengths_ref, maps_ref, rows_ref, others_ref, out_ref, last_ref, last_other):
        last_ref[...] = maps_ref[kept:]
        last_other[...] = others_ref[...]
        for k in range(kept):
            out_ref[k] = masked_rank(maps_ref[k], rows_ref[k * BLOCK : (k + 1) * BLOCK], lengths_ref[k])

    return call(
        kernel,
        (lengths,),
        (1,),
        [
            whole(maps),
            (features, pl.BlockSpec((kept * BLOCK, width), lambda i, *_: (0, 0), pipeline_mode=pl.Buffered(1))),
            (others, pl.BlockSpec(last_shapes[1], lambda i, *_: (kept, 0, 0), pipeline_mode=pl.Buffered(1))),
        ],
        [((blocks, rank, BLOCK), features.dtype, pl.BlockSpec((kept, rank, BLOCK), lambda i, *_: (0, 0, 0)))]
        + [(shape, features.dtype, constant_spec(shape)) for shape in last_shapes],
        vmem=60,
    )


def passed_on(partner, me, own, from_left, from_right, tokens):
    shape = own.shape

    def kernel(partner_ref, me_ref, own_ref, left_ref, right_ref, inner_ref, outer_ref):
        left = me_ref[0] == 1

        @pl.when(left)
        def _():
            inner_ref[...] = left_ref[...]
            outer_ref[...] = left_ref[...]

        @pl.when(jnp.logical_not(left))
        def _():
            inner_ref[...] = right_ref[...]
            outer_ref[...] = right_ref[...]

        @pl.when(partner_ref[me_ref[0]] == jnp.where(left, 3, 0))
        def _():
            outer_ref[...] = own_ref[...]

    return call(
        kernel,
        (partner, me.reshape(1)),
        (1,),
        [whole(array) for array in (own, from_left, from_right)],
        [(shape, own.dtype, constant_spec(shape))] * 2,
        tokens,
        1.0,
    )


def with_last_rank(lengths, partner, me, choices, features, ranks):
    shape = choices[0].shape
    block = ranks.shape[0] - 1
    size = partner.shape[0]

    def kernel(lengths_ref, partner_ref, me_ref, *refs):
        rows_ref, _, out_ref, chosen_ref = refs[-4:]
        for k, choice in enumerate(refs[:-4]):
            if len(choices) == 1:
                chosen_ref[...] = choice[...]
                continue

            @pl.when(partner_ref[lax.rem(me_ref[0] + (size - k), size)] == me_ref[0])
            def _():
                chosen_ref[...] = choice[...]

        out_ref[0] = masked_rank(chosen_ref[0], rows_ref[...], lengths_ref[block])

    return call(
        kernel,
        (lengths, partner, me.reshape(1)),
        (1,),
        [whole(choice) for choice in choices]
        + [(features, pl.BlockSpec((BLOCK, shape[2]), lambda i, *_: (block, 0), pipeline_mode=pl.Buffered(1)))]
        + [(ranks, ANYWHERE)],
        [
            (ranks.shape, ranks.dtype, pl.BlockSpec((1, *ranks.shape[1:]), lambda i, *_: (block, 0, 0))),
            (shape, features.dtype, constant_spec(shape)),
        ],
        aliases={4 + len(choices): 0},
        vmem=60,
    )


def streamed_ranks(lengths, partner, me, maps, choices, features, each, tokens=(), us=1.0):
    blocks, rank, width = maps.shape
    steps = pl.cdiv(blocks, each)
    end = blocks - 1 - (steps - 1) * each

    def picked(partner_ref, at):
        if len(choices) == 1:
            return [at == at]
        held = [
            partner_ref[at] == at,
            (partner_ref[jnp.maximum(at - 1, 0)] == at) & (at > 0),
            (partner_ref[jnp.minimum(at + 1, 3)] == at) & (at < 3),
        ]
        other = jnp.logical_not(held[0] | held[1] | held[2])
        inner = (at == 1) | (at == 2)
        return [*held, other & inner, other & jnp.logical_not(inner)]

    def kernel(lengths_ref, partner_ref, me_ref, *refs):
        maps_refs, rows_refs, choices_refs, out_ref = refs[:each], refs[each : 2 * each], refs[2 * each : -1], refs[-1]
        step = pl.program_id(0)

        def one(k):
            block = step * each + k
            out_ref[block] = masked_rank(maps_refs[k][0], rows_refs[k][...], lengths_ref[block])

        @pl.when(step < steps - 1)
        def _():
            for k in range(each):
                one(k)

        @pl.when(step == steps - 1)
        def _():
            for k in range(end):
                one(k)
            for choice, use in zip(choices_refs, picked(partner_ref, me_ref[0])):

                @pl.when(use)
                def _():
                    out_ref[blocks - 1] = masked_rank(choice[0], rows_refs[end][...], lengths_ref[blocks - 1])

    def at(i, k):
        block = i * each + k
        return jnp.where(block < blocks, block, block - each)

    return call(
        kernel,
        (lengths, partner, me.reshape(1)),
        (steps,),
        [(maps, pl.BlockSpec((1, rank, width), lambda i, *_, k=k: (at(i, k), 0, 0))) for k in range(each)]
        + [(features, pl.BlockSpec((BLOCK, width), lambda i, *_, k=k: (at(i, k), 0))) for k in range(each)]
        + [whole(choice) for choice in choices],
        [((blocks, rank, BLOCK), features.dtype, constant_spec((blocks, rank, BLOCK)))],
        tokens,
        us,
    )[0]


def summed(terms, at):
    return sum(term[at].astype(jnp.float32) for term in terms).astype(terms[0].dtype)


def down_rows(codes, first, parts, copies, ranks, features, tokens=(), us=1.0):
    blocks, rank, _ = ranks[0].shape
    width = features.shape[1]
    piece = min(width, 512)

    def block_at(code):
        return jnp.maximum((code >> 1) - 1, 0)

    def kernel(codes_ref, a, b, *refs):
        rows_refs, last_ref, outs = refs[:OWN], refs[OWN], refs[OWN + 1 :]
        step = pl.program_id(0)

        def fill(to):
            for k in range(OWN):
                code = codes_ref[first + step * OWN + k]
                mine = summed((a, b), block_at(code))
                mine = jnp.where(code > 1, mine, jnp.zeros_like(mine))

                def put(at, total):
                    value = (ADAPTER_SCALE * total).astype(features.dtype)
                    for out_ref in to:
                        out_ref[k, :, at] = value

                for at in [slice(c, c + piece) for c in range(0, width, piece)]:
                    put(at, jnp.dot(mine, rows_refs[k][:, at], preferred_element_type=jnp.float32))

                @pl.when((code & 1) > 0)
                def _():
                    late = summed((a, b), blocks - 1)
                    for at in [slice(c, c + piece) for c in range(0, width, piece)]:
                        put(
                            at,
                            jnp.dot(mine, rows_refs[k][:, at], preferred_element_type=jnp.float32)
                            + jnp.dot(late, last_ref[:, at], preferred_element_type=jnp.float32),
                        )

        if not copies or parts == 1:
            fill(outs)
        else:
            for part in range(parts):

                @pl.when(step == part)
                def _():
                    fill(outs[part:] if part == parts - 1 else outs[part : part + 1])

    def rows_spec(k):
        return pl.BlockSpec((BLOCK, width), lambda r, at: (block_at(at[first + r * OWN + k]), 0))

    shape = (OWN, rank, width)
    if copies:
        outs = [(shape, features.dtype, constant_spec(shape))] * (parts - 1 + copies)
    else:
        outs = [((parts * OWN, rank, width), features.dtype, pl.BlockSpec(shape, lambda r, *_: (r, 0, 0)))]
    return call(
        kernel,
        (codes,),
        (parts,),
        [whole(array) for array in ranks]
        + [(features, rows_spec(k)) for k in range(OWN)]
        + [(features, pl.BlockSpec((BLOCK, width), lambda r, *_: (blocks - 1, 0), pipeline_mode=pl.Buffered(1)))],
        outs,
        tokens,
        us,
    )


def up_rows(codes, parts, ranks, features):
    blocks, rank, _ = ranks[0].shape
    width = features.shape[1]

    def kernel(codes_ref, *refs):
        terms, rows_ref, outs = refs[: len(ranks)], refs[len(ranks)], refs[len(ranks) + 1 :]
        late = jnp.dot(
            summed(terms, blocks - 1), rows_ref[(blocks - 1) * BLOCK :], preferred_element_type=jnp.float32
        )
        done = 0
        for count, out in zip(parts, outs):

            def one_row(r, carry, out=out, done=done):
                code = codes_ref[done + r]
                at = jnp.maximum((code >> 1) - 1, 0)
                mine = summed(terms, at)
                mine = jnp.where(code > 1, mine, jnp.zeros_like(mine))
                mine_rows = rows_ref[pl.ds(pl.multiple_of(at * BLOCK, BLOCK), BLOCK), :]
                total = jnp.dot(mine, mine_rows, preferred_element_type=jnp.float32)
                total = total + jnp.where((code & 1) > 0, late, 0.0)
                out[r] = (ADAPTER_SCALE * total).astype(out.dtype)
                return carry

            if count <= OWN:
                for r in range(count):
                    one_row(r, 0)
            else:
                lax.fori_loop(0, count, one_row, 0)
            done += count

    return call(
        kernel,
        (codes,),
        (1,),
        [whole(array) for array in (*ranks, features)],
        [((count, rank, width), features.dtype, constant_spec((count, rank, width))) for count in parts],
    )


def values_of(lengths, base, ranks, maps, last_map, tokens=()):
    rows, width = base[0].shape
    blocks = rows // BLOCK

    def kernel(lengths_ref, one, two, three, *refs):
        terms, (maps_ref, last_ref, out_ref, last_out) = refs[: len(ranks)], refs[len(ranks) :]
        for k in range(blocks):
            at = slice(k * BLOCK, (k + 1) * BLOCK)
            adapter = maps_ref[k] if k < blocks - 1 else last_ref[0]
            added = lax.dot_general(
                summed(terms, k), adapter, (((0,), (0,)), ((), ())), preferred_element_type=jnp.float32
            )
            frozen = one[at].astype(jnp.float32) + two[at].astype(jnp.float32) + three[at].astype(jnp.float32)
            live = lax.broadcasted_iota(jnp.int32, frozen.shape, 0) < lengths_ref[k]
            values = jnp.where(live, frozen + ADAPTER_SCALE * added, 0.0).astype(out_ref.dtype)
            out_ref[at] = values
            if k == blocks - 1:
                last_out[...] = values

    return call(
        kernel,
        (lengths,),
        (1,),
        [whole(array) for array in (*base, *ranks, maps, last_map)],
        [
            ((rows, width), maps.dtype, constant_spec((rows, width))),
            ((BLOCK, width), maps.dtype, constant_spec((BLOCK, width))),
        ],
        tokens,
        100.0,
        vmem=60,
    )


def put_last(partner, me, values, choices, tokens):
    width = values.shape[1]
    block = values.shape[0] // BLOCK - 1
    size = partner.shape[0]

    def kernel(partner_ref, me_ref, *refs):
        for k, choice in enumerate(refs[:-2]):
            if len(choices) == 1:
                refs[-1][...] = choice[...]
                continue

            @pl.when(partner_ref[me_ref[0]] == lax.rem(me_ref[0] + (size - k), size))
            def _():
                refs[-1][...] = choice[...]

    return call(
        kernel,
        (partner, me.reshape(1)),
        (1,),
        [whole(choice) for choice in choices] + [(values, ANYWHERE)],
        [(values.shape, values.dtype, pl.BlockSpec((BLOCK, width), lambda i, *_: (block, 0)))],
        tokens,
        aliases={2 + len(choices): 0},
    )[0]


def base_terms(columns, hidden, weight, tokens=()):
    rows, depth = hidden.shape
    width = weight.shape[1] // 4
    tile = rows // 4

    def kernel(columns_ref, rows_ref, *refs):
        for k in range(4):
            out_ref = refs[4 + k]
            out_ref[...] = jnp.dot(rows_ref[...], refs[k][...], preferred_element_type=jnp.float32).astype(out_ref.dtype)

    def column(k):
        return pl.BlockSpec((depth, width), lambda i, at: (0, at[k]), pipeline_mode=pl.Buffered(1))

    return call(
        kernel,
        (columns,),
        (rows // tile,),
        [(hidden, pl.BlockSpec((tile, depth), lambda i, *_: (i, 0)))]
        + [(weight, column(k)) for k in range(4)],
        [((rows, width), hidden.dtype, pl.BlockSpec((tile, width), lambda i, *_: (i, 0)))] * 4,
        tokens,
        100.0,
    )


def shift(array, by):
    size = lax.axis_size("dp")
    return lax.ppermute(array, "dp", [(i, (i + by) % size) for i in range(size)])


def shifted(array, source):
    size = lax.axis_size("dp")
    me = lax.axis_index("dp")
    if size > 4:
        taken = lax.dynamic_index_in_dim(lax.all_gather(array, "dp"), source, 0, keepdims=False)
        return [taken], jnp.zeros((1,), jnp.int32)
    choices = [array] + [shift(array, by) for by in range(1, size)]
    return choices, ((me - source) % size).reshape(1)


def add(*arrays):
    return sum(array.astype(jnp.float32) for array in arrays).astype(arrays[0].dtype)


def crossed(array, by):
    return lax.ppermute(array, "tensor", [(i, i ^ by) for i in range(lax.axis_size("tensor"))])


def near(array):
    return crossed(array, 1)


def far(array):
    return crossed(array, 2)


def exchanged(array):
    array = add(array, near(array))
    return array, far(array)


def spread(array):
    return [array] + [crossed(array, by) for by in range(1, lax.axis_size("tensor"))]


def line_reduce_scatter(table):
    size = lax.axis_size("dp")
    me = lax.axis_index("dp")

    def entry(index):
        return lax.dynamic_index_in_dim(table, jnp.clip(index, 0, size - 1), 0, keepdims=False)

    from_left = from_right = None
    for step in range(size - 1):
        right = entry(size - 1 - step + me)
        left = entry(step - (size - 1 - me))
        if step > 0:
            right = add(right, from_left)
            left = add(left, from_right)
        from_left = lax.ppermute(right, "dp", [(i, i + 1) for i in range(step + 1)])
        from_right = lax.ppermute(left, "dp", [(i, i - 1) for i in range(size - 1 - step, size)])
    return entry(me) if size == 1 else add(entry(me), from_left, from_right)


ROLES = ((3, 2, 1, 0), (2, 3, 0, 1), (1, 0, 3, 2), (0, 1, 2, 3))


def body(
    partner,
    block_tenant_index,
    block_live_length,
    tenant_table_row,
    hidden,
    cotangent,
    frozen_value_weight,
    adapter_down_rows,
    adapter_up_matrix,
):
    blocks = block_tenant_index.shape[0]
    kept = blocks - SW
    devices = lax.axis_size("dp")
    me = lax.axis_index("dp")
    column = lax.axis_index("tensor")
    lengths = block_live_length
    line = devices == 4
    order = jnp.arange(devices, dtype=jnp.int32)
    holder = jnp.sum(jnp.where(partner == me, order, 0))

    cot_terms, up_own, down_own = kept_ranks(lengths, adapter_up_matrix, cotangent, adapter_down_rows)
    up_choices, _ = shifted(up_own, holder)
    cot_terms, up_last = with_last_rank(lengths, partner, me, up_choices, cotangent, cot_terms)
    rank_cot = exchanged(cot_terms)
    down_own = after(down_own, rank_cot[0])

    table_rows = jnp.sum(
        jnp.where(
            block_tenant_index[:, None] == jnp.arange(tenant_table_row.shape[0], dtype=jnp.int32)[None, :],
            tenant_table_row[None, :],
            0,
        ),
        axis=1,
    )
    weights = jnp.where(jnp.arange(blocks) < kept, 2 * (jnp.arange(blocks, dtype=jnp.int32) + 1), 1)

    def codes_of(owners):
        rows = (owners[:, None] * OWN + jnp.arange(OWN, dtype=jnp.int32)[None, :]).reshape(-1)
        return jnp.sum(jnp.where(rows[:, None] == table_rows[None, :], weights[None, :], 0), axis=1)

    columns = jnp.stack([column ^ 3, column ^ 2, column ^ 1, column]).astype(jnp.int32)

    def base(*tokens):
        return base_terms(columns, hidden, frozen_value_weight, tokens)

    def base_parts(terms, *tokens):
        sent, away, given, mine = terms
        away = add(after(away, *tokens), near(sent))
        return (mine, near(given), far(away)), away

    def inputs(down_choices, *tokens):
        return spread(
            streamed_ranks(lengths, partner, me, adapter_down_rows, down_choices, hidden, 4, tokens, 100.0)
        )

    if line:
        inner = (me == 1) | (me == 2)
        codes = codes_of(jnp.array(ROLES, jnp.int32)[me])
        (first,) = down_rows(codes, 0, 1, 1, rank_cot, hidden)
        from_end = lax.ppermute(first, "dp", [(0, 1), (3, 2)])
        from_left = lax.ppermute(down_own, "dp", [(0, 1), (1, 2), (2, 3)])
        from_right = lax.ppermute(down_own, "dp", [(3, 2), (2, 1), (1, 0)])
        passed, outward = passed_on(partner, me, down_own, from_left, from_right, [first])
        terms = base(first, passed)
        passed = lax.ppermute(passed, "dp", [(1, 2), (2, 1)])
        outward = lax.ppermute(outward, "dp", [(1, 3), (2, 0)])
        down_choices = [down_own, from_left, from_right, passed, outward]
        second, third, own = down_rows(codes, OWN, 3, 1, rank_cot, hidden, [terms[0], passed, outward], 100.0)
        second = add(second, jnp.where(inner, from_end, jnp.zeros((), first.dtype)))
        from_second = lax.ppermute(second, "dp", [(0, 1), (3, 2), (1, 3), (2, 0)])
        rank_in = inputs(down_choices, second)
        base_sums, _ = base_parts(terms, rank_in[0])
        up_codes = codes_of((me + jnp.array([1, 2, 3, 0], jnp.int32)) % devices)
        *sent, up_kept = up_rows(up_codes, [OWN] * 4, rank_in, cotangent)
        arrived = [shift(array, by + 1) for by, array in enumerate(sent)]
        middle = add(after(first, up_kept), from_second)
        third = after(third, from_second)
        from_inner = lax.ppermute(after(middle, third), "dp", [(1, 2), (2, 1)])
        up_out = add(after(up_kept, middle), *arrived)
        from_third = lax.ppermute(third, "dp", [(0, 1), (3, 2), (1, 0), (2, 3)])
        near_total = lax.optimization_barrier(
            after(own, middle).astype(jnp.float32) + jnp.where(inner, 0.0, from_second.astype(jnp.float32))
        )
        down_out = (near_total + from_inner.astype(jnp.float32) + from_third.astype(jnp.float32)).astype(own.dtype)

        values, last_values = values_of(lengths, base_sums, rank_in, adapter_up_matrix, up_last, [up_out])
        tokens = [down_out]
    else:
        codes = codes_of(order)
        (table,) = down_rows(codes, 0, devices, 0, rank_cot, hidden)
        down_choices, _ = shifted(down_own, holder)
        down_out = line_reduce_scatter(table.reshape(devices, OWN, *table.shape[1:]))
        rank_in = inputs(down_choices, table)
        values, last_values = values_of(
            lengths, base_parts(base(table))[0], rank_in, adapter_up_matrix, up_last
        )
        (up_table,) = up_rows(codes, [devices * OWN], rank_in, cotangent)
        up_out = line_reduce_scatter(up_table.reshape(devices, OWN, *up_table.shape[1:]))
        tokens = []
    value_choices, _ = shifted(last_values, partner[me])
    values = put_last(partner, me, values, value_choices, tokens)
    return (values, down_out, up_out)


def solution(mesh):
    in_specs = (
        P("groups"),
        P(("groups", "dp")),
        P(("groups", "dp")),
        P("groups"),
        P(("groups", "dp"), "tensor"),
        P(("groups", "dp"), "tensor"),
        P("tensor", None),
        P(("groups", "dp"), None, "tensor"),
        P(("groups", "dp"), None, "tensor"),
    )
    out_specs = (
        P(("groups", "dp"), "tensor"),
        P(("groups", "dp"), None, "tensor"),
        P(("groups", "dp"), None, "tensor"),
    )
    return jax.shard_map(body, mesh=mesh, in_specs=in_specs, out_specs=out_specs, check_vma=False)
```
